32 devices in a mesh: fsdp: 16 (over z, x, core), rep: 2 (over y).
Axes of the slice: x: 2, y: 2, z: 4, core: 2. Of those that a mesh axis runs over, the one named last changes fastest.
Arguments:
- tokens: bfloat16 [64, 512, 768], P(('fsdp', 'rep')), may hold values from -6 to 6
- segments: int32 [64, 512], P(('fsdp', 'rep')), may hold values from 0 to 7, never falling along the last dimension, each value on 1 to 128 neighbouring positions
- w_query: bfloat16 [768, 768], P('fsdp'), may hold values from -0.21875 to 0.21875
- b_query: bfloat16 [768], P('fsdp'), may hold values from -3 to 3
- w_key: bfloat16 [768, 768], P('fsdp'), may hold values from -0.21875 to 0.21875
- w_value: bfloat16 [768, 768], P('fsdp'), may hold values from -0.21875 to 0.21875
- b_value: bfloat16 [768], P('fsdp'), may hold values from -3 to 3
- w_out: bfloat16 [768, 768], P('fsdp'), may hold values from -1.75 to 1.75
- b_out: bfloat16 [768], P('fsdp'), may hold values from -3 to 3
- gain1: bfloat16 [768], P('fsdp'), may hold values from 0.5 to 1.5
- shift1: bfloat16 [768], P('fsdp'), may hold values from -2 to 2
- w_up: bfloat16 [768, 3072], P('fsdp'), may hold values from -0.21875 to 0.21875
- b_up: bfloat16 [3072], P('fsdp'), may hold values from -3 to 3
- w_down: bfloat16 [3072, 768], P('fsdp'), may hold values from -0.109375 to 0.109375
- b_down: bfloat16 [768], P('fsdp'), may hold values from -3 to 3
- gain2: bfloat16 [768], P('fsdp'), may hold values from 0.5 to 1.5
- shift2: bfloat16 [768], P('fsdp'), may hold values from -2 to 2
- out_grad: bfloat16 [64, 512, 768], P(('fsdp', 'rep')), may hold values from -6 to 6
Outputs:
- output: bfloat16 [64, 512, 768], P(('fsdp', 'rep'))
- pooled: float32 [64, 8, 768], P(('fsdp', 'rep'))
- grad_tokens: bfloat16 [64, 512, 768], P(('fsdp', 'rep'))
- grad_w_query: float32 [768, 768], P('fsdp')
- grad_b_query: float32 [768], P('fsdp')
- grad_w_key: float32 [768, 768], P('fsdp')
- grad_w_value: float32 [768, 768], P('fsdp')
- grad_b_value: float32 [768], P('fsdp')
- grad_w_out: float32 [768, 768], P('fsdp')
- grad_b_out: float32 [768], P('fsdp')
- grad_gain1: float32 [768], P('fsdp')
- grad_shift1: float32 [768], P('fsdp')
- grad_w_up: float32 [768, 3072], P('fsdp')
- grad_b_up: float32 [3072], P('fsdp')
- grad_w_down: float32 [3072, 768], P('fsdp')
- grad_b_down: float32 [768], P('fsdp')
- grad_gain2: float32 [768], P('fsdp')
- grad_shift2: float32 [768], P('fsdp')
The draws below stay inside these ranges and needn't reach their ends.
Inputs may be any that keep to these rules, and one draw needn't show every extreme that they name: `segments`: along each row the segment ids never fall and take every value from 0 to 7; a text has at most 128 tokens, and in every row one text has exactly 128.
All inputs are finite; a program needn't handle non-finite values.
Results may differ from the reference program's by a relative error of at most 0.015.
Values may be sent and summed in bfloat16 or wider, within the bound.
A program may use at most 192 MiB of HBM per device.

```python
import math
import jax
import jax.numpy as jnp
import numpy as np
from jax import lax

D = 768
H = 12
HEAD = 64
FF = 3072
L = 512
SEGS = 8
MOST = 128
ROWS = 64


def block_levels(rng, dims, split, smallest, high):
    def one(position, parts):
        draws = jax.random.uniform(jax.random.fold_in(jax.random.fold_in(rng, 6), position), (parts,), jnp.float32, smallest / len(split), high / len(split))
        return jnp.repeat(jnp.exp(draws), dims[position] // parts).reshape((-1,) + (1,) * (len(dims) - position - 1))

    level = one(*split[0])
    for cut in split[1:]:
        level = level * one(*cut)
    return level


def split_up(number_of, total, limit, lean):
    portions = [(1 << 20) // math.isqrt(rank ** lean) + 1 for rank in range(2, number_of + 1)]
    spare, given = total - limit - (number_of - 1), [1] * (number_of - 1)
    while spare > 0:
        candidates = [i for i in range(number_of - 1) if given[i] < limit]
        pool, budget = sum([portions[i] for i in candidates]), spare
        for i in candidates:
            more = min(limit - given[i], max(1, budget * portions[i] // pool), spare)
            given[i] = given[i] + more
            spare = spare - more
    return np.array([limit] + given)


def ragged_sizes(own_key, amount, total, limit, slope):
    if amount == 2:
        one = jax.random.randint(own_key, (), max(1, total - limit), min(limit, total - 1) + 1)
        return jnp.stack([one, total - one])
    lengths = jnp.asarray(split_up(amount, total, limit, slope), jnp.int32)
    couples = (amount - 1) // 2
    donor, taker = lengths[1:1 + 2 * couples:2], lengths[2:2 + 2 * couples:2]
    slack = jnp.minimum(donor - 1, limit - taker)
    moved = jax.random.randint(jax.random.fold_in(own_key, 1), (couples,), 0, 1 << 20) % (slack + 1)
    lengths = lengths.at[1:1 + 2 * couples:2].set(donor - moved).at[2:2 + 2 * couples:2].set(taker + moved)
    return lengths[jax.random.permutation(jax.random.fold_in(own_key, 2), amount)]


def centred(rng, shape, width, most, pieces=(), kind=jnp.bfloat16):
    factor_of = block_levels(rng, shape, pieces, -0.22, 0.18) if pieces else 1.0
    values = jax.random.normal(rng, shape, jnp.float32) * width * factor_of
    return jnp.minimum(jnp.maximum(values, -most), most).astype(kind)


def setup_inputs(seed: int = 0) -> dict:
    key_of = jax.random.split(jax.random.key(seed), 19)
    return {
        "tokens": centred(key_of[0], (ROWS, L, D), 1.0, 6.0, ((0, 32),)),
        "segments": jax.vmap(lambda own: jnp.searchsorted(jnp.cumsum(ragged_sizes(own, SEGS, L, MOST, 0)), jnp.arange(L), side="right"))(jax.random.split(key_of[1], ROWS)).reshape((ROWS, L)).astype(jnp.int32),
        "w_query": centred(key_of[2], (D, D), D ** -0.5, 0.21875, ((0, 16),)),
        "b_query": centred(key_of[3], (D,), 0.5, 3.0, ((0, 16),)),
        "w_key": centred(key_of[4], (D, D), D ** -0.5, 0.21875, ((0, 16),)),
        "w_value": centred(key_of[5], (D, D), D ** -0.5, 0.21875, ((0, 16),)),
        "b_value": centred(key_of[6], (D,), 0.5, 3.0, ((0, 16),)),
        "w_out": centred(key_of[7], (D, D), (D // 64) ** -0.5, 1.75, ((0, 16),)),
        "b_out": centred(key_of[8], (D,), 0.5, 3.0, ((0, 16),)),
        "gain1": jnp.clip(1.0 + 0.1 * jax.random.normal(key_of[9], (D,), jnp.float32), 0.5, 1.5).astype(jnp.bfloat16),
        "shift1": centred(key_of[10], (D,), 0.3, 2.0, ((0, 16),)),
        "w_up": centred(key_of[11], (D, FF), D ** -0.5, 0.21875, ((0, 16),)),
        "b_up": centred(key_of[12], (FF,), 0.5, 3.0, ((0, 16),)),
        "w_down": centred(key_of[13], (FF, D), FF ** -0.5, 0.109375, ((0, 16),)),
        "b_down": centred(key_of[14], (D,), 0.5, 3.0, ((0, 16),)),
        "gain2": jnp.clip(1.0 + 0.1 * jax.random.normal(key_of[15], (D,), jnp.float32), 0.5, 1.5).astype(jnp.bfloat16),
        "shift2": centred(key_of[16], (D,), 0.3, 2.0, ((0, 16),)),
        "out_grad": centred(key_of[17], (ROWS, L, D), 1.0, 6.0, ((0, 32),)),
    }


@jax.custom_vjp
def low(v):
    return lax.optimization_barrier(v.astype(jnp.bfloat16)).astype(jnp.float32)

@jax.custom_vjp
def low_back(v):
    return v

def low_keep(v):
    return (low(v), None)

def low_pass(kept, grad):
    return (grad,)

def back_keep(v):
    return (v, None)

def back_low(kept, grad):
    return (low(grad),)
low.defvjp(low_keep, low_pass)
low_back.defvjp(back_keep, back_low)
norm_eps = 1e-05
masked_score = -1e+30

def matmul(left, right):
    return jnp.matmul(left, right, precision=lax.Precision.HIGHEST)

def layer_norm(hidden, gain, shift):
    center = hidden - lax.optimization_barrier(jnp.mean(hidden, axis=-1, keepdims=True))
    spread = lax.optimization_barrier(jnp.mean(center * center, axis=-1, keepdims=True))
    return center * lax.rsqrt(spread + norm_eps) * gain + shift

def attend(queries, key_rows, values, segment_ids):
    group, seq_length, model_width = queries.shape
    query_heads = queries.reshape(group, seq_length, H, HEAD)
    key_heads = key_rows.reshape(group, seq_length, H, HEAD)
    value_heads = values.reshape(group, seq_length, H, HEAD)
    scores = jnp.einsum('gqhd,gkhd->ghqk', query_heads, key_heads, precision=lax.Precision.HIGHEST) * HEAD ** (-0.5)
    same = segment_ids[:, None, :, None] == segment_ids[:, None, None, :]
    scores = low_back(jnp.where(same, scores, masked_score))
    probs = low(jax.nn.softmax(scores, axis=-1))
    mixed = jnp.einsum('ghqk,gkhd->gqhd', probs, value_heads, precision=lax.Precision.HIGHEST)
    return low(low_back(mixed.reshape(group, seq_length, model_width)))

def layer_forward(params, tokens_f, segment_ids):
    w_query, b_query, w_key, w_value, b_value, w_out, b_out, gain1, shift1, w_up, b_up, w_down, b_down, gain2, shift2 = params
    queries = low(low_back(matmul(tokens_f, w_query) + b_query))
    key_rows = low(low_back(matmul(tokens_f, w_key)))
    values = low(low_back(matmul(tokens_f, w_value) + b_value))
    mixed = attend(queries, key_rows, values, segment_ids)
    branch = low_back(matmul(mixed, w_out) + b_out)
    normed = layer_norm(tokens_f + branch, gain1, shift1)
    hidden = low_back(matmul(low(normed), w_up) + b_up)
    active = low(jax.nn.gelu(hidden, approximate=False))
    fed = low_back(matmul(active, w_down) + b_down)
    return layer_norm(normed + fed, gain2, shift2)

def pool_texts(result, segment_ids):
    onehot = (segment_ids[:, :, None] == jnp.arange(SEGS, dtype=jnp.int32)[None, None, :]).astype(jnp.float32)
    counts = lax.optimization_barrier(jnp.sum(onehot, axis=1))
    summed = jnp.einsum('rls,rld->rsd', onehot, result, precision=lax.Precision.HIGHEST)
    return summed / counts[:, :, None]

def reference(tokens, segments, w_query, b_query, w_key, w_value, b_value, w_out, b_out, gain1, shift1, w_up, b_up, w_down, b_down, gain2, shift2, out_grad):
    params = tuple((weight.astype(jnp.float32) for weight in (w_query, b_query, w_key, w_value, b_value, w_out, b_out, gain1, shift1, w_up, b_up, w_down, b_down, gain2, shift2)))
    tokens_f = tokens.astype(jnp.float32)
    seg_grouped = segments.reshape(ROWS // 8, 8, L)

    def group_step(weights, pair):
        result = layer_forward(weights, pair[0], pair[1])
        return (result, pool_texts(result, pair[1]))

    def forward(weights, inputs):
        grouped = inputs.reshape(ROWS // 8, 8, L, D)
        step_fn = jax.checkpoint(lambda pair: group_step(weights, pair))
        results, pooled_groups = lax.map(step_fn, (grouped, seg_grouped))
        return (results.reshape(ROWS, L, D), pooled_groups.reshape(ROWS, SEGS, D))
    result, pullback, pooled = jax.vjp(forward, params, tokens_f, has_aux=True)
    gradients, grad_input = pullback(out_grad.astype(jnp.float32))
    return (result.astype(jnp.bfloat16), pooled, grad_input.astype(jnp.bfloat16), gradients[0], gradients[1], gradients[2], gradients[3], gradients[4], gradients[5], gradients[6], gradients[7], gradients[8], gradients[9], gradients[10], gradients[11], gradients[12], gradients[13], gradients[14])
```

```python
import functools
import math

import jax
import jax.numpy as jnp
from jax import lax
from jax.experimental import pallas as pl
from jax.experimental.pallas import tpu as pltpu
from jax.sharding import PartitionSpec as P

BF = jnp.bfloat16
F32 = jnp.float32
HEAD = 64
SEGS = 8
BLOCK = 128
EPS = 1e-5
MASKED = -1e30
MESH = pl.DeviceIdType.MESH
VMEM_LIMIT = 61 * 2**20


def nn(a, b):
    return lax.dot_general(a, b, (((1,), (0,)), ((), ())), preferred_element_type=F32)


def nt(a, b):
    return lax.dot_general(a, b, (((1,), (1,)), ((), ())), preferred_element_type=F32)


def tn(a, b):
    return lax.dot_general(a, b, (((0,), (0,)), ((), ())), preferred_element_type=F32)


def rmean(t):
    return jnp.mean(t, axis=-1, keepdims=True)


def csum(t):
    return jnp.sum(t, axis=0, keepdims=True)


def loop(count, step):
    def body(i, carry):
        step(i)
        return carry

    lax.fori_loop(0, count, body, 0)


def ds(start, size, multiple=None):
    if not isinstance(start, int):
        start = pl.multiple_of(start, multiple or size)
    return pl.ds(start, size)


def key_windows(length):
    blocks = length // BLOCK
    spans, offsets, total = [], [], 0
    for qb in range(blocks):
        span = (max(qb - 1, 0), min(qb + 2, blocks))
        spans.append(span)
        offsets.append(total)
        total += (span[1] - span[0]) * BLOCK
    return spans, offsets, total


def stack2(pair):
    lane = lax.broadcasted_iota(jnp.int32, pair.shape, 1)
    zero = jnp.zeros_like(pair)
    return jnp.concatenate(
        [jnp.where(lane < HEAD, pair, zero), jnp.where(lane < HEAD, zero, pair)], axis=0
    )


def unstack_t(both):
    return jnp.concatenate([both[:HEAD, :BLOCK], both[HEAD:, BLOCK:]], axis=0).T


def make_bias(seg, bias):
    rows, length = seg.shape
    spans, offsets, _ = key_windows(length)
    for row in range(rows):
        ids = seg[row : row + 1, :].astype(F32)
        keys = jnp.broadcast_to(ids, (BLOCK, length)).T
        for qb, (k0, k1) in enumerate(spans):
            same = keys[k0 * BLOCK : k1 * BLOCK, :] == ids[:, qb * BLOCK : (qb + 1) * BLOCK]
            bias[row, offsets[qb] : offsets[qb] + (k1 - k0) * BLOCK, :] = jnp.where(
                same, 0.0, MASKED
            )


def attend_pair(i, length, pairs, q, k, v, o, probs, bias):
    spans, offsets, _ = key_windows(length)
    row, pair = i // pairs, i % pairs
    r0, c = pl.multiple_of(row * length, length), ds(pair * BLOCK, BLOCK)
    vt = v[pl.ds(r0, length), c].T
    for qb, (k0, k1) in enumerate(spans):
        n, at = (k1 - k0) * BLOCK, offsets[qb]
        mine = pl.ds(r0 + qb * BLOCK, BLOCK)
        q2 = stack2(q[mine, c] * BF(HEAD**-0.5))
        s = nt(k[pl.ds(r0 + k0 * BLOCK, n), c], q2)
        b = bias[row, at : at + n, :]
        s = s + jnp.concatenate([b, b], axis=1)
        e = jnp.exp(s - jnp.max(s, axis=0, keepdims=True))
        p = (e * (1.0 / jnp.sum(e, axis=0, keepdims=True))).astype(BF)
        probs[i, at : at + n, :] = p
        o[mine, c] = unstack_t(nn(vt[:, k0 * BLOCK : k1 * BLOCK], p)).astype(BF)


def attend_back_pair(i, length, pairs, q, k, v, do, probs, dq, dk, dv, dk_sum, dv_sum):
    spans, offsets, _ = key_windows(length)
    last = len(spans) - 1
    row, pair = i // pairs, i % pairs
    r0, c = pl.multiple_of(row * length, length), ds(pair * BLOCK, BLOCK)
    kt = k[pl.ds(r0, length), c].T
    for qb, (k0, k1) in enumerate(spans):
        n, at = (k1 - k0) * BLOCK, offsets[qb]
        mine = pl.ds(r0 + qb * BLOCK, BLOCK)
        q2 = stack2(q[mine, c] * BF(HEAD**-0.5))
        do2 = stack2(do[mine, c])
        dp = nt(v[pl.ds(r0 + k0 * BLOCK, n), c], do2)
        low = probs[i, at : at + n, :]
        p = low.astype(F32)
        d_s = (p * (dp - jnp.sum(p * dp, axis=0, keepdims=True))).astype(BF)
        dv_part = nn(low, do2)
        dk_part = nn(d_s, q2)
        for kb in range(k0, k1):
            part = slice((kb - k0) * BLOCK, (kb - k0 + 1) * BLOCK)
            held = slice(kb * BLOCK, (kb + 1) * BLOCK)
            a, b = dv_part[part], dk_part[part]
            if qb != max(kb - 1, 0):
                a, b = a + dv_sum[held, :], b + dk_sum[held, :]
            if qb == min(kb + 1, last):
                there = pl.ds(r0 + kb * BLOCK, BLOCK)
                dv[there, c] = a.astype(BF)
                dk[there, c] = b.astype(BF)
            else:
                dv_sum[held, :] = a
                dk_sum[held, :] = b
        dqt = nn(kt[:, k0 * BLOCK : k1 * BLOCK], d_s)
        dq[mine, c] = (unstack_t(dqt) * HEAD**-0.5).astype(BF)


class Place:
    def __init__(self, depth):
        self.depth = depth
        self.f = lax.axis_index("fsdp")
        self.y = lax.axis_index("rep")
        self.c = self.f % 2
        self.x = self.f // 2 % 2
        self.z = self.f // 4
        self.sib = (self.f + 1 - 2 * self.c, self.y)
        self.xn = (self.f + 2 - 4 * self.x, self.y)
        self.yn = (self.f, 1 - self.y)
        self.up = (self.f + 4, self.y)
        self.down = (self.f - 4, self.y)

    def barrier(self):
        sem = pltpu.get_barrier_semaphore()
        for who in (self.sib, self.xn, self.yn):
            pl.semaphore_signal(sem, inc=1, device_id=who, device_id_type=MESH)

        @pl.when(self.z > 0)
        def _():
            pl.semaphore_signal(sem, inc=1, device_id=self.down, device_id_type=MESH)

        @pl.when(self.z < self.depth - 1)
        def _():
            pl.semaphore_signal(sem, inc=1, device_id=self.up, device_id_type=MESH)

        inner = (self.z > 0).astype(jnp.int32) + (self.z < self.depth - 1).astype(jnp.int32)
        pl.semaphore_wait(sem, 3 + inner)


def remote(src, dst, send, recv, who):
    return pltpu.make_async_remote_copy(
        src_ref=src, dst_ref=dst, send_sem=send, recv_sem=recv, device_id=who, device_id_type=MESH
    )


def gather_sems(groups, depth):
    return [
        pltpu.SemaphoreType.DMA((groups, 2, depth - 1)),
        pltpu.SemaphoreType.DMA((groups, depth)),
        pltpu.SemaphoreType.DMA((groups, depth)),
        pltpu.SemaphoreType.DMA((groups, 3, depth)),
    ] * 2 + [pltpu.SemaphoreType.DMA((groups,))]


class Gather:
    def __init__(self, place, g, shard, whole, sems):
        self.p, self.g, self.shard, self.whole = place, g, shard, whole
        self.sz, self.sx, self.sy, self.sc, self.rz, self.rx, self.ry, self.rc, self.own = sems
        self.rows, self.cols = shard.shape

    def piece(self, z, x, half=None):
        f = (z * 2 + x) * 2 + self.p.c
        at = self.whole.at[ds(f * self.rows, self.rows, 16)]
        if half is None:
            return at
        return self.whole.at[ds(f * self.rows, self.rows, 16), ds(half * (self.cols // 2), self.cols // 2)]

    def piece_of(self, z, x, c):
        return self.whole.at[ds(((z * 2 + x) * 2 + c) * self.rows, self.rows, 16)]

    def copy_z(self, direction, distance, z, src=None):
        dst = self.piece(z, self.p.x)
        return remote(
            dst if src is None else src,
            dst,
            self.sz.at[self.g, direction, distance],
            self.rz.at[self.g, direction, distance],
            self.p.up if direction == 0 else self.p.down,
        )

    def copy_x(self, z, src=None):
        dst = self.piece(z, self.p.x, self.p.y)
        return remote(dst if src is None else src, dst, self.sx.at[self.g, z], self.rx.at[self.g, z], self.p.xn)

    def copy_y(self, z):
        at = self.piece(z, 1 - self.p.x, self.p.y)
        return remote(at, at, self.sy.at[self.g, z], self.ry.at[self.g, z], self.p.yn)

    def copy_c(self, kind, z, src=None):
        if kind == 0:
            dst = self.piece(z, self.p.x)
        else:
            half = self.p.y if kind == 1 else 1 - self.p.y
            dst = self.piece(z, 1 - self.p.x, half)
        return remote(
            dst if src is None else src,
            dst,
            self.sc.at[self.g, kind, z],
            self.rc.at[self.g, kind, z],
            self.p.sib,
        )

    def local(self):
        return pltpu.make_async_copy(self.shard, self.piece(self.p.z, self.p.x), self.own.at[self.g])

    def z_step(self, k):
        p = self.p
        if k == 0:
            self.local().start()

            @pl.when(p.z < p.depth - 1)
            def _():
                self.copy_z(0, 0, p.z, self.shard).start()

            @pl.when(p.z > 0)
            def _():
                self.copy_z(1, 0, p.z, self.shard).start()

            half = self.shard.at[:, ds(p.y * (self.cols // 2), self.cols // 2)]
            self.copy_x(p.z, half).start()
            self.copy_c(0, p.z, self.shard).start()
            return

        for direction in (0, 1):
            z = p.z - k if direction == 0 else p.z + k

            @pl.when(z >= 0 if direction == 0 else z < p.depth)
            def _(direction=direction, z=z):
                self.copy_z(direction, k - 1, z).wait_recv()
                if k < p.depth - 1:

                    @pl.when(p.z < p.depth - 1 if direction == 0 else p.z > 0)
                    def _():
                        self.copy_z(direction, k, z).start()

                self.copy_x(z).start()
                self.copy_c(0, z).start()

    def at_distance(self, k, act):
        p = self.p
        if k == 0:
            act(p.z)
            return

        @pl.when(p.z - k >= 0)
        def _():
            act(p.z - k)

        @pl.when(p.z + k < p.depth)
        def _():
            act(p.z + k)

    def x_step(self, k):
        def act(z):
            self.copy_x_in(z).wait_recv()
            self.copy_y_out(z).start()
            self.copy_c(1, z).start()

        self.at_distance(k, act)

    def copy_x_in(self, z):
        at = self.piece(z, 1 - self.p.x, self.p.y)
        return remote(at, at, self.sx.at[self.g, z], self.rx.at[self.g, z], self.p.xn)

    def copy_y_out(self, z):
        return self.copy_y(z)

    def copy_y_in(self, z):
        at = self.piece(z, 1 - self.p.x, 1 - self.p.y)
        return remote(at, at, self.sy.at[self.g, z], self.ry.at[self.g, z], self.p.yn)

    def y_step(self, k):
        def act(z):
            self.copy_y_in(z).wait_recv()
            self.copy_c(2, z).start()

        self.at_distance(k, act)

    def core_in(self, kind, z):
        p = self.p
        at = self.whole.at[ds(((z * 2 + (p.x if kind == 0 else 1 - p.x)) * 2 + 1 - p.c) * self.rows, self.rows, 16)]
        if kind:
            half = p.y if kind == 1 else 1 - p.y
            at = self.whole.at[
                ds(((z * 2 + 1 - p.x) * 2 + 1 - p.c) * self.rows, self.rows, 16),
                ds(half * (self.cols // 2), self.cols // 2),
            ]
        return remote(at, at, self.sc.at[self.g, kind, z], self.rc.at[self.g, kind, z], p.sib)

    def c_step(self):
        self.local().wait()
        for kind in range(3):
            for z in range(self.p.depth):
                self.core_in(kind, z).wait_recv()

    def end(self):
        p = self.p
        for k in range(p.depth - 1):
            @pl.when((p.z < p.depth - 1) & (p.z - k >= 0))
            def _():
                self.copy_z(0, k, p.z - k).wait_send()

            @pl.when((p.z > 0) & (p.z + k < p.depth))
            def _():
                self.copy_z(1, k, p.z + k).wait_send()

        for z in range(p.depth):
            self.copy_x(z).wait_send()
            self.copy_y(z).wait_send()
            for kind in range(3):
                self.copy_c(kind, z).wait_send()

    def steps(self):
        d = self.p.depth
        out = []
        for n in range(d + 2):
            def step(n=n):
                if n < d:
                    self.z_step(n)
                if 0 <= n - 1 < d:
                    self.x_step(n - 1)
                if 0 <= n - 2 < d:
                    self.y_step(n - 2)
            out.append(step)
        out.append(self.c_step)
        return out


def scatter_sems(groups, depth):
    kinds = [(groups, 2), (groups,), (groups,), (groups, 2, depth), (groups,)]
    return [pltpu.SemaphoreType.DMA(k) for k in kinds] * 2 + [pltpu.SemaphoreType.DMA((groups, 2))]


def scatter_buffers(rows, cols, depth):
    return [
        pltpu.VMEM((depth, 2, rows, cols), BF),
        pltpu.VMEM((2, depth, rows, cols), BF),
        pltpu.VMEM((depth, rows, cols // 2), BF),
        pltpu.VMEM((depth, rows, cols // 2), BF),
        pltpu.VMEM((2, depth, rows, cols), BF),
        pltpu.VMEM((rows, cols), BF),
    ]


def add_into(depth, rows, target, other):
    piece = min(rows, 48)
    parts = rows // piece

    def step(i):
        z, at = i // parts, ds(i % parts * piece, piece, 16)
        t = target(z, at)
        t[...] = t[...] + other(z, at)[...]

    loop(depth * parts, step)


class Scatter:
    def __init__(self, place, g, grad, out, buffers, sems):
        self.p, self.g, self.grad, self.out = place, g, grad, out
        self.acc, self.in_c, self.in_y, self.in_x, self.in_z, self.in_f = buffers
        (self.sc, self.sy, self.sx, self.sz, self.sf, self.rc, self.ry, self.rx, self.rz, self.rf, self.own) = sems
        self.depth, _, self.rows, self.cols = self.acc.shape

    def half(self, h):
        return ds(h * (self.cols // 2), self.cols // 2)

    def copy_c(self, x):
        p = self.p
        return remote(self.grad.at[:, x, 1 - p.c], self.in_c.at[x], self.sc.at[self.g, x], self.rc.at[self.g, x], p.sib)

    def load(self, x):
        return pltpu.make_async_copy(self.grad.at[:, x, self.p.c], self.acc.at[:, x], self.own.at[self.g, x])

    def copy_y(self):
        p = self.p
        return remote(
            self.acc.at[:, 1 - p.x, :, self.half(1 - p.y)], self.in_y, self.sy.at[self.g], self.ry.at[self.g], p.yn
        )

    def copy_x(self):
        p = self.p
        return remote(
            self.acc.at[:, 1 - p.x, :, self.half(p.y)], self.in_x, self.sx.at[self.g], self.rx.at[self.g], p.xn
        )

    def copy_z(self, direction, z):
        p = self.p
        return remote(
            self.acc.at[z, p.x],
            self.in_z.at[direction, z],
            self.sz.at[self.g, direction, z],
            self.rz.at[self.g, direction, z],
            p.up if direction == 0 else p.down,
        )

    def copy_f(self):
        p = self.p
        return remote(self.acc.at[p.z, p.x], self.in_f, self.sf.at[self.g], self.rf.at[self.g], p.yn)

    def begin(self):
        for turn in (0, 1):
            x = 1 - self.p.x if turn == 0 else self.p.x
            self.copy_c(x).start()
            self.load(x).start()

    def cores(self, turn):
        p = self.p
        x = 1 - p.x if turn == 0 else p.x
        self.load(x).wait()
        self.copy_c(x).wait_recv()
        add_into(
            self.depth,
            self.rows,
            lambda z, at: self.acc.at[z, x, at],
            lambda z, at: self.in_c.at[x, z, at],
        )
        if turn == 0:
            self.copy_y().start()

    def over_y(self):
        p = self.p
        self.copy_y().wait_recv()
        add_into(
            self.depth,
            self.rows,
            lambda z, at: self.acc.at[z, 1 - p.x, at, self.half(p.y)],
            lambda z, at: self.in_y.at[z, at],
        )
        self.copy_x().start()

    def over_x(self):
        p = self.p
        self.copy_x().wait_recv()
        add_into(
            self.depth,
            self.rows,
            lambda z, at: self.acc.at[z, p.x, at, self.half(p.y)],
            lambda z, at: self.in_x.at[z, at],
        )

    def line(self, wave):
        p, top = self.p, self.depth - 1
        for direction in (0, 1):
            place = p.z if direction == 0 else top - p.z
            if wave == 0:

                @pl.when(place == 0)
                def _(direction=direction):
                    for far in range(top, 0, -1):
                        self.copy_z(direction, far if direction == 0 else top - far).start()

                continue

            @pl.when((place >= 1) & (place <= wave))
            def _(direction=direction, place=place):
                far = top - wave + place
                z = far if direction == 0 else top - far
                self.copy_z(direction, z).wait_recv()
                add_into(
                    1,
                    self.rows,
                    lambda _, at: self.acc.at[z, p.x, at],
                    lambda _, at: self.in_z.at[direction, z, at],
                )

                @pl.when(far > place)
                def _():
                    self.copy_z(direction, z).start()

    def share(self):
        self.copy_f().start()

    def finish(self):
        p = self.p
        self.copy_f().wait_recv()
        piece = min(self.rows, 48)

        def step(i):
            at = ds(i * piece, piece, 16)
            self.out[at, :] = self.acc[p.z, p.x, at, :].astype(F32) + self.in_f[at, :].astype(F32)

        loop(self.rows // piece, step)

    def end(self):
        p, top = self.p, self.depth - 1
        for x in (0, 1):
            self.copy_c(x).wait_send()
        self.copy_y().wait_send()
        self.copy_x().wait_send()
        for direction in (0, 1):
            for z in range(self.depth):

                @pl.when(p.z < z if direction == 0 else p.z > z)
                def _(direction=direction, z=z):
                    self.copy_z(direction, z).wait_send()

        self.copy_f().wait_send()

    def steps(self):
        def over_x_and_line():
            self.over_x()
            self.line(0)

        out = [lambda: self.cores(0), lambda: self.cores(1), self.over_y, over_x_and_line]
        for k in range(1, self.depth):
            out.append(functools.partial(self.line, k))
        out.append(self.share)
        out.append(self.finish)
        return out


def spread(width, owners_rows, parts):
    row = lax.broadcasted_iota(jnp.int32, (width, 1), 0)
    target = row
    for owner in range(1, width // owners_rows):
        target = target + jnp.where(row >= owner * owners_rows, (parts - 1) * owners_rows, 0)
    lane = lax.broadcasted_iota(jnp.int32, (width, width * parts), 1)
    return (lane == target).astype(BF)


def unpack_small(columns, shard, parts, vec, bup):
    rows = columns.astype(F32).T
    vec[...] = rows[:8, :]
    low = rows[8:16, :].astype(BF)
    width = 8 * shard
    place = spread(width, shard, parts)
    for t in range(columns.shape[0] // width):
        wide = nn(low[:, t * width : (t + 1) * width], place)
        total = wide[0:1]
        for i in range(1, parts):
            total = total + pltpu.roll(wide, i * shard, 1)[i : i + 1]
        bup[:, t * width * parts : (t + 1) * width * parts] = total


def pack_small(gv, gbu, shard, parts):
    width = 8 * shard
    model = gv.shape[1]
    place = spread(width, shard, parts)
    rows = []
    for i in range(parts):
        pieces = []
        for t in range(model // width):
            wide = jnp.broadcast_to(gbu[:, t * width * parts : (t + 1) * width * parts], (8, width * parts))
            if i:
                wide = pltpu.roll(wide, width * parts - i * shard, 1)
            pieces.append(nt(wide.astype(BF), place)[0:1])
        rows.append(jnp.concatenate(pieces, axis=1))
    blank = jnp.zeros((BLOCK - 8 - parts, model), F32)
    return jnp.concatenate([gv] + rows + [blank], axis=0).T.astype(BF)


ROWS = 256
CHUNK = 512


def phi_parts(u):
    cdf = 0.5 * (1.0 + lax.erf(u * math.sqrt(0.5)))
    pdf = jnp.exp(-0.5 * u * u) * (1.0 / math.sqrt(2.0 * math.pi))
    return cdf, pdf


def project(x, wa, vec, q, k, v):
    model = x.shape[1]

    def step(rt):
        rows = ds(rt * ROWS, ROWS)
        q[rows, :] = (nn(x[rows, :], wa[:, :model]) + vec[0:1, :]).astype(BF)
        k[rows, :] = nn(x[rows, :], wa[:, model : 2 * model]).astype(BF)
        v[rows, :] = (nn(x[rows, :], wa[:, 2 * model : 3 * model]) + vec[1:2, :]).astype(BF)

    loop(x.shape[0] // ROWS, step)


def ticked(count, step, ticks):
    def body(i):
        step(i)
        for n, tasks in enumerate(ticks):
            if tasks:

                @pl.when(i == n)
                def _(tasks=tasks):
                    for task in tasks:
                        task()

    loop(count, body)


def forward_kernel(depth, parts, *refs):
    (x, seg, sa, so, su, sd, q, k, v, o, probs, vec, bup, wa, wo, wu, wd, bias, *sems) = refs
    length, pairs = seg.shape[1], x.shape[1] // BLOCK
    place = Place(depth)
    ga, go, gu, gd = [
        Gather(place, g, shard, whole, sems)
        for g, (shard, whole) in enumerate(((sa, wa), (so, wo), (su, wu), (sd, wd)))
    ]
    a, b, c, d = ga.steps(), go.steps(), gu.steps(), gd.steps()
    place.barrier()
    for task in [a[0], a[1], b[0], a[2], c[0], a[3], d[0]]:
        task()
    make_bias(seg, bias)
    for task in a[4:]:
        task()
    model = x.shape[1]
    unpack_small(wa[:, 3 * model : 3 * model + BLOCK], sa.shape[0], parts, vec, bup)
    project(x, wa, vec, q, k, v)
    ticks = [[] for _ in range(seg.shape[0] * pairs)]
    order = [b[1], b[2], c[1], b[3], c[2], b[4], c[3], d[1], b[5], c[4], d[2], c[5], d[3]]
    for n, task in enumerate(order):
        ticks[min(n, len(ticks) - 1)].append(task)
    ticked(len(ticks), lambda i: attend_pair(i, length, pairs, q, k, v, o, probs, bias), ticks)
    for task in d[4:6] + [b[6], c[6], d[6]]:
        task()
    for one in (ga, go, gu, gd):
        one.end()


def mid_kernel(*refs):
    (x, o, og, seg, wo, wu, wd, vec, bup, out, pooled, g_down, g_up, g_out, do, dh1, gv, gbu,
     n1s, r1s, z_low, g, sl, df, dh2) = refs
    tokens, model = x.shape
    hidden = wu.shape[1]
    seqs, length = seg.shape
    gv[...] = jnp.zeros_like(gv)
    pooled[...] = jnp.zeros_like(pooled)

    def vrow(i):
        return vec[i : i + 1, :]

    def up(rt):
        rows = ds(rt * ROWS, ROWS)
        h = x[rows, :].astype(F32) + (nn(o[rows, :], wo[...]) + vrow(2))
        c = h - rmean(h)
        r = lax.rsqrt(rmean(c * c) + EPS)
        n = c * r
        n1s[rows, :] = n
        r1s[rows, :] = jnp.broadcast_to(r, (ROWS, BLOCK))
        z_low[rows, :] = (n * vrow(3) + vrow(4)).astype(BF)
        for cc in range(hidden // CHUNK):
            cs = slice(cc * CHUNK, (cc + 1) * CHUNK)
            u = nn(z_low[rows, :], wu[:, cs]) + bup[:, cs]
            cdf, pdf = phi_parts(u)
            g[rows, cs] = (u * cdf).astype(BF)
            sl[rows, cs] = (cdf + u * pdf).astype(BF)

    loop(tokens // ROWS, up)

    def down(rt):
        rows = ds(rt * ROWS, ROWS)
        h = (n1s[rows, :] * vrow(3) + vrow(4)) + (nn(g[rows, :], wd[...]) + vrow(5))
        c = h - rmean(h)
        r = lax.rsqrt(rmean(c * c) + EPS)
        n2 = c * r
        y = n2 * vrow(6) + vrow(7)
        y_low = y.astype(BF)
        out[rows, :] = y_low
        row = rt * ROWS // length
        ids = seg[pl.ds(row, 1), ds(rt * ROWS % length, ROWS)]
        onehot = (ids == lax.broadcasted_iota(jnp.int32, (SEGS, ROWS), 0)).astype(BF)
        pooled[row] = pooled[row] + (nn(onehot, y_low) + nn(onehot, (y - y_low.astype(F32)).astype(BF)))
        dy = og[rows, :].astype(F32)
        gv[6:7, :] += csum(dy * n2)
        gv[7:8, :] += csum(dy)
        e = dy * vrow(6)
        d = r * (e - rmean(e) - n2 * rmean(e * n2))
        dh2[rows, :] = d
        low = d.astype(BF)
        df[rows, :] = low
        gv[5:6, :] += csum(low.astype(F32))

    loop(tokens // ROWS, down)
    for row in range(seqs):
        onehot = (seg[row : row + 1, :] == lax.broadcasted_iota(jnp.int32, (SEGS, length), 0)).astype(F32)
        pooled[row] = pooled[row] / jnp.sum(onehot, axis=1, keepdims=True)

    def down_grad(cc):
        cs = ds(cc * CHUNK, CHUNK)
        g_down[cs, :] = tn(g[:, cs], df[...]).astype(BF)

    loop(hidden // CHUNK, down_grad)

    def up_back(cc):
        cs = ds(cc * CHUNK, CHUNK)
        total = jnp.zeros((1, CHUNK), F32)
        for rt in range(tokens // ROWS):
            rows = slice(rt * ROWS, (rt + 1) * ROWS)
            du = (nt(df[rows, :], wd[cs, :]) * sl[rows, cs].astype(F32)).astype(BF)
            sl[rows, cs] = du
            total += csum(du.astype(F32))
        gbu[:, cs] = total
        g_up[:, cs] = tn(z_low[...], sl[:, cs]).astype(BF)

    loop(hidden // CHUNK, up_back)

    def first_back(rt):
        rows = ds(rt * ROWS, ROWS)
        dz = dh2[rows, :] + nt(sl[rows, :], wu[...])
        n1 = n1s[rows, :]
        gv[3:4, :] += csum(dz * n1)
        gv[4:5, :] += csum(dz)
        e = dz * vrow(3)
        d = r1s[rows, 0:1] * (e - rmean(e) - n1 * rmean(e * n1))
        dh1[rows, :] = d
        da = d.astype(BF)
        df[rows, :] = da
        gv[2:3, :] += csum(da.astype(F32))
        do[rows, :] = nt(da, wo[...]).astype(BF)

    loop(tokens // ROWS, first_back)

    def out_grad_step(cc):
        cs = ds(cc * (model // 2), model // 2)
        g_out[cs, :] = tn(o[:, cs], df[...]).astype(BF)

    loop(2, out_grad_step)


def qkv_grads(x, dqkv, store):
    model = x.shape[1]
    part = model // 2
    for n, d in enumerate(dqkv):

        def step(t, n=n, d=d):
            store(n, t, tn(x[:, ds(t * part, part, BLOCK)], d[...]).astype(BF))

        loop(2, step)


def token_grads(dh1, dqkv, wa, out):
    model = dh1.shape[1]

    def step(rt):
        rows = ds(rt * ROWS, ROWS)
        total = dh1[rows, :]
        for n, d in enumerate(dqkv):
            total = total + nt(d[rows, :], wa[:, n * model : (n + 1) * model])
        out[rows, :] = total.astype(BF)

    loop(dh1.shape[0] // ROWS, step)


def schedule(sizes, begins, gather_gbs=90.0, core_gbs=350.0, delay=1.5):
    import heapq

    free = {"y": 0.0, "x": 0.0, "z": 0.0, "c": 0.0}
    heap, found = [], []

    def send(link, at, size):
        rate = core_gbs if link == "c" else gather_gbs / 2
        start = max(at, free[link])
        free[link] = start + size / rate * 1e-3
        return free[link] + delay

    for g, size in enumerate(sizes):
        heapq.heappush(heap, (begins[g], g, -1))
    while heap:
        at, g, step = heapq.heappop(heap)
        size = sizes[g]
        if step >= 0:
            found.append((at, g, step))
        if step == -1:
            heapq.heappush(heap, (send("c", at, 4 * size), g, 0))
            heapq.heappush(heap, (send("c", at, 4 * size), g, 1))
        elif step == 0:
            heapq.heappush(heap, (send("y", at + 0.5, 2 * size), g, 2))
        elif step == 2:
            heapq.heappush(heap, (send("x", at + 0.5, 2 * size), g, 3))
        elif step in (3, 4, 5):
            heapq.heappush(heap, (send("z", at + 0.5, size), g, step + 1))
        elif step == 6:
            heapq.heappush(heap, (at + 0.2, g, 7))
        elif step == 7:
            heapq.heappush(heap, (send("y", at, size), g, 8))
    return found


def backward_kernel(depth, parts, length, cuts, *refs):
    count = len(cuts)
    (q, k, v, do, probs, x, dh1, wa, g_down, g_up, g_out, gv, gbu, gtok, oa, oo, ou, od, small,
     dq, dk, dv, dk_sum, dv_sum, g_all, *rest) = refs
    sets = [rest[6 * n : 6 * n + 6] for n in range(count)]
    sems = rest[6 * count :]
    pairs = x.shape[1] // BLOCK
    model = x.shape[1]
    place = Place(depth)
    sources = {"a": (g_all, oa), "o": (g_out, oo), "u": (g_up, ou), "d": (g_down, od)}
    scatters = []
    for n, (name, r0, rows, c0, cols) in enumerate(cuts):
        grad, out = sources[name]
        scatters.append(
            Scatter(place, n, grad.at[:, :, :, r0 : r0 + rows, c0 : c0 + cols], out.at[r0 : r0 + rows, c0 : c0 + cols], sets[n], sems)
        )
    steps = [s.steps() for s in scatters]
    early = [n for n, cut in enumerate(cuts) if cut[0] != "a"]
    late = [n for n, cut in enumerate(cuts) if cut[0] == "a"]
    iterations = x.shape[0] // length * pairs
    per, tail = 2.3, 8.0
    begins = [0.0 if n in early else per * iterations + tail for n in range(count)]
    sizes = [rows * cols * 2 for _, _, rows, _, cols in cuts]
    found = schedule(sizes, begins)
    ticks = [[] for _ in range(iterations)]
    after = []
    for at, g, step in found:
        n = int(at // per)
        (ticks[n] if n < iterations else after).append(steps[g][step])
    place.barrier()
    for n in early:
        scatters[n].begin()
    ticked(
        iterations,
        lambda i: attend_back_pair(i, length, pairs, q, k, v, do, probs, dq, dk, dv, dk_sum, dv_sum),
        ticks,
    )
    half = model // 2
    owners = half // oo.shape[0]

    def store(n, t, value):
        shaped = value.reshape(owners // 4, 2, 2, oo.shape[0], model)
        g_all[pl.ds(t * (owners // 4), owners // 4), :, :, :, n * model : (n + 1) * model] = shaped

    qkv_grads(x, (dq, dk, dv), store)
    bq, bv = csum(dq[...].astype(F32)), csum(dv[...].astype(F32))
    vectors = jnp.concatenate([bq, bv, gv[2:8, :]], axis=0)
    columns = pack_small(vectors, gbu[...], oo.shape[0], parts)
    shaped = columns.reshape(depth, 2, 2, oo.shape[0], BLOCK)
    g_all[:, :, :, :, 3 * model : 3 * model + BLOCK] = shaped
    g_all[:, :, :, :, 3 * model + BLOCK :] = jnp.zeros_like(shaped)
    for n in late:
        scatters[n].begin()
    token_grads(dh1, (dq, dk, dv), wa, gtok)
    for task in after:
        task()
    for s in scatters:
        s.end()
    last = oa[:, 3 * model : 3 * model + BLOCK]
    square = jnp.concatenate([last, jnp.zeros((BLOCK - last.shape[0], BLOCK), F32)], axis=0).T
    small[...] = square[:16, :]


V = pl.BlockSpec(memory_space=pltpu.VMEM)
ANY = pl.BlockSpec(memory_space=pl.ANY)
sds = jax.ShapeDtypeStruct


def params(collective_id=None):
    if collective_id is None:
        return pltpu.CompilerParams(vmem_limit_bytes=VMEM_LIMIT)
    return pltpu.CompilerParams(
        vmem_limit_bytes=VMEM_LIMIT, collective_id=collective_id, has_side_effects=True
    )


def run_forward(depth, x, seg, sa, so, su, sd):
    tokens, model = x.shape
    owners = depth * 4
    hidden = su.shape[1]
    parts = hidden // model
    seqs, length = seg.shape
    band = key_windows(length)[2]
    act = sds((tokens, model), BF)
    wholes = [sds((owners * s.shape[0], s.shape[1]), BF) for s in (sa, so, su, sd)]
    return pl.pallas_call(
        functools.partial(forward_kernel, depth, parts),
        out_shape=(act, act, act, act, sds((seqs * model // BLOCK, band, 2 * BLOCK), BF),
                   sds((8, model), F32), sds((1, hidden), F32), *wholes),
        in_specs=[V, V, ANY, ANY, ANY, ANY],
        out_specs=(V,) * 8 + (ANY,) * 3,
        scratch_shapes=[pltpu.VMEM((seqs, band, BLOCK), F32)] + gather_sems(4, depth),
        compiler_params=params(0),
        name="forward",
    )(x, seg, sa, so, su, sd)


def run_mid(x, o, og, seg, wo, wu, wd, vec, bup):
    tokens, model = x.shape
    hidden = wu.shape[1]
    wide = pltpu.VMEM((tokens, hidden), BF)
    act = sds((tokens, model), BF)
    return pl.pallas_call(
        mid_kernel,
        out_shape=(act, sds((seg.shape[0], SEGS, model), F32), sds(wd.shape, BF), sds(wu.shape, BF), sds(wo.shape, BF),
                   act, sds((tokens, model), F32), sds((8, model), F32), sds((1, hidden), F32)),
        in_specs=[V] * 9,
        out_specs=(V,) * 9,
        scratch_shapes=[pltpu.VMEM((tokens, model), F32), pltpu.VMEM((tokens, BLOCK), F32), pltpu.VMEM((tokens, model), BF),
                        wide, wide, pltpu.VMEM((tokens, model), BF), pltpu.VMEM((tokens, model), F32)],
        compiler_params=params(),
        name="middle",
    )(x, o, og, seg, wo, wu, wd, vec, bup)


def run_backward(depth, length, shards, q, k, v, do, probs, x, dh1, wa, g_down, g_up, g_out, gv, gbu):
    tokens, model = x.shape
    sa, so, su, sd = shards
    parts = su[1] // model

    def owned(t, s):
        return t.reshape(depth, 2, 2, *s)

    cuts = [("o", 0, so[0], 0, so[1])]
    for part in range(2):
        cuts.append(("d", part * (sd[0] // 2), sd[0] // 2, 0, sd[1]))
    for part in range(2):
        cuts.append(("u", 0, su[0], part * (su[1] // 2), su[1] // 2))
    for part in range(2):
        cuts.append(("a", 0, sa[0], part * (sa[1] // 2), sa[1] // 2))
    buffers = []
    for _, _, rows, _, cols in cuts:
        buffers += scatter_buffers(rows, cols, depth)
    act = pltpu.VMEM((tokens, model), BF)
    half_sum = pltpu.VMEM((length, BLOCK), F32)
    return pl.pallas_call(
        functools.partial(backward_kernel, depth, parts, length, tuple(cuts)),
        out_shape=(sds((tokens, model), BF), sds(sa, F32), sds(so, F32), sds(su, F32), sds(sd, F32), sds((16, BLOCK), F32)),
        in_specs=[V] * 8 + [ANY] * 3 + [V] * 2,
        out_specs=(V,) * 6,
        scratch_shapes=[act, act, act, half_sum, half_sum, pltpu.VMEM((depth, 2, 2, *sa), BF), *buffers,
                        *scatter_sems(len(cuts), depth)],
        compiler_params=params(1),
        name="backward",
    )(q, k, v, do, probs, x, dh1, wa, owned(g_down, sd), owned(g_up, su), owned(g_out, so), gv, gbu)


def local_ring(depth, *args):
    (tokens, segments, w_query, b_query, w_key, w_value, b_value, w_out, b_out, gain1, shift1, w_up, b_up, w_down,
     b_down, gain2, shift2, out_grad) = args
    seqs, length, model = tokens.shape
    shard = w_query.shape[0]
    parts = w_up.shape[1] // model
    x = tokens.reshape(seqs * length, model)
    og = out_grad.reshape(seqs * length, model)
    small = jnp.stack([b_query, b_value, b_out, gain1, shift1, b_down, gain2, shift2] + [
        b_up[i * shard : (i + 1) * shard] for i in range(parts)
    ], axis=1)
    small = jnp.pad(small, ((0, 0), (0, 2 * BLOCK - 8 - parts)))
    sa = jnp.concatenate([w_query, w_key, w_value, small], axis=1)
    q, k, v, o, probs, vec, bup, wa, wo, wu, wd = run_forward(depth, x, segments, sa, w_out, w_up, w_down)
    out, pooled, g_down, g_up, g_out, do, dh1, gv, gbu = run_mid(x, o, og, segments, wo, wu, wd, vec, bup)
    gtok, ga, go, gu, gd, gs = run_backward(
        depth, length, (sa.shape, w_out.shape, w_up.shape, w_down.shape),
        q, k, v, do, probs, x, dh1, wa, g_down, g_up, g_out, gv, gbu,
    )
    vectors = [gs[i, :shard] for i in range(8)]
    gbq, gbv, gbo, gg1, gs1, gbd, gg2, gs2 = vectors
    gb_up = gs[8 : 8 + parts, :shard].reshape(parts * shard)
    return (
        out.reshape(tokens.shape), pooled, gtok.reshape(tokens.shape),
        ga[:, :model], gbq, ga[:, model : 2 * model], ga[:, 2 * model : 3 * model], gbv,
        go, gbo, gg1, gs1, gu, gb_up, gd, gbd, gg2, gs2,
    )


def qkv_kernel(x, wa, vec, seg, q, k, v, o, probs, bias):
    length, pairs = seg.shape[1], x.shape[1] // BLOCK
    make_bias(seg, bias)
    project(x, wa, vec, q, k, v)
    loop(seg.shape[0] * pairs, lambda i: attend_pair(i, length, pairs, q, k, v, o, probs, bias))


def back_kernel(length, q, k, v, do, probs, x, dh1, wa, gtok, g_qkv, gb, dq, dk, dv, dk_sum, dv_sum):
    pairs, model = x.shape[1] // BLOCK, x.shape[1]
    loop(
        x.shape[0] // length * pairs,
        lambda i: attend_back_pair(i, length, pairs, q, k, v, do, probs, dq, dk, dv, dk_sum, dv_sum),
    )

    def store(n, t, value):
        g_qkv[ds(t * (model // 2), model // 2), n * model : (n + 1) * model] = value

    qkv_grads(x, (dq, dk, dv), store)
    token_grads(dh1, (dq, dk, dv), wa, gtok)
    gb[...] = jnp.concatenate([csum(dq[...].astype(F32)), csum(dv[...].astype(F32)), jnp.zeros((6, model), F32)], axis=0)


def local_plain(*args):
    (tokens, segments, w_query, b_query, w_key, w_value, b_value, w_out, b_out, gain1, shift1, w_up, b_up, w_down,
     b_down, gain2, shift2, out_grad) = args
    seqs, length, model = tokens.shape
    count = seqs * length
    band = key_windows(length)[2]
    x = tokens.reshape(count, model)
    og = out_grad.reshape(count, model)

    def gathered(t):
        return lax.all_gather(t, "fsdp", axis=0, tiled=True)

    wa = gathered(jnp.concatenate([w_query, w_key, w_value], axis=1))
    small = gathered(jnp.stack([b_query, b_value, b_out, gain1, shift1, b_down, gain2, shift2], axis=1))
    vec = small.T.astype(F32)
    bup = gathered(b_up).astype(F32)[None]
    wo, wu, wd = gathered(w_out), gathered(w_up), gathered(w_down)
    act = sds((count, model), BF)
    q, k, v, o, probs = pl.pallas_call(
        qkv_kernel,
        out_shape=(act, act, act, act, sds((seqs * model // BLOCK, band, 2 * BLOCK), BF)),
        in_specs=[V] * 4,
        out_specs=(V,) * 5,
        scratch_shapes=[pltpu.VMEM((seqs, band, BLOCK), F32)],
        compiler_params=params(),
        name="attention",
    )(x, wa, vec, segments)
    out, pooled, g_down, g_up, g_out, do, dh1, gv, gbu = run_mid(x, o, og, segments, wo, wu, wd, vec, bup)
    kept = pltpu.VMEM((count, model), BF)
    part = pltpu.VMEM((length, BLOCK), F32)
    gtok, g_qkv, gb = pl.pallas_call(
        functools.partial(back_kernel, length),
        out_shape=(act, sds((model, 3 * model), BF), sds((8, model), F32)),
        in_specs=[V] * 8,
        out_specs=(V,) * 3,
        scratch_shapes=[kept, kept, kept, part, part],
        compiler_params=params(),
        name="attention_back",
    )(q, k, v, do, probs, x, dh1, wa)
    vectors = jnp.concatenate([gb[:2], gv[2:8]], axis=0).T

    def shared(t):
        mine = lax.psum_scatter(t.astype(F32), "fsdp", scatter_dimension=0, tiled=True)
        return lax.psum(mine.astype(BF), "rep").astype(F32)

    ga, gs = shared(g_qkv), shared(vectors)
    go, gu, gd, gb_up = shared(g_out), shared(g_up), shared(g_down), shared(gbu[0])
    gbq, gbv, gbo, gg1, gs1, gbd, gg2, gs2 = [gs[:, i] for i in range(8)]
    return (
        out.reshape(tokens.shape), pooled, gtok.reshape(tokens.shape),
        ga[:, :model], gbq, ga[:, model : 2 * model], ga[:, 2 * model :], gbv,
        go, gbo, gg1, gs1, gu, gb_up, gd, gbd, gg2, gs2,
    )


def solution(mesh):
    rows = P(("fsdp", "rep"))
    split = P("fsdp")
    placed = (rows, rows) + (split,) * 15 + (rows,)
    results = (rows,) * 3 + (split,) * 15
    owners = mesh.shape["fsdp"]

    def whole(*args):
        shard = args[2].shape[0] // owners
        ring = owners % 4 == 0 and mesh.shape["rep"] == 2 and shard % 16 == 0
        body = functools.partial(local_ring, owners // 4) if ring else local_plain
        return jax.shard_map(body, mesh=mesh, in_specs=placed, out_specs=results, check_vma=False)(*args)

    return whole
```

```python
import functools
import heapq
import math

import jax
import jax.numpy as jnp
from jax import lax
from jax.experimental import pallas as pl
from jax.experimental.pallas import tpu as pltpu
from jax.sharding import PartitionSpec as P

BF = jnp.bfloat16
F32 = jnp.float32
HEAD = 64
SEGS = 8
BLOCK = 128
EPS = 1e-5
MASKED = -1e30
MESH = pl.DeviceIdType.MESH
VMEM_LIMIT = int(63.5 * 2**20)


def nn(a, b):
    return lax.dot_general(a, b, (((1,), (0,)), ((), ())), preferred_element_type=F32)


def nt(a, b):
    return lax.dot_general(a, b, (((1,), (1,)), ((), ())), preferred_element_type=F32)


def tn(a, b):
    return lax.dot_general(a, b, (((0,), (0,)), ((), ())), preferred_element_type=F32)


def rmean(t):
    return jnp.mean(t, axis=-1, keepdims=True)


def csum(t):
    return jnp.sum(t, axis=0, keepdims=True)


def loop(count, step):
    def body(i, carry):
        step(i)
        return carry

    lax.fori_loop(0, count, body, 0)


def ds(start, size, multiple=None):
    if not isinstance(start, int):
        start = pl.multiple_of(start, multiple or size)
    return pl.ds(start, size)


def key_windows(length):
    blocks = length // BLOCK
    spans, offsets, total = [], [], 0
    for qb in range(blocks):
        span = (max(qb - 1, 0), min(qb + 2, blocks))
        spans.append(span)
        offsets.append(total)
        total += (span[1] - span[0]) * BLOCK
    return spans, offsets, total


def stack2(pair):
    lane = lax.broadcasted_iota(jnp.int32, pair.shape, 1)
    zero = jnp.zeros_like(pair)
    return jnp.concatenate(
        [jnp.where(lane < HEAD, pair, zero), jnp.where(lane < HEAD, zero, pair)], axis=0
    )


def unstack_t(both):
    return jnp.concatenate([both[:HEAD, :BLOCK], both[HEAD:, BLOCK:]], axis=0).T


def make_bias(seg, bias_at):
    rows, length = seg.shape
    spans, _, _ = key_windows(length)
    for row in range(rows):
        ids = seg[row : row + 1, :].astype(F32)
        keys = jnp.broadcast_to(ids, (BLOCK, length)).T
        for qb, (k0, k1) in enumerate(spans):
            same = keys[k0 * BLOCK : k1 * BLOCK, :] == ids[:, qb * BLOCK : (qb + 1) * BLOCK]
            bias_at(row, qb)[...] = jnp.where(same, 0.0, MASKED)


def attend_pair(i, length, pairs, q, k, v, o, probs_at, bias_at):
    spans, _, _ = key_windows(length)
    row, pair = i // pairs, i % pairs
    r0, c = pl.multiple_of(row * length, length), ds(pair * BLOCK, BLOCK)
    vt = v[pl.ds(r0, length), c].T
    for qb, (k0, k1) in enumerate(spans):
        n = (k1 - k0) * BLOCK
        mine = pl.ds(r0 + qb * BLOCK, BLOCK)
        q2 = stack2(q[mine, c] * BF(HEAD**-0.5))
        s = nt(k[pl.ds(r0 + k0 * BLOCK, n), c], q2)
        b = bias_at(row, qb)[...]
        s = s + jnp.concatenate([b, b], axis=1)
        e = jnp.exp(s - jnp.max(s, axis=0, keepdims=True))
        p = (e * (1.0 / jnp.sum(e, axis=0, keepdims=True))).astype(BF)
        probs_at(i, qb)[...] = p
        o[mine, c] = unstack_t(nn(vt[:, k0 * BLOCK : k1 * BLOCK], p)).astype(BF)


def attend_back_pair(i, length, pairs, q, k, v, do, probs_at, dq, dk, dv, dk_sum, dv_sum):
    spans, _, _ = key_windows(length)
    last = len(spans) - 1
    row, pair = i // pairs, i % pairs
    r0, c = pl.multiple_of(row * length, length), ds(pair * BLOCK, BLOCK)
    kt = k[pl.ds(r0, length), c].T
    for qb, (k0, k1) in enumerate(spans):
        n = (k1 - k0) * BLOCK
        mine = pl.ds(r0 + qb * BLOCK, BLOCK)
        q2 = stack2(q[mine, c] * BF(HEAD**-0.5))
        do2 = stack2(do[mine, c])
        dp = nt(v[pl.ds(r0 + k0 * BLOCK, n), c], do2)
        low = probs_at(i, qb)[...]
        p = low.astype(F32)
        d_s = (p * (dp - jnp.sum(p * dp, axis=0, keepdims=True))).astype(BF)
        dv_part = nn(low, do2)
        dk_part = nn(d_s, q2)
        for kb in range(k0, k1):
            part = slice((kb - k0) * BLOCK, (kb - k0 + 1) * BLOCK)
            held = slice(kb * BLOCK, (kb + 1) * BLOCK)
            a, b = dv_part[part], dk_part[part]
            if qb != max(kb - 1, 0):
                a, b = a + dv_sum[held, :], b + dk_sum[held, :]
            if qb == min(kb + 1, last):
                there = pl.ds(r0 + kb * BLOCK, BLOCK)
                dv[there, c] = a.astype(BF)
                dk[there, c] = b.astype(BF)
            else:
                dv_sum[held, :] = a
                dk_sum[held, :] = b
        dqt = nn(kt[:, k0 * BLOCK : k1 * BLOCK], d_s)
        dq[mine, c] = (unstack_t(dqt) * HEAD**-0.5).astype(BF)


class Place:
    def __init__(self, depth):
        self.depth = depth
        self.f = lax.axis_index("fsdp")
        self.y = lax.axis_index("rep")
        self.c = self.f % 2
        self.x = self.f // 2 % 2
        self.z = self.f // 4
        self.sib = (self.f + 1 - 2 * self.c, self.y)
        self.xn = (self.f + 2 - 4 * self.x, self.y)
        self.yn = (self.f, 1 - self.y)
        self.up = (self.f + 4, self.y)
        self.down = (self.f - 4, self.y)

    def barrier(self):
        sem = pltpu.get_barrier_semaphore()
        for who in (self.sib, self.xn, self.yn):
            pl.semaphore_signal(sem, inc=1, device_id=who, device_id_type=MESH)

        @pl.when(self.z > 0)
        def _():
            pl.semaphore_signal(sem, inc=1, device_id=self.down, device_id_type=MESH)

        @pl.when(self.z < self.depth - 1)
        def _():
            pl.semaphore_signal(sem, inc=1, device_id=self.up, device_id_type=MESH)

        inner = (self.z > 0).astype(jnp.int32) + (self.z < self.depth - 1).astype(jnp.int32)
        pl.semaphore_wait(sem, 3 + inner)


def remote(src, dst, send, recv, who):
    return pltpu.make_async_remote_copy(
        src_ref=src, dst_ref=dst, send_sem=send, recv_sem=recv, device_id=who, device_id_type=MESH
    )


def gather_sems(groups, depth):
    return [
        pltpu.SemaphoreType.DMA((groups, 2, depth - 1)),
        pltpu.SemaphoreType.DMA((groups, depth)),
        pltpu.SemaphoreType.DMA((groups, depth)),
        pltpu.SemaphoreType.DMA((groups, 3, depth)),
    ] * 2 + [pltpu.SemaphoreType.DMA((groups,))]


class Gather:
    def __init__(self, place, g, shard, whole, sems):
        self.p, self.g, self.shard, self.whole = place, g, shard, whole
        self.sz, self.sx, self.sy, self.sc, self.rz, self.rx, self.ry, self.rc, self.own = sems
        self.rows, self.cols = shard.shape
        self.done = False

    def piece(self, z, x, half=None):
        return self.piece_of(z, x, self.p.c, half)

    def piece_of(self, z, x, c, half=None):
        if half is None:
            return self.whole.at[z, x, c]
        return self.whole.at[z, x, c, :, ds(half * (self.cols // 2), self.cols // 2)]

    def copy_z(self, direction, distance, z, src=None):
        dst = self.piece(z, self.p.x)
        return remote(
            dst if src is None else src,
            dst,
            self.sz.at[self.g, direction, distance],
            self.rz.at[self.g, direction, distance],
            self.p.up if direction == 0 else self.p.down,
        )

    def copy_x(self, z, src=None):
        dst = self.piece(z, self.p.x, self.p.y)
        return remote(dst if src is None else src, dst, self.sx.at[self.g, z], self.rx.at[self.g, z], self.p.xn)

    def copy_y(self, z):
        at = self.piece(z, 1 - self.p.x, self.p.y)
        return remote(at, at, self.sy.at[self.g, z], self.ry.at[self.g, z], self.p.yn)

    def copy_c(self, kind, z, src=None):
        if kind == 0:
            dst = self.piece(z, self.p.x)
        else:
            half = self.p.y if kind == 1 else 1 - self.p.y
            dst = self.piece(z, 1 - self.p.x, half)
        return remote(
            dst if src is None else src,
            dst,
            self.sc.at[self.g, kind, z],
            self.rc.at[self.g, kind, z],
            self.p.sib,
        )

    def local(self):
        return pltpu.make_async_copy(self.shard, self.piece(self.p.z, self.p.x), self.own.at[self.g])

    def z_step(self, k):
        p = self.p
        if k == 0:
            self.local().start()

            @pl.when(p.z < p.depth - 1)
            def _():
                self.copy_z(0, 0, p.z, self.shard).start()

            @pl.when(p.z > 0)
            def _():
                self.copy_z(1, 0, p.z, self.shard).start()

            half = self.shard.at[:, ds(p.y * (self.cols // 2), self.cols // 2)]
            self.copy_x(p.z, half).start()
            self.copy_c(0, p.z, self.shard).start()
            return

        for direction in (0, 1):
            z = p.z - k if direction == 0 else p.z + k

            @pl.when(z >= 0 if direction == 0 else z < p.depth)
            def _(direction=direction, z=z):
                self.copy_z(direction, k - 1, z).wait_recv()
                if k < p.depth - 1:

                    @pl.when(p.z < p.depth - 1 if direction == 0 else p.z > 0)
                    def _():
                        self.copy_z(direction, k, z).start()

                self.copy_x(z).start()
                self.copy_c(0, z).start()

    def at_distance(self, k, act):
        p = self.p
        if k == 0:
            act(p.z)
            return

        @pl.when(p.z - k >= 0)
        def _():
            act(p.z - k)

        @pl.when(p.z + k < p.depth)
        def _():
            act(p.z + k)

    def x_step(self, k):
        def act(z):
            self.copy_x_in(z).wait_recv()
            self.copy_y_out(z).start()
            self.copy_c(1, z).start()

        self.at_distance(k, act)

    def copy_x_in(self, z):
        at = self.piece(z, 1 - self.p.x, self.p.y)
        return remote(at, at, self.sx.at[self.g, z], self.rx.at[self.g, z], self.p.xn)

    def copy_y_out(self, z):
        return self.copy_y(z)

    def copy_y_in(self, z):
        at = self.piece(z, 1 - self.p.x, 1 - self.p.y)
        return remote(at, at, self.sy.at[self.g, z], self.ry.at[self.g, z], self.p.yn)

    def y_step(self, k):
        def act(z):
            self.copy_y_in(z).wait_recv()
            self.copy_c(2, z).start()

        self.at_distance(k, act)

    def core_in(self, kind, z):
        p = self.p
        if kind == 0:
            at = self.piece_of(z, p.x, 1 - p.c)
        else:
            at = self.piece_of(z, 1 - p.x, 1 - p.c, p.y if kind == 1 else 1 - p.y)
        return remote(at, at, self.sc.at[self.g, kind, z], self.rc.at[self.g, kind, z], p.sib)

    def c_step(self):
        self.done = True
        self.local().wait()
        for kind in range(3):
            for z in range(self.p.depth):
                self.core_in(kind, z).wait_recv()

    def end(self):
        p = self.p
        for k in range(p.depth - 1):
            @pl.when((p.z < p.depth - 1) & (p.z - k >= 0))
            def _():
                self.copy_z(0, k, p.z - k).wait_send()

            @pl.when((p.z > 0) & (p.z + k < p.depth))
            def _():
                self.copy_z(1, k, p.z + k).wait_send()

        for z in range(p.depth):
            self.copy_x(z).wait_send()
            self.copy_y(z).wait_send()
            for kind in range(3):
                self.copy_c(kind, z).wait_send()

    def steps(self):
        d = self.p.depth
        out = []
        for n in range(d + 2):
            def step(n=n):
                if n < d:
                    self.z_step(n)
                if 0 <= n - 1 < d:
                    self.x_step(n - 1)
                if 0 <= n - 2 < d:
                    self.y_step(n - 2)
            out.append(step)
        out.append(self.c_step)
        return out


def scatter_sems(groups, depth):
    kinds = [(groups, 2), (groups,), (groups,), (groups, 2, depth - 1), (groups,)]
    return [pltpu.SemaphoreType.DMA(k) for k in kinds] * 2 + [pltpu.SemaphoreType.DMA((groups, 2))]


def scatter_buffers(rows, cols, depth):
    return [
        pltpu.VMEM((2, depth, rows, cols), BF),
        pltpu.VMEM((depth, rows, cols // 2), BF),
        pltpu.VMEM((depth, rows, cols // 2), BF),
        pltpu.VMEM((2, depth - 1, rows, cols), BF),
        pltpu.VMEM((rows, cols), BF),
    ]


def add_into(depth, rows, target, other):
    piece = min(rows, 48)
    parts = rows // piece

    def step(i):
        z, at = i // parts, ds(i % parts * piece, piece, 16)
        t = target(z, at)
        t[...] = t[...] + other(z, at)[...]

    loop(depth * parts, step)


class Scatter:
    def __init__(self, place, g, grad, landing, buffers, sems):
        self.p, self.g, self.grad, self.landing = place, g, grad, landing
        self.in_c, self.in_y, self.in_x, self.in_z, self.in_f = buffers
        (self.sc, self.sy, self.sx, self.sz, self.sf, self.rc, self.ry, self.rx, self.rz, self.rf, self.out) = sems
        _, self.depth, self.rows, self.cols = self.in_c.shape

    def half(self, h):
        return ds(h * (self.cols // 2), self.cols // 2)

    def copy_c(self, x):
        p = self.p
        return remote(self.grad.at[:, x, 1 - p.c], self.in_c.at[x], self.sc.at[self.g, x], self.rc.at[self.g, x], p.sib)

    def copy_y(self):
        p = self.p
        return remote(
            self.grad.at[:, 1 - p.x, p.c, :, self.half(1 - p.y)], self.in_y, self.sy.at[self.g], self.ry.at[self.g], p.yn
        )

    def copy_x(self):
        p = self.p
        return remote(
            self.grad.at[:, 1 - p.x, p.c, :, self.half(p.y)], self.in_x, self.sx.at[self.g], self.rx.at[self.g], p.xn
        )

    def copy_z(self, direction, z, slot):
        p = self.p
        return remote(
            self.grad.at[z, p.x, p.c],
            self.in_z.at[direction, slot],
            self.sz.at[self.g, direction, slot],
            self.rz.at[self.g, direction, slot],
            p.up if direction == 0 else p.down,
        )

    def copy_f(self):
        p = self.p
        return remote(self.grad.at[p.z, p.x, p.c], self.in_f, self.sf.at[self.g], self.rf.at[self.g], p.yn)

    def begin(self):
        self.copy_c(1 - self.p.x).start()
        self.copy_c(self.p.x).start()

    def cores(self, turn):
        p = self.p
        x = 1 - p.x if turn == 0 else p.x
        self.copy_c(x).wait_recv()
        add_into(
            self.depth,
            self.rows,
            lambda z, at: self.grad.at[z, x, p.c, at],
            lambda z, at: self.in_c.at[x, z, at],
        )
        if turn == 0:
            self.copy_y().start()

    def over_y(self):
        p = self.p
        self.copy_y().wait_recv()
        add_into(
            self.depth,
            self.rows,
            lambda z, at: self.grad.at[z, 1 - p.x, p.c, at, self.half(p.y)],
            lambda z, at: self.in_y.at[z, at],
        )
        self.copy_x().start()

    def over_x(self):
        p = self.p
        self.copy_x().wait_recv()
        add_into(
            self.depth,
            self.rows,
            lambda z, at: self.grad.at[z, p.x, p.c, at, self.half(p.y)],
            lambda z, at: self.in_x.at[z, at],
        )

    def line(self, wave):
        p, top = self.p, self.depth - 1
        for direction in (0, 1):
            place = p.z if direction == 0 else top - p.z
            if wave == 0:

                @pl.when(place == 0)
                def _(direction=direction):
                    for far in range(top, 0, -1):
                        self.copy_z(direction, far if direction == 0 else top - far, far - 1).start()

                continue

            @pl.when((place >= 1) & (place <= wave))
            def _(direction=direction, place=place):
                far = top - wave + place
                z = far if direction == 0 else top - far
                slot = top - wave
                self.copy_z(direction, z, slot).wait_recv()
                add_into(
                    1,
                    self.rows,
                    lambda _, at: self.grad.at[z, p.x, p.c, at],
                    lambda _, at: self.in_z.at[direction, slot, at],
                )
                if slot > 0:
                    self.copy_z(direction, z, slot - 1).start()

    def share(self):
        self.copy_f().start()

    def copy_out(self, n):
        view, result = self.landing[n]
        return pltpu.make_async_copy(view, result, self.out.at[self.g, n])

    def finish(self):
        p = self.p
        self.copy_f().wait_recv()
        piece = min(self.rows, 48)
        c0 = 0
        for n, (view, result) in enumerate(self.landing):
            cols = view.shape[1]

            def step(i, view=view, c0=c0, cols=cols):
                at = ds(i * piece, piece, 16)
                cs = pl.ds(c0, cols)
                view[at, :] = self.grad[p.z, p.x, p.c, at, cs].astype(F32) + self.in_f[at, cs].astype(F32)

            loop(self.rows // piece, step)
            if result is not None:
                self.copy_out(n).start()
            c0 += cols

    def end(self):
        p, top = self.p, self.depth - 1
        for x in (0, 1):
            self.copy_c(x).wait_send()
        self.copy_y().wait_send()
        self.copy_x().wait_send()
        for direction in (0, 1):
            place = p.z if direction == 0 else top - p.z
            for slot in range(top):

                @pl.when(place + slot < top)
                def _(direction=direction, slot=slot):
                    self.copy_z(direction, 0, slot).wait_send()

        self.copy_f().wait_send()
        for n, (_, result) in enumerate(self.landing):
            if result is not None:
                self.copy_out(n).wait()

    def steps(self):
        def over_x_and_line():
            self.over_x()
            self.line(0)

        out = [lambda: self.cores(0), lambda: self.cores(1), self.over_y, over_x_and_line]
        for wave in range(1, self.depth):
            out.append(functools.partial(self.line, wave))
        return out + [self.share, self.finish]


def spread(width, owners_rows, parts):
    row = lax.broadcasted_iota(jnp.int32, (width, 1), 0)
    target = row
    for owner in range(1, width // owners_rows):
        target = target + jnp.where(row >= owner * owners_rows, (parts - 1) * owners_rows, 0)
    lane = lax.broadcasted_iota(jnp.int32, (width, width * parts), 1)
    return (lane == target).astype(BF)


def unpack_small(columns, shard, parts, vec, bup):
    rows = columns.astype(F32).T
    vec[...] = rows[:8, :]
    low = rows[8:16, :].astype(BF)
    width = 8 * shard
    place = spread(width, shard, parts)
    for t in range(columns.shape[0] // width):
        wide = nn(low[:, t * width : (t + 1) * width], place)
        total = wide[0:1]
        for i in range(1, parts):
            total = total + pltpu.roll(wide, i * shard, 1)[i : i + 1]
        bup[:, t * width * parts : (t + 1) * width * parts] = total


def pack_small(gv, gbu, shard, parts):
    width = 8 * shard
    model = gv.shape[1]
    place = spread(width, shard, parts)
    rows = []
    for i in range(parts):
        pieces = []
        for t in range(model // width):
            wide = jnp.broadcast_to(gbu[:, t * width * parts : (t + 1) * width * parts], (8, width * parts))
            if i:
                wide = pltpu.roll(wide, width * parts - i * shard, 1)
            pieces.append(nt(wide.astype(BF), place)[0:1])
        rows.append(jnp.concatenate(pieces, axis=1))
    blank = jnp.zeros((BLOCK - 8 - parts, model), F32)
    return jnp.concatenate([gv] + rows + [blank], axis=0).T.astype(BF)


ROWS = 256
CHUNK = 512


def phi_parts(u):
    cdf = 0.5 * (1.0 + lax.erf(u * math.sqrt(0.5)))
    pdf = jnp.exp(-0.5 * u * u) * (1.0 / math.sqrt(2.0 * math.pi))
    return cdf, pdf


V = pl.BlockSpec(memory_space=pltpu.VMEM)
ANY = pl.BlockSpec(memory_space=pl.ANY)
sds = jax.ShapeDtypeStruct


def params(collective_id=None):
    if collective_id is None:
        return pltpu.CompilerParams(vmem_limit_bytes=VMEM_LIMIT)
    return pltpu.CompilerParams(
        vmem_limit_bytes=VMEM_LIMIT, collective_id=collective_id, has_side_effects=True
    )


class Links:
    rate = {"c": 350.0, "x": 45.0, "y": 45.0, "z": 45.0}
    lag = 1.5

    def __init__(self):
        self.free = dict.fromkeys(self.rate, 0.0)
        self.heap = []
        self.count = 0

    def send(self, link, at, size):
        self.free[link] = max(at, self.free[link]) + size / self.rate[link] * 1e-3
        return self.free[link] + self.lag

    def push(self, at, task, then=None):
        self.count += 1
        heapq.heappush(self.heap, (at, self.count, task, then))

    def gather(self, gather, at):
        size = gather.rows * gather.cols * 2
        depth = gather.p.depth

        def zed(k):
            def then(now):
                if k < depth - 1:
                    self.push(self.send("z", now, size), lambda: gather.z_step(k + 1), zed(k + 1))
                self.push(self.send("x", now, size / 2), lambda: gather.x_step(k), ex(k))

            return then

        def ex(k):
            return lambda now: self.push(
                self.send("y", now, size / 2), lambda: gather.y_step(k), lambda now: None if k < depth - 1
                else self.push(now + 2.0, gather.c_step)
            )

        self.push(at, lambda: gather.z_step(0), zed(0))

    def scatter(self, scatter, at):
        size = scatter.rows * scatter.cols * 2
        steps = scatter.steps()
        last = len(steps) - 1

        def after(n):
            def then(now):
                now = now + 0.3
                if n == 0:
                    self.push(self.send("y", now, 2 * size), steps[2], after(2))
                elif n == 2:
                    self.push(self.send("x", now, 2 * size), steps[3], after(3))
                elif 3 <= n < last - 2:
                    self.push(self.send("z", now, size), steps[n + 1], after(n + 1))
                elif n == last - 2:
                    self.push(now, steps[last - 1], after(last - 1))
                elif n == last - 1:
                    self.push(self.send("y", now, size), steps[last])

            return then

        self.push(self.send("c", at, 4 * size), steps[0], after(0))
        self.push(self.send("c", at, 4 * size), steps[1])

    def due(self, now):
        found = []
        while self.heap and self.heap[0][0] <= now:
            at, _, task, then = heapq.heappop(self.heap)
            found.append(task)
            if then:
                then(at)
        return found

    def all(self):
        return self.due(float("inf"))

    def next(self):
        return self.heap[0][0]


class Clock:
    def __init__(self, links):
        self.links, self.now = links, 0.0

    def run(self, tasks):
        for task in tasks:
            task()

    def spend(self, time):
        self.now += time
        self.run(self.links.due(self.now))

    def until(self, gather):
        while not gather.done:
            self.now = max(self.now, self.links.next())
            self.run(self.links.due(self.now))

    def loop(self, count, step, time):
        ticks = []
        for _ in range(count):
            self.now += time
            ticks.append(self.links.due(self.now))

        def body(i):
            step(i)
            for n, tasks in enumerate(ticks):
                if tasks:

                    @pl.when(i == n)
                    def _(tasks=tasks):
                        self.run(tasks)

        loop(count, body)


def layer_kernel(depth, parts, cuts, *refs):
    it = iter(refs)

    def take(n):
        return [next(it) for _ in range(n)]

    x_in, seg, sa, so, su, sd, og_in = take(7)
    out, pooled, gtok, gq, gk, gv_w, go_w, gu_w, gd_w, small, p_main, p_last = take(12)
    x, q, k, v, o, z_low, df, n1s, dh, r1s, g, sl, stage = take(13)
    wa, wo, wu, wd, gv, gbu, vec, bup, dk_sum, dv_sum = take(10)
    sets = [take(5) for _ in cuts]
    gsems, ssems, msem, osem, psem = take(9), take(11), *take(3)

    seqs, length = seg.shape
    tokens, model = x.shape
    hidden = g.shape[1]
    shard = so.shape[0]
    pairs = model // BLOCK
    spans, offsets, _ = key_windows(length)
    final = len(spans) - 1
    tiles = tokens // ROWS

    def span_rows(qb):
        return (spans[qb][1] - spans[qb][0]) * BLOCK

    def bias_at(row, qb):
        at = 0 if qb == final else offsets[qb]
        lane = (row * 2 + (1 if qb == final else 0)) * BLOCK
        return dh.at[at : at + span_rows(qb), ds(lane, BLOCK)]

    def probs_at(i, qb):
        held, at = (sl, 0) if qb == final else (g, offsets[qb])
        return held.at[at : at + span_rows(qb), ds(i * 2 * BLOCK, 2 * BLOCK)]

    place = Place(depth)
    links = Links()
    clock = Clock(links)
    loads = [pltpu.make_async_copy(x_in, x, msem.at[0]), pltpu.make_async_copy(og_in, df, msem.at[1])]
    for load in loads:
        load.start()
    gathers = [
        Gather(place, n, s, w, gsems) for n, (s, w) in enumerate(((sa, wa), (so, wo), (su, wu), (sd, wd)))
    ]
    for gather, at in zip(gathers, BEGINS):
        links.gather(gather, at)
    place.barrier()
    clock.spend(1.0)
    make_bias(seg, bias_at)
    loads[0].wait()
    clock.until(gathers[0])
    unpack_small(wa[:, :, :, :, 3 * model : 3 * model + BLOCK].reshape(model, BLOCK), shard, parts, vec, bup)

    def vrow(i):
        return vec[i : i + 1, :]

    def project(rt):
        rows = ds(rt * ROWS, ROWS)
        for n, (to, bias) in enumerate(((q, 0), (k, None), (v, 1))):
            weight = wa[:, :, :, :, n * model : (n + 1) * model].reshape(model, model)
            value = nn(x[rows, :], weight)
            to[rows, :] = (value if bias is None else value + vrow(bias)).astype(BF)

    clock.loop(tiles, project, 1.5)

    def copy_probs(i, which, back=False):
        lanes = ds(i * 2 * BLOCK, 2 * BLOCK)
        here = g.at[:, lanes] if which == 0 else sl.at[: span_rows(final), lanes]
        there = (p_main if which == 0 else p_last).at[:, lanes]
        return pltpu.make_async_copy(here, there, psem.at[which, i])

    def attend(i):
        attend_pair(i, length, pairs, q, k, v, o, probs_at, bias_at)
        copy_probs(i, 0).start()
        copy_probs(i, 1).start()

    clock.loop(seqs * pairs, attend, 2.1)
    for i in range(seqs * pairs):
        copy_probs(i, 0).wait()
        copy_probs(i, 1).wait()

    def up(rt):
        rows = ds(rt * ROWS, ROWS)
        h = x[rows, :].astype(F32) + (nn(o[rows, :], wo[...].reshape(model, model)) + vrow(2))
        c = h - rmean(h)
        r = lax.rsqrt(rmean(c * c) + EPS)
        n = c * r
        n1s[rows, :] = n
        r1s[rows, :] = jnp.broadcast_to(r, (ROWS, BLOCK))
        z_low[rows, :] = (n * vrow(3) + vrow(4)).astype(BF)
        for cc in range(hidden // CHUNK):
            cs = slice(cc * CHUNK, (cc + 1) * CHUNK)
            u = nn(z_low[rows, :], wu[:, :, :, :, cs].reshape(model, CHUNK)) + bup[:, cs]
            cdf, pdf = phi_parts(u)
            g[rows, cs] = (u * cdf).astype(BF)
            sl[rows, cs] = (cdf + u * pdf).astype(BF)

    clock.until(gathers[1])
    clock.until(gathers[2])
    clock.loop(tiles, up, 5.0)
    clock.until(gathers[3])
    for gather in gathers:
        gather.end()
    loads[1].wait()
    gv[...] = jnp.zeros_like(gv)
    pooled[...] = jnp.zeros_like(pooled)

    def copy_tile(rt):
        return pltpu.make_async_copy(stage.at[rt % 2], out.at[ds(rt * ROWS, ROWS)], osem.at[rt % 2])

    def down(rt):
        rows = ds(rt * ROWS, ROWS)
        h = (n1s[rows, :] * vrow(3) + vrow(4)) + (nn(g[rows, :], wd[...].reshape(hidden, model)) + vrow(5))
        c = h - rmean(h)
        r = lax.rsqrt(rmean(c * c) + EPS)
        n2 = c * r
        y = n2 * vrow(6) + vrow(7)
        y_low = y.astype(BF)

        @pl.when(rt >= 2)
        def _():
            copy_tile(rt - 2).wait()

        stage[rt % 2] = y_low
        copy_tile(rt).start()
        row = rt * ROWS // length
        ids = seg[pl.ds(row, 1), ds(rt * ROWS % length, ROWS)]
        onehot = (ids == lax.broadcasted_iota(jnp.int32, (SEGS, ROWS), 0)).astype(BF)
        pooled[row] = pooled[row] + (nn(onehot, y_low) + nn(onehot, (y - y_low.astype(F32)).astype(BF)))
        dy = df[rows, :].astype(F32)
        gv[6:7, :] += csum(dy * n2)
        gv[7:8, :] += csum(dy)
        e = dy * vrow(6)
        d = r * (e - rmean(e) - n2 * rmean(e * n2))
        dh[rows, :] = d
        low = d.astype(BF)
        df[rows, :] = low
        gv[5:6, :] += csum(low.astype(F32))

    clock.loop(tiles, down, 3.0)
    for rt in (tiles - 2, tiles - 1):
        copy_tile(rt).wait()
    for row in range(seqs):
        onehot = (seg[row : row + 1, :] == lax.broadcasted_iota(jnp.int32, (SEGS, length), 0)).astype(F32)
        pooled[row] = pooled[row] / jnp.sum(onehot, axis=1, keepdims=True)

    pair_rows = 2 * sd.shape[0]

    def up_back(cc):
        cs = ds(cc * pair_rows, pair_rows, BLOCK)
        zz, xx = cc // 2, cc % 2
        weight = wd[zz, xx].reshape(pair_rows, model)
        total = jnp.zeros((1, pair_rows), F32)
        for rt in range(tiles):
            rows = slice(rt * ROWS, (rt + 1) * ROWS)
            du = (nt(df[rows, :], weight) * sl[rows, cs].astype(F32)).astype(BF)
            sl[rows, cs] = du
            total += csum(du.astype(F32))
        gbu[:, cs] = total
        wd[zz, xx] = tn(g[:, cs], df[...]).astype(BF).reshape(2, sd.shape[0], model)

    clock.loop(hidden // pair_rows, up_back, 1.8)

    at = 0
    blocks = {}
    for name, rows, cols in (("d", sd.shape[0], model), ("o", shard, model), ("u", shard, hidden),
                             ("q", shard, model), ("k", shard, model), ("v", shard, model)):
        blocks[name] = [at + n * rows for n in range(cols // model)]
        at += rows * (cols // model)
    blocks["small"] = [at]
    results = {"d": gd_w, "o": go_w, "u": gu_w, "q": gq, "k": gk, "v": gv_w}
    weights = {"d": wd, "o": wo, "u": wu, "q": wa, "k": wa, "v": wa}
    first = {"q": 0, "k": model, "v": 2 * model}
    scatters = {}
    for n, (name, r0, rows, c0, cols) in enumerate(cuts):
        landing = []
        for c in range(c0, c0 + cols, model):
            width = min(model, c0 + cols - c)
            base = blocks["small" if width < model else name][0 if width < model else c // model] + r0
            view = n1s.at[base : base + rows, 0:width]
            result = None if width < model else results[name].at[r0 : r0 + rows, c : c + width]
            landing.append((view, result))
        c1 = c0 + first.get(name, 0)
        scatters.setdefault(name, []).append(
            Scatter(place, n, weights[name].at[:, :, :, r0 : r0 + rows, c1 : c1 + cols], landing, sets[n], ssems)
        )

    def send_home(name):
        for s in scatters[name]:
            s.begin()
            links.scatter(s, clock.now)

    send_home("d")
    bring = [
        pltpu.make_async_copy(p_main, g, msem.at[2]),
        pltpu.make_async_copy(p_last, sl.at[: span_rows(final)], msem.at[3]),
    ]
    bring[0].start()

    def first_back(rt):
        rows = ds(rt * ROWS, ROWS)
        dz = dh[rows, :] + nt(sl[rows, :], wu[...].reshape(model, hidden))
        n1 = n1s[rows, :]
        gv[3:4, :] += csum(dz * n1)
        gv[4:5, :] += csum(dz)
        e = dz * vrow(3)
        d = r1s[rows, 0:1] * (e - rmean(e) - n1 * rmean(e * n1))
        dh[rows, :] = d
        da = d.astype(BF)
        df[rows, :] = da
        gv[2:3, :] += csum(da.astype(F32))

    clock.loop(tiles, first_back, 2.0)

    def up_grad(cc):
        cs = ds(cc * CHUNK, CHUNK)
        wu[:, :, :, :, cs] = tn(z_low[...], sl[:, cs]).astype(BF).reshape(depth, 2, 2, shard, CHUNK)

    clock.loop(hidden // CHUNK, up_grad, 1.0)
    send_home("u")
    bring[1].start()
    do = z_low

    def out_back(rt):
        rows = ds(rt * ROWS, ROWS)
        do[rows, :] = nt(df[rows, :], wo[...].reshape(model, model)).astype(BF)

    clock.loop(tiles, out_back, 0.4)
    half = model // 2

    def halves(n, to, left, right):
        def step(t):
            value = tn(left[:, ds(t * half, half, BLOCK)], right[...]).astype(BF)
            to[pl.ds(t * (depth // 2), depth // 2), :, :, :, n * model : (n + 1) * model] = value.reshape(
                depth // 2, 2, 2, shard, model
            )

        clock.loop(2, step, 0.8)

    halves(0, wo, o, df)
    send_home("o")
    bring[0].wait()
    bring[1].wait()
    clock.loop(
        seqs * pairs,
        lambda i: attend_back_pair(i, length, pairs, q, k, v, do, probs_at, q, k, v, dk_sum, dv_sum),
        2.2,
    )

    def copy_tokens(rt):
        rows = ds(rt * ROWS, ROWS)
        return pltpu.make_async_copy(o.at[rows], gtok.at[rows], psem.at[0, rt])

    for n, (name, d) in enumerate((("q", q), ("k", k), ("v", v))):

        def token_step(rt, n=n, d=d):
            rows = ds(rt * ROWS, ROWS)
            weight = wa[:, :, :, :, n * model : (n + 1) * model].reshape(model, model)
            total = dh[rows, :] + nt(d[rows, :], weight)
            if n < 2:
                dh[rows, :] = total
            else:
                o[rows, :] = total.astype(BF)
                copy_tokens(rt).start()

        clock.loop(tiles, token_step, 0.4)
        halves(n, wa, x, d)
        if name == "v":
            bq, bv = csum(q[...].astype(F32)), csum(v[...].astype(F32))
            vectors = jnp.concatenate([bq, bv, gv[2:8, :]], axis=0)
            columns = pack_small(vectors, gbu[...], shard, parts).reshape(depth, 2, 2, shard, BLOCK)
            wa[:, :, :, :, 3 * model : 3 * model + BLOCK] = columns
        send_home(name)
    clock.run(links.all())
    for group in scatters.values():
        for s in group:
            s.end()
    for rt in range(tiles):
        copy_tokens(rt).wait()
    base = blocks["small"][0]
    last = n1s[base : base + shard, :BLOCK]
    square = jnp.concatenate([last, jnp.zeros((BLOCK - shard, BLOCK), F32)], axis=0).T
    small[...] = square[:16, :]


BEGINS = (0.0, 6.0, 9.0, 14.0)


def run_layer(depth, x, seg, sa, so, su, sd, og):
    tokens, model = x.shape
    hidden = su.shape[1]
    parts = hidden // model
    seqs, length = seg.shape
    spans, offsets, band = key_windows(length)
    final_rows = band - offsets[-1]
    shard = so.shape[0]
    cuts = []
    for part in range(2):
        cuts.append(("d", part * (sd.shape[0] // 2), sd.shape[0] // 2, 0, model))
    for part in range(2):
        cuts.append(("u", 0, shard, part * (hidden // 2), hidden // 2))
    cuts.append(("o", 0, shard, 0, model))
    cuts += [("q", 0, shard, 0, model), ("k", 0, shard, 0, model), ("v", 0, shard, 0, model + 2 * BLOCK)]
    buffers = []
    for _, _, rows, _, cols in cuts:
        buffers += scatter_buffers(rows, cols, depth)

    def own(s):
        return pltpu.VMEM((depth, 2, 2, *s.shape), BF)

    act, wide = pltpu.VMEM((tokens, model), BF), pltpu.VMEM((tokens, hidden), BF)
    full = pltpu.VMEM((tokens, model), F32)
    part = pltpu.VMEM((length, BLOCK), F32)
    weight = sds((shard, model), F32)
    iterations = seqs * model // BLOCK
    return pl.pallas_call(
        functools.partial(layer_kernel, depth, parts, tuple(cuts)),
        out_shape=(sds((tokens, model), BF), sds((seqs, SEGS, model), F32), sds((tokens, model), BF),
                   weight, weight, weight, weight, sds(su.shape, F32), sds(sd.shape, F32), sds((16, BLOCK), F32),
                   sds((tokens, hidden), BF), sds((final_rows, hidden), BF)),
        in_specs=[ANY, V, ANY, ANY, ANY, ANY, ANY],
        out_specs=(ANY, V, ANY) + (ANY,) * 6 + (V, ANY, ANY),
        scratch_shapes=[act] * 7 + [full, full, pltpu.VMEM((tokens, BLOCK), F32), wide, wide,
                        pltpu.VMEM((2, ROWS, model), BF), own(sa), own(so), own(su), own(sd),
                        pltpu.VMEM((8, model), F32), pltpu.VMEM((1, hidden), F32), pltpu.VMEM((8, model), F32),
                        pltpu.VMEM((1, hidden), F32), part, part, *buffers, *gather_sems(4, depth),
                        *scatter_sems(len(cuts), depth), pltpu.SemaphoreType.DMA((4,)), pltpu.SemaphoreType.DMA((2,)),
                        pltpu.SemaphoreType.DMA((2, iterations))],
        compiler_params=params(0),
        name="layer",
    )(x, seg, sa, so, su, sd, og)


def local_ring(depth, *args):
    (tokens, segments, w_query, b_query, w_key, w_value, b_value, w_out, b_out, gain1, shift1, w_up, b_up, w_down,
     b_down, gain2, shift2, out_grad) = args
    seqs, length, model = tokens.shape
    shard = w_query.shape[0]
    parts = w_up.shape[1] // model
    x = tokens.reshape(seqs * length, model)
    og = out_grad.reshape(seqs * length, model)
    small = jnp.stack([b_query, b_value, b_out, gain1, shift1, b_down, gain2, shift2] + [
        b_up[i * shard : (i + 1) * shard] for i in range(parts)
    ], axis=1)
    small = jnp.pad(small, ((0, 0), (0, 2 * BLOCK - 8 - parts)))
    sa = jnp.concatenate([w_query, w_key, w_value, small], axis=1)
    out, pooled, gtok, gq, gk, gv, go, gu, gd, gs, _, _ = run_layer(depth, x, segments, sa, w_out, w_up, w_down, og)
    gbq, gbv, gbo, gg1, gs1, gbd, gg2, gs2 = [gs[i, :shard] for i in range(8)]
    gb_up = gs[8 : 8 + parts, :shard].reshape(parts * shard)
    return (
        out.reshape(tokens.shape), pooled, gtok.reshape(tokens.shape),
        gq, gbq, gk, gv, gbv, go, gbo, gg1, gs1, gu, gb_up, gd, gbd, gg2, gs2,
    )


def project(x, wa, vec, q, k, v):
    model = x.shape[1]

    def step(rt):
        rows = ds(rt * ROWS, ROWS)
        q[rows, :] = (nn(x[rows, :], wa[:, :model]) + vec[0:1, :]).astype(BF)
        k[rows, :] = nn(x[rows, :], wa[:, model : 2 * model]).astype(BF)
        v[rows, :] = (nn(x[rows, :], wa[:, 2 * model : 3 * model]) + vec[1:2, :]).astype(BF)

    loop(x.shape[0] // ROWS, step)


def mid_kernel(*refs):
    (x, o, og, seg, wo, wu, wd, vec, bup, out, pooled, g_down, g_up, g_out, do, dh1, gv, gbu,
     n1s, r1s, z_low, g, sl, df, dh2) = refs
    tokens, model = x.shape
    hidden = wu.shape[1]
    seqs, length = seg.shape
    gv[...] = jnp.zeros_like(gv)
    pooled[...] = jnp.zeros_like(pooled)

    def vrow(i):
        return vec[i : i + 1, :]

    def up(rt):
        rows = ds(rt * ROWS, ROWS)
        h = x[rows, :].astype(F32) + (nn(o[rows, :], wo[...]) + vrow(2))
        c = h - rmean(h)
        r = lax.rsqrt(rmean(c * c) + EPS)
        n = c * r
        n1s[rows, :] = n
        r1s[rows, :] = jnp.broadcast_to(r, (ROWS, BLOCK))
        z_low[rows, :] = (n * vrow(3) + vrow(4)).astype(BF)
        for cc in range(hidden // CHUNK):
            cs = slice(cc * CHUNK, (cc + 1) * CHUNK)
            u = nn(z_low[rows, :], wu[:, cs]) + bup[:, cs]
            cdf, pdf = phi_parts(u)
            g[rows, cs] = (u * cdf).astype(BF)
            sl[rows, cs] = (cdf + u * pdf).astype(BF)

    loop(tokens // ROWS, up)

    def down(rt):
        rows = ds(rt * ROWS, ROWS)
        h = (n1s[rows, :] * vrow(3) + vrow(4)) + (nn(g[rows, :], wd[...]) + vrow(5))
        c = h - rmean(h)
        r = lax.rsqrt(rmean(c * c) + EPS)
        n2 = c * r
        y = n2 * vrow(6) + vrow(7)
        y_low = y.astype(BF)
        out[rows, :] = y_low
        row = rt * ROWS // length
        ids = seg[pl.ds(row, 1), ds(rt * ROWS % length, ROWS)]
        onehot = (ids == lax.broadcasted_iota(jnp.int32, (SEGS, ROWS), 0)).astype(BF)
        pooled[row] = pooled[row] + (nn(onehot, y_low) + nn(onehot, (y - y_low.astype(F32)).astype(BF)))
        dy = og[rows, :].astype(F32)
        gv[6:7, :] += csum(dy * n2)
        gv[7:8, :] += csum(dy)
        e = dy * vrow(6)
        d = r * (e - rmean(e) - n2 * rmean(e * n2))
        dh2[rows, :] = d
        low = d.astype(BF)
        df[rows, :] = low
        gv[5:6, :] += csum(low.astype(F32))

    loop(tokens // ROWS, down)
    for row in range(seqs):
        onehot = (seg[row : row + 1, :] == lax.broadcasted_iota(jnp.int32, (SEGS, length), 0)).astype(F32)
        pooled[row] = pooled[row] / jnp.sum(onehot, axis=1, keepdims=True)

    def down_grad(cc):
        cs = ds(cc * CHUNK, CHUNK)
        g_down[cs, :] = tn(g[:, cs], df[...]).astype(BF)

    loop(hidden // CHUNK, down_grad)

    def up_back(cc):
        cs = ds(cc * CHUNK, CHUNK)
        total = jnp.zeros((1, CHUNK), F32)
        for rt in range(tokens // ROWS):
            rows = slice(rt * ROWS, (rt + 1) * ROWS)
            du = (nt(df[rows, :], wd[cs, :]) * sl[rows, cs].astype(F32)).astype(BF)
            sl[rows, cs] = du
            total += csum(du.astype(F32))
        gbu[:, cs] = total
        g_up[:, cs] = tn(z_low[...], sl[:, cs]).astype(BF)

    loop(hidden // CHUNK, up_back)

    def first_back(rt):
        rows = ds(rt * ROWS, ROWS)
        dz = dh2[rows, :] + nt(sl[rows, :], wu[...])
        n1 = n1s[rows, :]
        gv[3:4, :] += csum(dz * n1)
        gv[4:5, :] += csum(dz)
        e = dz * vrow(3)
        d = r1s[rows, 0:1] * (e - rmean(e) - n1 * rmean(e * n1))
        dh1[rows, :] = d
        da = d.astype(BF)
        df[rows, :] = da
        gv[2:3, :] += csum(da.astype(F32))
        do[rows, :] = nt(da, wo[...]).astype(BF)

    loop(tokens // ROWS, first_back)

    def out_grad_step(cc):
        cs = ds(cc * (model // 2), model // 2)
        g_out[cs, :] = tn(o[:, cs], df[...]).astype(BF)

    loop(2, out_grad_step)


def qkv_grads(x, dqkv, store):
    model = x.shape[1]
    part = model // 2
    for n, d in enumerate(dqkv):

        def step(t, n=n, d=d):
            store(n, t, tn(x[:, ds(t * part, part, BLOCK)], d[...]).astype(BF))

        loop(2, step)


def token_grads(dh1, dqkv, wa, out):
    model = dh1.shape[1]

    def step(rt):
        rows = ds(rt * ROWS, ROWS)
        total = dh1[rows, :]
        for n, d in enumerate(dqkv):
            total = total + nt(d[rows, :], wa[:, n * model : (n + 1) * model])
        out[rows, :] = total.astype(BF)

    loop(dh1.shape[0] // ROWS, step)


def run_mid(x, o, og, seg, wo, wu, wd, vec, bup):
    tokens, model = x.shape
    hidden = wu.shape[1]
    wide = pltpu.VMEM((tokens, hidden), BF)
    act = sds((tokens, model), BF)
    return pl.pallas_call(
        mid_kernel,
        out_shape=(act, sds((seg.shape[0], SEGS, model), F32), sds(wd.shape, BF), sds(wu.shape, BF), sds(wo.shape, BF),
                   act, sds((tokens, model), F32), sds((8, model), F32), sds((1, hidden), F32)),
        in_specs=[V] * 9,
        out_specs=(V,) * 9,
        scratch_shapes=[pltpu.VMEM((tokens, model), F32), pltpu.VMEM((tokens, BLOCK), F32), pltpu.VMEM((tokens, model), BF),
                        wide, wide, pltpu.VMEM((tokens, model), BF), pltpu.VMEM((tokens, model), F32)],
        compiler_params=params(),
        name="middle",
    )(x, o, og, seg, wo, wu, wd, vec, bup)


def plain_views(length, bias, probs):
    spans, offsets, _ = key_windows(length)

    def view(held):
        return lambda i, qb: held.at[i, pl.ds(offsets[qb], (spans[qb][1] - spans[qb][0]) * BLOCK)]

    return view(bias), view(probs)


def qkv_kernel(x, wa, vec, seg, q, k, v, o, probs, bias):
    length, pairs = seg.shape[1], x.shape[1] // BLOCK
    bias_at, probs_at = plain_views(length, bias, probs)
    make_bias(seg, bias_at)
    project(x, wa, vec, q, k, v)
    loop(seg.shape[0] * pairs, lambda i: attend_pair(i, length, pairs, q, k, v, o, probs_at, bias_at))


def back_kernel(length, q, k, v, do, probs, x, dh1, wa, gtok, g_qkv, gb, dq, dk, dv, dk_sum, dv_sum):
    pairs, model = x.shape[1] // BLOCK, x.shape[1]
    loop(
        x.shape[0] // length * pairs,
        lambda i: attend_back_pair(i, length, pairs, q, k, v, do, plain_views(length, None, probs)[1], dq, dk, dv, dk_sum, dv_sum),
    )

    def store(n, t, value):
        g_qkv[ds(t * (model // 2), model // 2), n * model : (n + 1) * model] = value

    qkv_grads(x, (dq, dk, dv), store)
    token_grads(dh1, (dq, dk, dv), wa, gtok)
    gb[...] = jnp.concatenate([csum(dq[...].astype(F32)), csum(dv[...].astype(F32)), jnp.zeros((6, model), F32)], axis=0)


def local_plain(*args):
    (tokens, segments, w_query, b_query, w_key, w_value, b_value, w_out, b_out, gain1, shift1, w_up, b_up, w_down,
     b_down, gain2, shift2, out_grad) = args
    seqs, length, model = tokens.shape
    count = seqs * length
    band = key_windows(length)[2]
    x = tokens.reshape(count, model)
    og = out_grad.reshape(count, model)

    def gathered(t):
        return lax.all_gather(t, "fsdp", axis=0, tiled=True)

    wa = gathered(jnp.concatenate([w_query, w_key, w_value], axis=1))
    small = gathered(jnp.stack([b_query, b_value, b_out, gain1, shift1, b_down, gain2, shift2], axis=1))
    vec = small.T.astype(F32)
    bup = gathered(b_up).astype(F32)[None]
    wo, wu, wd = gathered(w_out), gathered(w_up), gathered(w_down)
    act = sds((count, model), BF)
    q, k, v, o, probs = pl.pallas_call(
        qkv_kernel,
        out_shape=(act, act, act, act, sds((seqs * model // BLOCK, band, 2 * BLOCK), BF)),
        in_specs=[V] * 4,
        out_specs=(V,) * 5,
        scratch_shapes=[pltpu.VMEM((seqs, band, BLOCK), F32)],
        compiler_params=params(),
        name="attention",
    )(x, wa, vec, segments)
    out, pooled, g_down, g_up, g_out, do, dh1, gv, gbu = run_mid(x, o, og, segments, wo, wu, wd, vec, bup)
    kept = pltpu.VMEM((count, model), BF)
    part = pltpu.VMEM((length, BLOCK), F32)
    gtok, g_qkv, gb = pl.pallas_call(
        functools.partial(back_kernel, length),
        out_shape=(act, sds((model, 3 * model), BF), sds((8, model), F32)),
        in_specs=[V] * 8,
        out_specs=(V,) * 3,
        scratch_shapes=[kept, kept, kept, part, part],
        compiler_params=params(),
        name="attention_back",
    )(q, k, v, do, probs, x, dh1, wa)
    vectors = jnp.concatenate([gb[:2], gv[2:8]], axis=0).T

    def shared(t):
        mine = lax.psum_scatter(t.astype(F32), "fsdp", scatter_dimension=0, tiled=True)
        return lax.psum(mine.astype(BF), "rep").astype(F32)

    ga, gs = shared(g_qkv), shared(vectors)
    go, gu, gd, gb_up = shared(g_out), shared(g_up), shared(g_down), shared(gbu[0])
    gbq, gbv, gbo, gg1, gs1, gbd, gg2, gs2 = [gs[:, i] for i in range(8)]
    return (
        out.reshape(tokens.shape), pooled, gtok.reshape(tokens.shape),
        ga[:, :model], gbq, ga[:, model : 2 * model], ga[:, 2 * model :], gbv,
        go, gbo, gg1, gs1, gu, gb_up, gd, gbd, gg2, gs2,
    )


def solution(mesh):
    rows = P(("fsdp", "rep"))
    split = P("fsdp")
    placed = (rows, rows) + (split,) * 15 + (rows,)
    results = (rows,) * 3 + (split,) * 15
    owners = mesh.shape["fsdp"]

    def whole(*args):
        shard = args[2].shape[0] // owners
        ring = owners % 4 == 0 and mesh.shape["rep"] == 2 and shard % 16 == 0
        body = functools.partial(local_ring, owners // 4) if ring else local_plain
        return jax.shard_map(body, mesh=mesh, in_specs=placed, out_specs=results, check_vma=False)(*args)

    return whole
```

```python
import functools
import heapq
import math

import jax
import jax.numpy as jnp
from jax import lax
from jax.experimental import pallas as pl
from jax.experimental.pallas import tpu as pltpu
from jax.sharding import PartitionSpec as P

BF = jnp.bfloat16
F32 = jnp.float32
HEAD = 64
SEGS = 8
BLOCK = 128
EPS = 1e-5
MASKED = -1e30
MESH = pl.DeviceIdType.MESH
VMEM_LIMIT = int(63.5 * 2**20)


def nn(a, b):
    return lax.dot_general(a, b, (((1,), (0,)), ((), ())), preferred_element_type=F32)


def nt(a, b):
    return lax.dot_general(a, b, (((1,), (1,)), ((), ())), preferred_element_type=F32)


def tn(a, b):
    return lax.dot_general(a, b, (((0,), (0,)), ((), ())), preferred_element_type=F32)


def rmean(t):
    return jnp.mean(t, axis=-1, keepdims=True)


def csum(t):
    return jnp.sum(t, axis=0, keepdims=True)


def loop(count, step):
    def body(i, carry):
        step(i)
        return carry

    lax.fori_loop(0, count, body, 0)


def ds(start, size, multiple=None):
    if not isinstance(start, int):
        start = pl.multiple_of(start, multiple or size)
    return pl.ds(start, size)


def key_windows(length):
    blocks = length // BLOCK
    spans, offsets, total = [], [], 0
    for qb in range(blocks):
        span = (max(qb - 1, 0), min(qb + 2, blocks))
        spans.append(span)
        offsets.append(total)
        total += (span[1] - span[0]) * BLOCK
    return spans, offsets, total


def stack2(pair):
    lane = lax.broadcasted_iota(jnp.int32, pair.shape, 1)
    zero = jnp.zeros_like(pair)
    return jnp.concatenate(
        [jnp.where(lane < HEAD, pair, zero), jnp.where(lane < HEAD, zero, pair)], axis=0
    )


def unstack_t(both):
    return jnp.concatenate([both[:HEAD, :BLOCK], both[HEAD:, BLOCK:]], axis=0).T


def make_bias(seg, bias_at):
    rows, length = seg.shape
    spans, _, _ = key_windows(length)
    for row in range(rows):
        ids = seg[row : row + 1, :].astype(F32)
        keys = jnp.broadcast_to(ids, (BLOCK, length)).T
        for qb, (k0, k1) in enumerate(spans):
            same = keys[k0 * BLOCK : k1 * BLOCK, :] == ids[:, qb * BLOCK : (qb + 1) * BLOCK]
            bias_at(row, qb)[...] = jnp.where(same, 0.0, MASKED)


def attend_pair(row, length, q, k, v, o, probs_at, bias_at):
    spans, _, _ = key_windows(length)
    (q, cq), (k, ck), (v, cv), (o, co) = q, k, v, o
    r0 = pl.multiple_of(row * length, length)
    vt = v[pl.ds(r0, length), cv].T
    for qb, (k0, k1) in enumerate(spans):
        n = (k1 - k0) * BLOCK
        mine = pl.ds(r0 + qb * BLOCK, BLOCK)
        q2 = stack2(q[mine, cq] * BF(HEAD**-0.5))
        s = nt(k[pl.ds(r0 + k0 * BLOCK, n), ck], q2)
        b = bias_at(qb)[...]
        s = s + jnp.concatenate([b, b], axis=1)
        e = jnp.exp(s - jnp.max(s, axis=0, keepdims=True))
        p = (e * (1.0 / jnp.sum(e, axis=0, keepdims=True))).astype(BF)
        probs_at(qb)[...] = p
        o[mine, co] = unstack_t(nn(vt[:, k0 * BLOCK : k1 * BLOCK], p)).astype(BF)


def attend_back_pair(row, length, q, k, v, do, dq, probs_at, dk_sum, dv_sum):
    spans, _, _ = key_windows(length)
    last = len(spans) - 1
    (q, cq), (k, ck), (v, cv), (do, co) = q, k, v, do
    r0 = pl.multiple_of(row * length, length)
    kt = k[pl.ds(r0, length), ck].T
    for qb, (k0, k1) in enumerate(spans):
        n = (k1 - k0) * BLOCK
        mine = pl.ds(r0 + qb * BLOCK, BLOCK)
        q2 = stack2(q[mine, cq] * BF(HEAD**-0.5))
        do2 = stack2(do[mine, co])
        dp = nt(v[pl.ds(r0 + k0 * BLOCK, n), cv], do2)
        low = probs_at(qb)[...]
        p = low.astype(F32)
        d_s = (p * (dp - jnp.sum(p * dp, axis=0, keepdims=True))).astype(BF)
        dv_part = nn(low, do2)
        dk_part = nn(d_s, q2)
        for kb in range(k0, k1):
            part = slice((kb - k0) * BLOCK, (kb - k0 + 1) * BLOCK)
            held = slice(kb * BLOCK, (kb + 1) * BLOCK)
            a, b = dv_part[part], dk_part[part]
            if qb != max(kb - 1, 0):
                a, b = a + dv_sum[held, :], b + dk_sum[held, :]
            if qb == min(kb + 1, last):
                there = pl.ds(r0 + kb * BLOCK, BLOCK)
                v[there, cv] = a.astype(BF)
                k[there, ck] = b.astype(BF)
            else:
                dv_sum[held, :] = a
                dk_sum[held, :] = b
        dqt = nn(kt[:, k0 * BLOCK : k1 * BLOCK], d_s)
        dq[mine, co] = (unstack_t(dqt) * HEAD**-0.5).astype(BF)


class Place:
    def __init__(self, depth):
        self.depth = depth
        self.f = lax.axis_index("fsdp")
        self.y = lax.axis_index("rep")
        self.c = self.f % 2
        self.x = self.f // 2 % 2
        self.z = self.f // 4
        self.sib = (self.f + 1 - 2 * self.c, self.y)
        self.xn = (self.f + 2 - 4 * self.x, self.y)
        self.yn = (self.f, 1 - self.y)
        self.up = (self.f + 4, self.y)
        self.down = (self.f - 4, self.y)

    def barrier(self):
        sem = pltpu.get_barrier_semaphore()
        for who in (self.sib, self.xn, self.yn):
            pl.semaphore_signal(sem, inc=1, device_id=who, device_id_type=MESH)

        @pl.when(self.z > 0)
        def _():
            pl.semaphore_signal(sem, inc=1, device_id=self.down, device_id_type=MESH)

        @pl.when(self.z < self.depth - 1)
        def _():
            pl.semaphore_signal(sem, inc=1, device_id=self.up, device_id_type=MESH)

        inner = (self.z > 0).astype(jnp.int32) + (self.z < self.depth - 1).astype(jnp.int32)
        pl.semaphore_wait(sem, 3 + inner)


def remote(src, dst, send, recv, who):
    return pltpu.make_async_remote_copy(
        src_ref=src, dst_ref=dst, send_sem=send, recv_sem=recv, device_id=who, device_id_type=MESH
    )


def gather_sems(groups, depth):
    return [
        pltpu.SemaphoreType.DMA((groups, 2, depth - 1)),
        pltpu.SemaphoreType.DMA((groups, depth)),
        pltpu.SemaphoreType.DMA((groups, depth)),
        pltpu.SemaphoreType.DMA((groups, depth + 1)),
        pltpu.SemaphoreType.DMA((groups, depth)),
    ] * 2 + [pltpu.SemaphoreType.DMA((groups,))]


class Gather:
    def __init__(self, place, g, shard, whole, sems, halved=False):
        self.p, self.g, self.shard, self.whole = place, g, shard, whole
        self.halved = halved
        self.sz, self.sx, self.sy, self.sc, self.so, self.rz, self.rx, self.ry, self.rc, self.ro, self.own = sems
        self.rows, self.cols = whole.shape[3:]
        self.done = False

    def piece(self, z, x, half=None):
        return self.piece_of(z, x, self.p.c, half)

    def piece_of(self, z, x, c, half=None):
        if half is None:
            return self.whole.at[z, x, c]
        return self.whole.at[z, x, c, :, ds(half * (self.cols // 2), self.cols // 2)]

    def copy_z(self, direction, distance, z, src=None):
        dst = self.piece(z, self.p.x, self.p.y if self.halved else None)
        return remote(
            dst if src is None else src,
            dst,
            self.sz.at[self.g, direction, distance],
            self.rz.at[self.g, direction, distance],
            self.p.up if direction == 0 else self.p.down,
        )

    def copy_x(self, z, src=None):
        dst = self.piece(z, self.p.x, self.p.y)
        return remote(dst if src is None else src, dst, self.sx.at[self.g, z], self.rx.at[self.g, z], self.p.xn)

    def copy_y(self, z):
        at = self.piece(z, 1 - self.p.x, self.p.y)
        return remote(at, at, self.sy.at[self.g, z], self.ry.at[self.g, z], self.p.yn)

    def copy_c(self, z, src=None):
        dst = self.piece(z, self.p.x)
        return remote(dst if src is None else src, dst, self.sc.at[self.g, z], self.rc.at[self.g, z], self.p.sib)

    def copy_o(self, z):
        at = self.piece(z, self.p.x, self.p.y)
        return remote(at, at, self.so.at[self.g, z], self.ro.at[self.g, z], self.p.yn)

    def o_step(self, k):
        def act(z):
            at = self.piece(z, self.p.x, 1 - self.p.y)
            remote(at, at, self.so.at[self.g, z], self.ro.at[self.g, z], self.p.yn).wait_recv()
            self.copy_c(z).start()

        self.at_distance(k, act)

    def copy_column(self):
        at = self.whole.at[:, 1 - self.p.x, self.p.c]
        n = self.p.depth
        return remote(at, at, self.sc.at[self.g, n], self.rc.at[self.g, n], self.p.sib)

    def local(self):
        return pltpu.make_async_copy(self.shard, self.piece(self.p.z, self.p.x), self.own.at[self.g])

    def z_step(self, k):
        p = self.p
        if k == 0:
            if self.shard is None:
                shard, half = self.piece(p.z, p.x), self.piece(p.z, p.x, p.y)
            else:
                self.local().start()
                shard, half = self.shard, self.shard.at[:, ds(p.y * (self.cols // 2), self.cols // 2)]
            mine = half if self.halved else shard

            @pl.when(p.z < p.depth - 1)
            def _():
                self.copy_z(0, 0, p.z, mine).start()

            @pl.when(p.z > 0)
            def _():
                self.copy_z(1, 0, p.z, mine).start()

            self.copy_x(p.z, half).start()
            self.copy_c(p.z, shard).start()
            return

        for direction in (0, 1):
            z = p.z - k if direction == 0 else p.z + k

            @pl.when(z >= 0 if direction == 0 else z < p.depth)
            def _(direction=direction, z=z):
                self.copy_z(direction, k - 1, z).wait_recv()
                if k < p.depth - 1:

                    @pl.when(p.z < p.depth - 1 if direction == 0 else p.z > 0)
                    def _():
                        self.copy_z(direction, k, z).start()

                self.copy_x(z).start()
                if self.halved:
                    self.copy_o(z).start()
                else:
                    self.copy_c(z).start()

    def at_distance(self, k, act):
        p = self.p
        if k == 0:
            act(p.z)
            return

        @pl.when(p.z - k >= 0)
        def _():
            act(p.z - k)

        @pl.when(p.z + k < p.depth)
        def _():
            act(p.z + k)

    def x_step(self, k):
        def act(z):
            self.copy_x_in(z).wait_recv()
            self.copy_y(z).start()

        self.at_distance(k, act)

    def copy_x_in(self, z):
        at = self.piece(z, 1 - self.p.x, self.p.y)
        return remote(at, at, self.sx.at[self.g, z], self.rx.at[self.g, z], self.p.xn)

    def copy_y_in(self, z):
        at = self.piece(z, 1 - self.p.x, 1 - self.p.y)
        return remote(at, at, self.sy.at[self.g, z], self.ry.at[self.g, z], self.p.yn)

    def y_step(self, k):
        def act(z):
            self.copy_y_in(z).wait_recv()

        self.at_distance(k, act)
        if k == self.p.depth - 1:
            self.copy_column().start()

    def c_step(self):
        self.done = True
        if self.shard is not None:
            self.local().wait()
        p, n = self.p, self.p.depth
        for z in range(n):
            at = self.whole.at[z, p.x, 1 - p.c]
            remote(at, at, self.sc.at[self.g, z], self.rc.at[self.g, z], p.sib).wait_recv()
        at = self.whole.at[:, 1 - p.x, 1 - p.c]
        remote(at, at, self.sc.at[self.g, n], self.rc.at[self.g, n], p.sib).wait_recv()

    def end(self):
        p = self.p
        for k in range(p.depth - 1):
            @pl.when((p.z < p.depth - 1) & (p.z - k >= 0))
            def _():
                self.copy_z(0, k, p.z - k).wait_send()

            @pl.when((p.z > 0) & (p.z + k < p.depth))
            def _():
                self.copy_z(1, k, p.z + k).wait_send()

        for z in range(p.depth):
            self.copy_x(z).wait_send()
            self.copy_y(z).wait_send()
            self.copy_c(z).wait_send()
            if self.halved:

                @pl.when(p.z != z)
                def _(z=z):
                    self.copy_o(z).wait_send()

        self.copy_column().wait_send()


def scatter_sems(groups, depth):
    kinds = [(groups, 2), (groups,), (groups,), (groups, 2, depth - 1), (groups,)]
    return [pltpu.SemaphoreType.DMA(k) for k in kinds] * 2 + [pltpu.SemaphoreType.DMA((groups, 5))]


def scatter_buffers(rows, cols, depth):
    return [
        pltpu.VMEM((2, depth, rows, cols), BF),
        pltpu.VMEM((depth, rows, cols // 2), BF),
        pltpu.VMEM((depth, rows, cols // 2), BF),
        pltpu.VMEM((2 * depth - 3, rows, cols), BF),
        pltpu.VMEM((rows, cols), BF),
    ]


def scatter_half_buffers(rows, cols, depth):
    return [
        pltpu.VMEM((2, depth, rows, cols), BF),
        pltpu.VMEM((depth, rows, cols // 2), BF),
        pltpu.VMEM((depth, rows, cols), BF),
        pltpu.VMEM((2 * depth - 3, rows, cols // 2), BF),
        pltpu.VMEM((rows, cols // 2), BF),
    ]


def add_into(depth, rows, target, other):
    piece = min(rows, 48)
    parts = rows // piece

    def step(i):
        z, at = i // parts, ds(i % parts * piece, piece, 16)
        t = target(z, at)
        t[...] = t[...] + other(z, at)[...]

    loop(depth * parts, step)


class Scatter:
    first, second, along, last = ("y", 2), ("x", 2), 1.0, 1.0

    def __init__(self, place, g, grad, landing, buffers, sems):
        self.p, self.g, self.grad, self.landing = place, g, grad, landing
        self.in_c, self.in_y, self.in_x, self.in_z, self.in_f = buffers
        (self.sc, self.sy, self.sx, self.sz, self.sf, self.rc, self.ry, self.rx, self.rz, self.rf, self.out) = sems
        _, self.depth, self.rows, self.cols = self.in_c.shape

    def half(self, h):
        return ds(h * (self.cols // 2), self.cols // 2)

    def copy_c(self, x):
        p = self.p
        return remote(self.grad.at[:, x, 1 - p.c], self.in_c.at[x], self.sc.at[self.g, x], self.rc.at[self.g, x], p.sib)

    def copy_y(self):
        p = self.p
        return remote(
            self.grad.at[:, 1 - p.x, p.c, :, self.half(1 - p.y)], self.in_y, self.sy.at[self.g], self.ry.at[self.g], p.yn
        )

    def copy_x(self):
        p = self.p
        return remote(
            self.grad.at[:, 1 - p.x, p.c, :, self.half(p.y)], self.in_x, self.sx.at[self.g], self.rx.at[self.g], p.xn
        )

    def line_slot(self, direction, slot):
        far = self.depth - 2
        return 2 * far if slot == far else 2 * slot + direction

    def copy_z(self, direction, z, slot):
        p = self.p
        return remote(
            self.line_piece(z),
            self.in_z.at[self.line_slot(direction, slot)],
            self.sz.at[self.g, direction, slot],
            self.rz.at[self.g, direction, slot],
            p.up if direction == 0 else p.down,
        )

    def copy_f(self):
        p = self.p
        return remote(self.grad.at[p.z, p.x, p.c], self.in_f, self.sf.at[self.g], self.rf.at[self.g], p.yn)

    def receive(self):
        self.copy_f().wait_recv()

    def end_y(self):
        self.copy_y().wait_send()

    def begin(self):
        self.copy_c(1 - self.p.x).start()
        self.copy_c(self.p.x).start()

    def cores(self, turn):
        p = self.p
        x = 1 - p.x if turn == 0 else p.x
        self.copy_c(x).wait_recv()
        add_into(
            self.depth,
            self.rows,
            lambda z, at: self.grad.at[z, x, p.c, at],
            lambda z, at: self.in_c.at[x, z, at],
        )
        if turn == 0:
            self.begin_exchange()

    def begin_exchange(self):
        self.copy_y().start()

    def line_piece(self, z):
        return self.grad.at[z, self.p.x, self.p.c]

    def over_y(self):
        p = self.p
        self.copy_y().wait_recv()
        add_into(
            self.depth,
            self.rows,
            lambda z, at: self.grad.at[z, 1 - p.x, p.c, at, self.half(p.y)],
            lambda z, at: self.in_y.at[z, at],
        )
        self.copy_x().start()

    def over_x(self):
        p = self.p
        self.copy_x().wait_recv()
        add_into(
            self.depth,
            self.rows,
            lambda z, at: self.grad.at[z, p.x, p.c, at, self.half(p.y)],
            lambda z, at: self.in_x.at[z, at],
        )

    def line(self, wave):
        p, top = self.p, self.depth - 1
        for direction in (0, 1):
            place = p.z if direction == 0 else top - p.z
            if wave == 0:

                @pl.when(place == 0)
                def _(direction=direction):
                    for far in range(top, 0, -1):
                        self.copy_z(direction, far if direction == 0 else top - far, far - 1).start()

                continue

            @pl.when((place >= 1) & (place <= wave))
            def _(direction=direction, place=place):
                far = top - wave + place
                z = far if direction == 0 else top - far
                slot = top - wave
                self.copy_z(direction, z, slot).wait_recv()
                add_into(
                    1,
                    self.rows,
                    lambda _, at: self.line_piece(z).at[at],
                    lambda _, at: self.in_z.at[self.line_slot(direction, slot), at],
                )
                if slot > 0:
                    self.copy_z(direction, z, slot - 1).start()

    def share(self):
        self.copy_f().start()

    def copy_out(self, n):
        _, view, result = self.landing[n]
        return pltpu.make_async_copy(view, result, self.out.at[self.g, n])

    def finish(self):
        p = self.p
        self.receive()
        piece = min(self.rows, 48)
        c0 = 0
        for n, (cols, view, result) in enumerate(self.landing):
            if view is None:
                c0 += cols
                continue

            def step(i, view=view, c0=c0, cols=cols):
                at = ds(i * piece, piece, 16)
                cs = pl.ds(c0, cols)
                view[at, :] = self.total(at, cs)

            loop(self.rows // piece, step)
            if result is not None:
                self.copy_out(n).start()
            c0 += cols

    def total(self, at, cs):
        p = self.p
        return self.grad[p.z, p.x, p.c, at, cs].astype(F32) + self.in_f[at, cs].astype(F32)

    def end(self):
        p, top = self.p, self.depth - 1
        for x in (0, 1):
            self.copy_c(x).wait_send()
        self.end_y()
        self.copy_x().wait_send()
        for direction in (0, 1):
            place = p.z if direction == 0 else top - p.z
            for slot in range(top):

                @pl.when(place + slot < top)
                def _(direction=direction, slot=slot):
                    self.copy_z(direction, 0, slot).wait_send()

        self.copy_f().wait_send()
        for n, (_, _, result) in enumerate(self.landing):
            if result is not None:
                self.copy_out(n).wait()

    def exchanges(self):
        return [self.over_y, self.over_x]

    def steps(self):
        one, two = self.exchanges()

        def two_and_line():
            two()
            self.line(0)

        out = [lambda: self.cores(0), lambda: self.cores(1), one, two_and_line]
        for wave in range(1, self.depth):
            out.append(functools.partial(self.line, wave))
        return out + [self.share, self.finish]


class HalfScatter(Scatter):
    first, second, along, last = ("x", 4), ("y", 2), 0.5, 0.5

    def copy_x(self):
        p = self.p
        return remote(self.grad.at[:, 1 - p.x, p.c], self.in_x, self.sx.at[self.g], self.rx.at[self.g], p.xn)

    def copy_y(self):
        p = self.p
        return remote(
            self.grad.at[:, p.x, p.c, :, self.half(1 - p.y)], self.in_y, self.sy.at[self.g], self.ry.at[self.g], p.yn
        )

    def begin_exchange(self):
        self.copy_x().start()

    def exchanges(self):
        return [self.over_x, self.over_y]

    def over_x(self):
        p = self.p
        self.copy_x().wait_recv()
        add_into(
            self.depth,
            self.rows,
            lambda z, at: self.grad.at[z, p.x, p.c, at],
            lambda z, at: self.in_x.at[z, at],
        )
        self.copy_y().start()

    def over_y(self):
        p = self.p
        self.copy_y().wait_recv()
        add_into(
            self.depth,
            self.rows,
            lambda z, at: self.line_piece(z).at[at],
            lambda z, at: self.in_y.at[z, at],
        )

    def line_piece(self, z):
        return self.grad.at[z, self.p.x, self.p.c, :, self.half(self.p.y)]

    def copy_f(self):
        return remote(self.line_piece(self.p.z), self.in_f, self.sf.at[self.g], self.rf.at[self.g], self.p.yn)

    def receive(self):
        p = self.p
        self.copy_f().wait_recv()
        self.copy_y().wait_send()
        self.grad[p.z, p.x, p.c, :, self.half(1 - p.y)] = self.in_f[...]

    def end_y(self):
        pass

    def total(self, at, cs):
        p = self.p
        return self.grad[p.z, p.x, p.c, at, cs].astype(F32)


def spread(place, owners_rows, parts):
    width = place.shape[0]
    row = lax.broadcasted_iota(jnp.int32, (width, 1), 0)
    target = row
    for owner in range(1, width // owners_rows):
        target = target + jnp.where(row >= owner * owners_rows, (parts - 1) * owners_rows, 0)
    lane = lax.broadcasted_iota(jnp.int32, (width, width * parts), 1)
    place[...] = (lane == target).astype(BF)


def unpack_small(columns, shard, parts, vec, bup, room):
    rows = columns.astype(F32).T
    vec[...] = rows[:8, :]
    low = rows[8:16, :].astype(BF)
    width = 8 * shard
    place = room.at[:width, : width * parts]
    spread(place, shard, parts)
    for t in range(columns.shape[0] // width):
        wide = nn(low[:, t * width : (t + 1) * width], place[...])
        total = wide[0:1]
        for i in range(1, parts):
            total = total + pltpu.roll(wide, i * shard, 1)[i : i + 1]
        bup[:, t * width * parts : (t + 1) * width * parts] = total


def pack_small(gv, gbu, shard, parts, room):
    width = 8 * shard
    wide = width * parts
    model = gv.shape[1]
    place = room.at[:width, :wide]
    spread(place, shard, parts)
    columns = jnp.concatenate([gv, jnp.zeros((BLOCK - 8, model), F32)], axis=0).T
    found = []
    for t in range(model // width):
        piece = jnp.broadcast_to(gbu[:, t * wide : (t + 1) * wide], (8, wide))
        rows = [jnp.zeros((8, wide), F32)]
        for i in range(parts):
            rows.append((pltpu.roll(piece, wide - i * shard, 1) if i else piece)[0:1])
        rows.append(jnp.zeros((BLOCK - 8 - parts, wide), F32))
        found.append(nt(place[...], jnp.concatenate(rows, axis=0).astype(BF)))
    return (columns + jnp.concatenate(found, axis=0)).astype(BF)


ROWS = 256
CHUNK = 512


def phi_parts(u):
    cdf = 0.5 * (1.0 + lax.erf(u * math.sqrt(0.5)))
    pdf = jnp.exp(-0.5 * u * u) * (1.0 / math.sqrt(2.0 * math.pi))
    return cdf, pdf


V = pl.BlockSpec(memory_space=pltpu.VMEM)
ANY = pl.BlockSpec(memory_space=pl.ANY)
sds = jax.ShapeDtypeStruct


def params(collective_id=None):
    if collective_id is None:
        return pltpu.CompilerParams(vmem_limit_bytes=VMEM_LIMIT)
    return pltpu.CompilerParams(
        vmem_limit_bytes=VMEM_LIMIT, collective_id=collective_id, has_side_effects=True
    )


class Links:
    core_rate = 350.0

    def __init__(self):
        self.free = dict.fromkeys("cxyz", 0.0)
        self.heap = []
        self.count = 0
        self.rate, self.lag = GATHER

    def send(self, link, at, size):
        rate = self.core_rate if link == "c" else self.rate
        self.free[link] = max(at, self.free[link]) + size / rate * 1e-3
        return self.free[link] + self.lag

    def push(self, at, task, then=None):
        self.count += 1
        heapq.heappush(self.heap, (at, self.count, task, then))

    def gather(self, gather, at):
        size = gather.rows * gather.cols * 2
        part = size / 2 if gather.halved else size
        depth = gather.p.depth

        def zed(k):
            def then(now):
                if k < depth - 1:
                    self.push(self.send("z", now, part), lambda: gather.z_step(k + 1), zed(k + 1))
                self.push(self.send("x", now, size / 2), lambda: gather.x_step(k), ex(k))
                if k and gather.halved:
                    self.push(self.send("y", now, size / 2), lambda: gather.o_step(k))

            return then

        def ex(k):
            return lambda now: self.push(
                self.send("y", now, size / 2), lambda: gather.y_step(k), lambda now: None if k < depth - 1
                else self.push(now + 2.0, gather.c_step)
            )

        self.push(at, lambda: gather.z_step(0), zed(0))

    def scatter(self, scatter, at):
        size = scatter.rows * scatter.cols * 2
        steps = scatter.steps()
        last = len(steps) - 1

        def after(n):
            def then(now):
                now = now + 0.3
                if n == 0:
                    link, count = scatter.first
                    self.push(self.send(link, now, count * size), steps[2], after(2))
                elif n == 2:
                    link, count = scatter.second
                    self.push(self.send(link, now, count * size), steps[3], after(3))
                elif 3 <= n < last - 2:
                    self.push(self.send("z", now, scatter.along * size), steps[n + 1], after(n + 1))
                elif n == last - 2:
                    self.push(now, steps[last - 1], after(last - 1))
                elif n == last - 1:
                    self.push(self.send("y", now, scatter.last * size), steps[last])

            return then

        self.push(self.send("c", at, 4 * size), steps[0], after(0))
        self.push(self.send("c", at, 4 * size), steps[1])

    def due(self, now):
        found = []
        while self.heap and self.heap[0][0] <= now:
            at, _, task, then = heapq.heappop(self.heap)
            found.append(task)
            if then:
                then(at)
        return found

    def all(self):
        return self.due(float("inf"))

    def next(self):
        return self.heap[0][0]


class Clock:
    def __init__(self, links):
        self.links, self.now = links, 0.0

    def run(self, tasks):
        for task in tasks:
            task()

    def spend(self, time):
        self.now += time
        self.run(self.links.due(self.now))

    def until(self, gather):
        while not gather.done:
            self.now = max(self.now, self.links.next())
            self.run(self.links.due(self.now))

    def loop(self, count, step, time):
        ticks = []
        for _ in range(count):
            self.now += time
            ticks.append(self.links.due(self.now))

        def body(i):
            step(i)
            for n, tasks in enumerate(ticks):
                if tasks:

                    @pl.when(i == n)
                    def _(tasks=tasks):
                        self.run(tasks)

        loop(count, body)


def head_groups(pairs):
    few = pairs // 3
    return [(0, few), (few, pairs - few)]


def group_columns(pairs):
    groups = head_groups(pairs)
    blank = 2 * BLOCK
    return [(0, blank), (3 * groups[0][1] * BLOCK + blank, 0)]


LIGHT = ("o", 0, 1)


def column_cuts(model):
    third = model // 3
    return [(0, third), (third, model - third)]


def layer_kernel(depth, parts, cuts, *refs):
    it = iter(refs)

    def take(n):
        return [next(it) for _ in range(n)]

    x_in, seg, sq, sk, sv, small_in, so, su, sd, og_in = take(10)
    out, pooled, gtok, gq, gk, gv_w, go_w, gu_w, gd_w, small, p_main, p_last = take(12)
    x, q, k, v, o, z_low, df, n1s, dh, r1s, g, sl, stage = take(13)
    wa, wo, wu, wd, gv, gbu, vec, bup = take(8)
    sets = [take(5) for _ in cuts]
    gsems, ssems, msem, osem, psem, asem = take(11), take(11), *take(4)

    seqs, length = seg.shape
    tokens, model = x.shape
    hidden = g.shape[1]
    dk_sum, dv_sum = r1s.at[:length], r1s.at[length : 2 * length]
    shard = so.shape[0]
    pairs = model // BLOCK
    spans, offsets, _ = key_windows(length)
    final = len(spans) - 1
    tiles = tokens // ROWS

    def span_rows(qb):
        return (spans[qb][1] - spans[qb][0]) * BLOCK

    def bias_at(row, qb):
        at = 0 if qb == final else offsets[qb]
        lane = (row * 2 + (1 if qb == final else 0)) * BLOCK
        return dh.at[at : at + span_rows(qb), ds(lane, BLOCK)]

    def probs_of(i):
        def at(qb):
            held, at = (sl, 0) if qb == final else (g, offsets[qb])
            return held.at[at : at + span_rows(qb), ds(i * 2 * BLOCK, 2 * BLOCK)]

        return at

    groups = head_groups(pairs)
    packed = group_columns(pairs)

    def group_span(n):
        first, size = groups[n]
        return slice(first * BLOCK, (first + size) * BLOCK)

    def weight_span(n, part):
        width = groups[n][1] * BLOCK
        return slice(packed[n][0] + part * width, packed[n][0] + (part + 1) * width)

    def weight_of(span):
        return wa[:, :, :, :, span].reshape(model, span.stop - span.start)

    place = Place(depth)
    links = Links()
    clock = Clock(links)
    loads = [pltpu.make_async_copy(x_in, x, msem.at[0]), pltpu.make_async_copy(og_in, df, msem.at[1])]
    mine = wa.at[place.z, place.x, place.c]
    packs = [pltpu.make_async_copy(small_in, mine.at[:, 3 * groups[0][1] * BLOCK : packed[1][0]], asem.at[0])]
    for n in range(len(groups)):
        for part, source in enumerate((sq, sk, sv)):
            there = mine.at[:, weight_span(n, part)]
            packs.append(pltpu.make_async_copy(source.at[:, group_span(n)], there, asem.at[len(packs)]))
    for load in packs + loads:
        load.start()
    early = packed[1][0]
    sources = (
        (None, wa.at[:, :, :, :, :early]),
        (None, wa.at[:, :, :, :, early:]),
        (so, wo), (su, wu), (sd, wd),
    )
    gathers = [Gather(place, n, s, w, gsems, n in HALVED) for n, (s, w) in enumerate(sources)]
    for gather, at in zip(gathers, BEGINS):
        links.gather(gather, at)
    for load in packs:
        load.wait()
    place.barrier()
    clock.spend(1.0)
    make_bias(seg, bias_at)
    loads[0].wait()
    clock.until(gathers[0])
    at = packed[0][0] + 3 * groups[0][1] * BLOCK
    unpack_small(wa[:, :, :, :, at : at + BLOCK].reshape(model, BLOCK), shard, parts, vec, bup, g)

    def vrow(i):
        return vec[i : i + 1, :]

    def project(n):
        here = group_span(n)

        def step(rt):
            rows = ds(rt * ROWS, ROWS)
            for part, (to, bias) in enumerate(((q, 0), (k, None), (v, 1))):
                value = nn(x[rows, :], weight_of(weight_span(n, part)))
                to[rows, here] = (value if bias is None else value + vec[bias : bias + 1, here]).astype(BF)

        clock.loop(tiles, step, 0.25 * groups[n][1])

    def copy_probs(i, which, back=False):
        lanes = ds(i * 2 * BLOCK, 2 * BLOCK)
        here = g.at[:, lanes] if which == 0 else sl.at[: span_rows(final), lanes]
        there = (p_main if which == 0 else p_last).at[:, lanes]
        return pltpu.make_async_copy(here, there, psem.at[which, i])

    def attend(n):
        first, size = groups[n]

        def step(j):
            row, local = j // size, j % size
            i = row * pairs + first + local
            c = ds((first + local) * BLOCK, BLOCK)
            attend_pair(row, length, (q, c), (k, c), (v, c), (o, c), probs_of(i), functools.partial(bias_at, row))
            copy_probs(i, 0).start()
            copy_probs(i, 1).start()

        clock.loop(seqs * size, step, ATTEND)

    for n in range(len(groups)):
        clock.until(gathers[min(n, 1)])
        project(n)
        attend(n)
    for i in range(seqs * pairs):
        copy_probs(i, 0).wait()
        copy_probs(i, 1).wait()

    chunks = hidden // CHUNK

    def up(i):
        rows = ds(i // chunks * ROWS, ROWS)

        @pl.when(i % chunks == 0)
        def _():
            h = x[rows, :].astype(F32) + (nn(o[rows, :], wo[...].reshape(model, model)) + vrow(2))
            c = h - rmean(h)
            r = lax.rsqrt(rmean(c * c) + EPS)
            n = c * r
            n1s[rows, :] = n
            r1s[rows, :] = jnp.broadcast_to(r, (ROWS, BLOCK))
            z_low[rows, :] = (n * vrow(3) + vrow(4)).astype(BF)

        cs = ds(i % chunks * CHUNK, CHUNK)
        u = nn(z_low[rows, :], wu[:, :, :, :, cs].reshape(model, CHUNK)) + bup[:, cs]
        cdf, pdf = phi_parts(u)
        g[rows, cs] = (u * cdf).astype(BF)
        sl[rows, cs] = (cdf + u * pdf).astype(BF)

    clock.until(gathers[2])
    clock.until(gathers[3])
    clock.loop(tiles * chunks, up, 22.0 / (tiles * chunks))
    clock.until(gathers[4])
    for gather in gathers:
        gather.end()
    loads[1].wait()
    gv[...] = jnp.zeros_like(gv)
    pooled[...] = jnp.zeros_like(pooled)

    def copy_tile(rt):
        return pltpu.make_async_copy(stage, out.at[ds(rt * ROWS, ROWS)], osem.at[0])

    def down(rt):
        rows = ds(rt * ROWS, ROWS)
        h = (n1s[rows, :] * vrow(3) + vrow(4)) + (nn(g[rows, :], wd[...].reshape(hidden, model)) + vrow(5))
        c = h - rmean(h)
        r = lax.rsqrt(rmean(c * c) + EPS)
        n2 = c * r
        y = n2 * vrow(6) + vrow(7)
        y_low = y.astype(BF)

        @pl.when(rt > 0)
        def _():
            copy_tile(rt - 1).wait()

        stage[...] = y_low
        copy_tile(rt).start()
        row = rt * ROWS // length
        ids = seg[pl.ds(row, 1), ds(rt * ROWS % length, ROWS)]
        onehot = (ids == lax.broadcasted_iota(jnp.int32, (SEGS, ROWS), 0)).astype(BF)
        pooled[row] = pooled[row] + (nn(onehot, y_low) + nn(onehot, (y - y_low.astype(F32)).astype(BF)))
        dy = df[rows, :].astype(F32)
        gv[6:7, :] += csum(dy * n2)
        gv[7:8, :] += csum(dy)
        e = dy * vrow(6)
        d = r * (e - rmean(e) - n2 * rmean(e * n2))
        dh[rows, :] = d
        low = d.astype(BF)
        df[rows, :] = low
        gv[5:6, :] += csum(low.astype(F32))

    clock.loop(tiles, down, 3.0)
    copy_tile(tiles - 1).wait()
    for row in range(seqs):
        onehot = (seg[row : row + 1, :] == lax.broadcasted_iota(jnp.int32, (SEGS, length), 0)).astype(F32)
        pooled[row] = pooled[row] / jnp.sum(onehot, axis=1, keepdims=True)

    pair_rows = 2 * sd.shape[0]

    def up_back(cc):
        cs = ds(cc * pair_rows, pair_rows, BLOCK)
        weight = wd[cc // 2, cc % 2].reshape(pair_rows, model)
        total = jnp.zeros((1, pair_rows), F32)
        for rt in range(tiles):
            rows = slice(rt * ROWS, (rt + 1) * ROWS)
            du = (nt(df[rows, :], weight) * sl[rows, cs].astype(F32)).astype(BF)
            sl[rows, cs] = du
            total += csum(du.astype(F32))
        gbu[:, cs] = total
        wd[cc // 2, cc % 2] = tn(g[:, cs], df[...]).astype(BF).reshape(2, sd.shape[0], model)

    clock.loop(hidden // pair_rows, up_back, 1.7)
    links.rate, links.lag = SCATTER

    base = {}
    at = 0
    for name, rows in (("d", sd.shape[0]), ("o", shard), ("u", shard * (hidden // model)), ("q", shard), ("k", shard),
                       ("v", shard), ("small", shard)):
        base[name] = at
        at += rows
    results = {"d": gd_w, "o": go_w, "u": gu_w, "q": gq, "k": gk, "v": gv_w}
    weights = {"d": wd, "o": wo, "u": wu}
    scatters = {}
    for n, (name, r0, rows, c0, cols) in enumerate(cuts):
        landing = []
        if isinstance(name, int):
            first, size = groups[name]
            cs = slice(first * BLOCK, (first + size) * BLOCK)
            spans_of = [(weight, cs.start + at, part * size * BLOCK + at) for part, weight in enumerate("qkv")
                        for at in range(0, size * BLOCK, 2 * BLOCK)]
            for weight, to, at in spans_of:
                if c0 <= at < c0 + cols:
                    ends = slice(to, to + 2 * BLOCK)
                    landing.append((2 * BLOCK, n1s.at[base[weight] : base[weight] + shard, ends], results[weight].at[:, ends]))
            if packed[name][1] and c0 + cols > 3 * size * BLOCK:
                landing.append((BLOCK, n1s.at[base["small"] : base["small"] + shard, :BLOCK], None))
            grad = wa.at[:, :, :, :, packed[name][0] + c0 : packed[name][0] + c0 + cols]
        else:
            for c in range(c0, c0 + cols, model):
                top = base[name] + c // model * shard + r0
                width = min(model, c0 + cols - c)
                at = c % model
                landing.append((width, n1s.at[top : top + rows, at : at + width],
                                results[name].at[r0 : r0 + rows, c : c + width]))
            grad = weights[name].at[:, :, :, r0 : r0 + rows, c0 : c0 + cols]
        kind = HalfScatter if name in LIGHT else Scatter
        scatters.setdefault(name, []).append(kind(place, n, grad, landing, sets[n], ssems))

    def send_home(name, number=None):
        for n, s in enumerate(scatters[name]):
            if number is None or n == number:
                s.begin()
                links.scatter(s, clock.now)

    send_home("d")
    bring = [
        pltpu.make_async_copy(p_main, g, msem.at[2]),
        pltpu.make_async_copy(p_last, sl.at[: span_rows(final)], msem.at[3]),
    ]
    bring[0].start()

    def first_back(rt):
        rows = ds(rt * ROWS, ROWS)
        dz = dh[rows, :] + nt(sl[rows, :], wu[...].reshape(model, hidden))
        n1 = n1s[rows, :]
        gv[3:4, :] += csum(dz * n1)
        gv[4:5, :] += csum(dz)
        e = dz * vrow(3)
        d = r1s[rows, 0:1] * (e - rmean(e) - n1 * rmean(e * n1))
        dh[rows, :] = d
        da = d.astype(BF)
        df[rows, :] = da
        gv[2:3, :] += csum(da.astype(F32))

    clock.loop(tiles, first_back, 2.0)

    quarter = hidden // 4
    for n in range(2):

        def up_grad(cc, n=n):
            cs = ds((2 * n + cc) * quarter, quarter, BLOCK)
            wu[:, :, :, :, cs] = tn(z_low[...], sl[:, cs]).astype(BF).reshape(depth, 2, 2, shard, quarter)

        clock.loop(2, up_grad, 1.5)
        send_home("u", n)

    bring[1].start()
    do = z_low

    def out_back(rt):
        rows = ds(rt * ROWS, ROWS)
        do[rows, :] = nt(df[rows, :], wo[...].reshape(model, model)).astype(BF)

    clock.loop(tiles, out_back, 0.4)
    half = model // 2

    def halves(left, right, columns, to, at, time):
        width = columns.stop - columns.start

        def step(t):
            value = tn(left[:, ds(t * half, half, BLOCK)], right[:, columns]).astype(BF)
            shaped = value.reshape(depth // 2, 2, 2, shard, width)
            to[pl.ds(t * (depth // 2), depth // 2), :, :, :, at : at + width] = shaped

        clock.loop(2, step, time)

    halves(o, df, slice(0, model), wo, 0, 0.8)
    send_home("o")
    bring[0].wait()
    bring[1].wait()

    dq = o

    def copy_tokens(rt):
        rows = ds(rt * ROWS, ROWS)
        return pltpu.make_async_copy(x.at[rows], gtok.at[rows], psem.at[0, rt])

    for n in reversed(range(len(groups))):
        first, size = groups[n]
        here = group_span(n)

        def back(j, first=first, size=size):
            row, local = j // size, j % size
            c = ds((first + local) * BLOCK, BLOCK)
            attend_back_pair(row, length, (q, c), (k, c), (v, c), (do, c), dq, probs_of(row * pairs + first + local),
                             dk_sum, dv_sum)

        clock.loop(seqs * size, back, BACK)

        def token_step(rt, n=n, here=here):
            rows = ds(rt * ROWS, ROWS)
            total = dh[rows, :]
            for part, d in enumerate((dq, k, v)):
                total = total + nt(d[rows, here], weight_of(weight_span(n, part)))
            dh[rows, :] = total
            gv[0:1, here] += csum(dq[rows, here].astype(F32))
            gv[1:2, here] += csum(v[rows, here].astype(F32))

        clock.loop(tiles, token_step, 0.25 * size)
        for part, d in enumerate((dq, k, v)):
            span = weight_span(n, part)
            halves(x, d, here, wa, span.start, 0.15 * size)
        if n == 0:
            blank = packed[0][0] + 3 * size * BLOCK

            @pl.when(place.z >= 0)
            def _(blank=blank):
                columns = pack_small(gv[...], gbu[...], shard, parts, g).reshape(depth, 2, 2, shard, BLOCK)
                wa[:, :, :, :, blank : blank + BLOCK] = columns

        send_home(n)

    def token_out(rt):
        rows = ds(rt * ROWS, ROWS)
        x[rows, :] = dh[rows, :].astype(BF)
        copy_tokens(rt).start()

    clock.loop(tiles, token_out, 0.2)
    clock.run(links.all())
    for group in scatters.values():
        for s in group:
            s.end()
    for rt in range(tiles):
        copy_tokens(rt).wait()
    last = n1s[base["small"] : base["small"] + shard, :BLOCK]
    square = jnp.concatenate([last, jnp.zeros((BLOCK - shard, BLOCK), F32)], axis=0).T
    small[...] = square[:16, :]


BEGINS = (0.0, 5.0, 13.0, 16.0, 24.0)
HALVED = ()
GATHER, SCATTER = (52.0, 3.0), (50.0, 2.0)
ATTEND, BACK = 1.6, 1.7


def run_layer(depth, x, seg, sq, sk, sv, small, so, su, sd, og):
    tokens, model = x.shape
    hidden = su.shape[1]
    parts = hidden // model
    seqs, length = seg.shape
    spans, offsets, band = key_windows(length)
    final_rows = band - offsets[-1]
    shard = so.shape[0]
    cuts = []
    for at, width in column_cuts(model):
        cuts.append(("d", 0, sd.shape[0], at, width))
    for part in range(2):
        cuts.append(("u", 0, shard, part * (hidden // 2), hidden // 2))
    cuts.append(("o", 0, shard, 0, model))
    groups = head_groups(model // BLOCK)
    for n, (_, blank) in enumerate(group_columns(model // BLOCK)):
        width = 3 * groups[n][1] * BLOCK + blank
        cuts += [(n, 0, shard, part * (width // 2), width // 2) for part in range(2)]
    buffers = []
    for name, _, rows, _, cols in cuts:
        buffers += (scatter_half_buffers if name in LIGHT else scatter_buffers)(rows, cols, depth)

    def own(s):
        return pltpu.VMEM((depth, 2, 2, *s), BF)

    act, wide = pltpu.VMEM((tokens, model), BF), pltpu.VMEM((tokens, hidden), BF)
    full = pltpu.VMEM((tokens, model), F32)
    weight = sds((shard, model), F32)
    iterations = seqs * model // BLOCK
    return pl.pallas_call(
        functools.partial(layer_kernel, depth, parts, tuple(cuts)),
        out_shape=(sds((tokens, model), BF), sds((seqs, SEGS, model), F32), sds((tokens, model), BF),
                   weight, weight, weight, weight, sds(su.shape, F32), sds(sd.shape, F32), sds((16, BLOCK), F32),
                   sds((tokens, hidden), BF), sds((final_rows, hidden), BF)),
        in_specs=[ANY, V] + [ANY] * 8,
        out_specs=(ANY, V, ANY) + (ANY,) * 6 + (V, ANY, ANY),
        scratch_shapes=[act] * 7 + [full, full, pltpu.VMEM((max(tokens, 2 * length), BLOCK), F32), wide, wide,
                        pltpu.VMEM((ROWS, model), BF), own((shard, 3 * model + small.shape[1])), own(so.shape), own(su.shape), own(sd.shape),
                        pltpu.VMEM((8, model), F32), pltpu.VMEM((1, hidden), F32), pltpu.VMEM((8, model), F32),
                        pltpu.VMEM((1, hidden), F32), *buffers, *gather_sems(5, depth),
                        *scatter_sems(len(cuts), depth), pltpu.SemaphoreType.DMA((4,)), pltpu.SemaphoreType.DMA((1,)),
                        pltpu.SemaphoreType.DMA((2, iterations)),
                        pltpu.SemaphoreType.DMA((1 + 3 * len(groups),))],
        compiler_params=params(0),
        name="layer",
    )(x, seg, sq, sk, sv, small, so, su, sd, og)


def hand_over_kernel(count, shard, parts, *refs):
    ins, small = refs[:count], refs[count]
    outs, vectors = refs[count + 1 : 2 * count + 1], refs[2 * count + 1 : 2 * count + 10]
    rooms, sems = refs[2 * count + 10 : -1], refs[-1]
    fetches = [pltpu.make_async_copy(a, b, sems.at[0, n]) for n, (a, b) in enumerate(zip(ins, rooms))]
    copies = [pltpu.make_async_copy(a, b, sems.at[1, n]) for n, (a, b) in enumerate(zip(rooms, outs))]
    for copy in fetches:
        copy.start()
    for n in range(8):
        vectors[n][...] = small[n, :shard]
    rows = jnp.concatenate([small[8:16, :], jnp.zeros((8, BLOCK), F32)], axis=1)
    total = rows[0]
    for i in range(1, parts):
        total = total + pltpu.roll(rows, i * shard, 1)[i]
    vectors[8][...] = total[: parts * shard]
    for fetch, copy in zip(fetches, copies):
        fetch.wait()
        copy.start()
    for copy in copies:
        copy.wait()


def hand_over(results, small, shard, parts):
    count = len(results)
    return pl.pallas_call(
        functools.partial(hand_over_kernel, count, shard, parts),
        out_shape=[sds(r.shape, r.dtype) for r in results] + [sds((shard,), F32)] * 8 + [sds((parts * shard,), F32)],
        in_specs=[ANY] * count + [V],
        out_specs=[ANY] * count + [V] * 9,
        scratch_shapes=[pltpu.VMEM(r.shape, r.dtype) for r in results] + [pltpu.SemaphoreType.DMA((2, count))],
        name="hand_over",
    )(*results, small)


def local_ring(depth, *args):
    (tokens, segments, w_query, b_query, w_key, w_value, b_value, w_out, b_out, gain1, shift1, w_up, b_up, w_down,
     b_down, gain2, shift2, out_grad) = args
    seqs, length, model = tokens.shape
    shard = w_query.shape[0]
    parts = w_up.shape[1] // model
    x = tokens.reshape(seqs * length, model)
    og = out_grad.reshape(seqs * length, model)
    small = jnp.stack([b_query, b_value, b_out, gain1, shift1, b_down, gain2, shift2] + [
        b_up[i * shard : (i + 1) * shard] for i in range(parts)
    ], axis=1)
    small = jnp.pad(small, ((0, 0), (0, 2 * BLOCK - 8 - parts)))
    *results, gs, _, _ = run_layer(depth, x, segments, w_query, w_key, w_value, small, w_out, w_up, w_down, og)
    out, pooled, gtok, gq, gk, gv, go, gu, gd, gbq, gbv, gbo, gg1, gs1, gbd, gg2, gs2, gb_up = hand_over(
        results, gs, shard, parts
    )
    return (
        out.reshape(tokens.shape), pooled, gtok.reshape(tokens.shape),
        gq, gbq, gk, gv, gbv, go, gbo, gg1, gs1, gu, gb_up, gd, gbd, gg2, gs2,
    )


def mid_kernel(*refs):
    (x, o, og, seg, wo, wu, wd, vec, bup, out, pooled, g_down, g_up, g_out, do, dh1, gv, gbu,
     n1s, r1s, z_low, g, sl, df, dh2) = refs
    tokens, model = x.shape
    hidden = wu.shape[1]
    seqs, length = seg.shape
    gv[...] = jnp.zeros_like(gv)
    pooled[...] = jnp.zeros_like(pooled)

    def vrow(i):
        return vec[i : i + 1, :]

    def up(rt):
        rows = ds(rt * ROWS, ROWS)
        h = x[rows, :].astype(F32) + (nn(o[rows, :], wo[...]) + vrow(2))
        c = h - rmean(h)
        r = lax.rsqrt(rmean(c * c) + EPS)
        n = c * r
        n1s[rows, :] = n
        r1s[rows, :] = jnp.broadcast_to(r, (ROWS, BLOCK))
        z_low[rows, :] = (n * vrow(3) + vrow(4)).astype(BF)
        for cc in range(hidden // CHUNK):
            cs = slice(cc * CHUNK, (cc + 1) * CHUNK)
            u = nn(z_low[rows, :], wu[:, cs]) + bup[:, cs]
            cdf, pdf = phi_parts(u)
            g[rows, cs] = (u * cdf).astype(BF)
            sl[rows, cs] = (cdf + u * pdf).astype(BF)

    loop(tokens // ROWS, up)

    def down(rt):
        rows = ds(rt * ROWS, ROWS)
        h = (n1s[rows, :] * vrow(3) + vrow(4)) + (nn(g[rows, :], wd[...]) + vrow(5))
        c = h - rmean(h)
        r = lax.rsqrt(rmean(c * c) + EPS)
        n2 = c * r
        y = n2 * vrow(6) + vrow(7)
        y_low = y.astype(BF)
        out[rows, :] = y_low
        row = rt * ROWS // length
        ids = seg[pl.ds(row, 1), ds(rt * ROWS % length, ROWS)]
        onehot = (ids == lax.broadcasted_iota(jnp.int32, (SEGS, ROWS), 0)).astype(BF)
        pooled[row] = pooled[row] + (nn(onehot, y_low) + nn(onehot, (y - y_low.astype(F32)).astype(BF)))
        dy = og[rows, :].astype(F32)
        gv[6:7, :] += csum(dy * n2)
        gv[7:8, :] += csum(dy)
        e = dy * vrow(6)
        d = r * (e - rmean(e) - n2 * rmean(e * n2))
        dh2[rows, :] = d
        low = d.astype(BF)
        df[rows, :] = low
        gv[5:6, :] += csum(low.astype(F32))

    loop(tokens // ROWS, down)
    for row in range(seqs):
        onehot = (seg[row : row + 1, :] == lax.broadcasted_iota(jnp.int32, (SEGS, length), 0)).astype(F32)
        pooled[row] = pooled[row] / jnp.sum(onehot, axis=1, keepdims=True)

    def down_grad(cc):
        cs = ds(cc * CHUNK, CHUNK)
        g_down[cs, :] = tn(g[:, cs], df[...]).astype(BF)

    loop(hidden // CHUNK, down_grad)

    def up_back(cc):
        cs = ds(cc * CHUNK, CHUNK)
        total = jnp.zeros((1, CHUNK), F32)
        for rt in range(tokens // ROWS):
            rows = slice(rt * ROWS, (rt + 1) * ROWS)
            du = (nt(df[rows, :], wd[cs, :]) * sl[rows, cs].astype(F32)).astype(BF)
            sl[rows, cs] = du
            total += csum(du.astype(F32))
        gbu[:, cs] = total
        g_up[:, cs] = tn(z_low[...], sl[:, cs]).astype(BF)

    loop(hidden // CHUNK, up_back)

    def first_back(rt):
        rows = ds(rt * ROWS, ROWS)
        dz = dh2[rows, :] + nt(sl[rows, :], wu[...])
        n1 = n1s[rows, :]
        gv[3:4, :] += csum(dz * n1)
        gv[4:5, :] += csum(dz)
        e = dz * vrow(3)
        d = r1s[rows, 0:1] * (e - rmean(e) - n1 * rmean(e * n1))
        dh1[rows, :] = d
        da = d.astype(BF)
        df[rows, :] = da
        gv[2:3, :] += csum(da.astype(F32))
        do[rows, :] = nt(da, wo[...]).astype(BF)

    loop(tokens // ROWS, first_back)

    def out_grad_step(cc):
        cs = ds(cc * (model // 2), model // 2)
        g_out[cs, :] = tn(o[:, cs], df[...]).astype(BF)

    loop(2, out_grad_step)


def qkv_grads(x, dqkv, store):
    model = x.shape[1]
    part = model // 2
    for n, d in enumerate(dqkv):

        def step(t, n=n, d=d):
            store(n, t, tn(x[:, ds(t * part, part, BLOCK)], d[...]).astype(BF))

        loop(2, step)


def token_grads(dh1, dqkv, wa, out):
    model = dh1.shape[1]

    def step(rt):
        rows = ds(rt * ROWS, ROWS)
        total = dh1[rows, :]
        for n, d in enumerate(dqkv):
            total = total + nt(d[rows, :], wa[:, n * model : (n + 1) * model])
        out[rows, :] = total.astype(BF)

    loop(dh1.shape[0] // ROWS, step)


def run_mid(x, o, og, seg, wo, wu, wd, vec, bup):
    tokens, model = x.shape
    hidden = wu.shape[1]
    wide = pltpu.VMEM((tokens, hidden), BF)
    act = sds((tokens, model), BF)
    return pl.pallas_call(
        mid_kernel,
        out_shape=(act, sds((seg.shape[0], SEGS, model), F32), sds(wd.shape, BF), sds(wu.shape, BF), sds(wo.shape, BF),
                   act, sds((tokens, model), F32), sds((8, model), F32), sds((1, hidden), F32)),
        in_specs=[V] * 9,
        out_specs=(V,) * 9,
        scratch_shapes=[pltpu.VMEM((tokens, model), F32), pltpu.VMEM((tokens, BLOCK), F32), pltpu.VMEM((tokens, model), BF),
                        wide, wide, pltpu.VMEM((tokens, model), BF), pltpu.VMEM((tokens, model), F32)],
        compiler_params=params(),
        name="middle",
    )(x, o, og, seg, wo, wu, wd, vec, bup)


def plain_views(length, bias, probs):
    spans, offsets, _ = key_windows(length)

    def rows(held, i):
        return lambda qb: held.at[i, pl.ds(offsets[qb], (spans[qb][1] - spans[qb][0]) * BLOCK)]

    return functools.partial(rows, bias), functools.partial(rows, probs)


def pair_columns(pairs, pair):
    return [ds((part * pairs + pair) * BLOCK, BLOCK) for part in range(3)] + [ds(pair * BLOCK, BLOCK)]


def qkv_kernel(x, wa, vec, seg, qkv, o, probs, bias):
    length, model = seg.shape[1], x.shape[1]
    pairs = model // BLOCK
    bias_of, probs_of = plain_views(length, bias, probs)
    make_bias(seg, lambda row, qb: bias_of(row)(qb))
    for n, row in enumerate((0, None, 1)):
        cs = slice(n * model, (n + 1) * model)

        def project(rt, cs=cs, row=row):
            rows = ds(rt * ROWS, ROWS)
            value = nn(x[rows, :], wa[:, cs])
            qkv[rows, cs] = (value if row is None else value + vec[row : row + 1, :]).astype(BF)

        loop(x.shape[0] // ROWS, project)

    def step(i):
        row = i // pairs
        cq, ck, cv, co = pair_columns(pairs, i % pairs)
        attend_pair(row, length, (qkv, cq), (qkv, ck), (qkv, cv), (o, co), probs_of(i), bias_of(row))

    loop(seg.shape[0] * pairs, step)


def back_kernel(length, qkv_in, do, probs, x, dh1, wa, gtok, g_qkv, gb, qkv, dq, dk_sum, dv_sum):
    model = x.shape[1]
    pairs = model // BLOCK
    qkv[...] = qkv_in[...]
    probs_of = plain_views(length, None, probs)[1]

    def step(i):
        row = i // pairs
        cq, ck, cv, co = pair_columns(pairs, i % pairs)
        attend_back_pair(row, length, (qkv, cq), (qkv, ck), (qkv, cv), (do, co), dq, probs_of(i), dk_sum, dv_sum)

    loop(x.shape[0] // length * pairs, step)
    qkv[:, :model] = dq[...]

    def weight_step(t):
        rows = ds(t * (model // 2), model // 2)
        for n in range(3):
            cs = slice(n * model, (n + 1) * model)
            g_qkv[rows, cs] = tn(x[:, rows], qkv[:, cs]).astype(BF)

    loop(2, weight_step)

    def token_step(rt):
        rows = ds(rt * ROWS, ROWS)
        gtok[rows, :] = (dh1[rows, :] + nt(qkv[rows, :], wa[...])).astype(BF)

    loop(x.shape[0] // ROWS, token_step)
    gb[...] = jnp.concatenate(
        [csum(qkv[:, :model].astype(F32)), csum(qkv[:, 2 * model :].astype(F32)), jnp.zeros((6, model), F32)], axis=0
    )


def local_plain(*args):
    (tokens, segments, w_query, b_query, w_key, w_value, b_value, w_out, b_out, gain1, shift1, w_up, b_up, w_down,
     b_down, gain2, shift2, out_grad) = args
    seqs, length, model = tokens.shape
    count = seqs * length
    band = key_windows(length)[2]
    x = tokens.reshape(count, model)
    og = out_grad.reshape(count, model)

    def gathered(t):
        return lax.all_gather(t, "fsdp", axis=0, tiled=True)

    wa = gathered(jnp.concatenate([w_query, w_key, w_value], axis=1))
    small = gathered(jnp.stack([b_query, b_value, b_out, gain1, shift1, b_down, gain2, shift2], axis=1))
    vec = small.T.astype(F32)
    bup = gathered(b_up).astype(F32)[None]
    wo, wu, wd = gathered(w_out), gathered(w_up), gathered(w_down)
    act = sds((count, model), BF)
    wide = sds((count, 3 * model), BF)
    qkv, o, probs = pl.pallas_call(
        qkv_kernel,
        out_shape=(wide, act, sds((seqs * model // BLOCK, band, 2 * BLOCK), BF)),
        in_specs=[V] * 4,
        out_specs=(V,) * 3,
        scratch_shapes=[pltpu.VMEM((seqs, band, BLOCK), F32)],
        compiler_params=params(),
        name="attention",
    )(x, wa, vec, segments)
    out, pooled, g_down, g_up, g_out, do, dh1, gv, gbu = run_mid(x, o, og, segments, wo, wu, wd, vec, bup)
    part = pltpu.VMEM((length, BLOCK), F32)
    gtok, g_qkv, gb = pl.pallas_call(
        functools.partial(back_kernel, length),
        out_shape=(act, sds((model, 3 * model), BF), sds((8, model), F32)),
        in_specs=[V] * 6,
        out_specs=(V,) * 3,
        scratch_shapes=[pltpu.VMEM((count, 3 * model), BF), pltpu.VMEM((count, model), BF), part, part],
        compiler_params=params(),
        name="attention_back",
    )(qkv, do, probs, x, dh1, wa)
    vectors = jnp.concatenate([gb[:2], gv[2:8]], axis=0).T

    def shared(t):
        mine = lax.psum_scatter(t.astype(F32), "fsdp", scatter_dimension=0, tiled=True)
        return lax.psum(mine.astype(BF), "rep").astype(F32)

    ga, gs = shared(g_qkv), shared(vectors)
    go, gu, gd, gb_up = shared(g_out), shared(g_up), shared(g_down), shared(gbu[0])
    gbq, gbv, gbo, gg1, gs1, gbd, gg2, gs2 = [gs[:, i] for i in range(8)]
    return (
        out.reshape(tokens.shape), pooled, gtok.reshape(tokens.shape),
        ga[:, :model], gbq, ga[:, model : 2 * model], ga[:, 2 * model :], gbv,
        go, gbo, gg1, gs1, gu, gb_up, gd, gbd, gg2, gs2,
    )


def solution(mesh):
    rows = P(("fsdp", "rep"))
    split = P("fsdp")
    placed = (rows, rows) + (split,) * 15 + (rows,)
    results = (rows,) * 3 + (split,) * 15
    owners = mesh.shape["fsdp"]

    def whole(*args):
        shard = args[2].shape[0] // owners
        ring = owners % 8 == 0 and mesh.shape["rep"] == 2 and shard % 16 == 0
        body = functools.partial(local_ring, owners // 4) if ring else local_plain
        return jax.shard_map(body, mesh=mesh, in_specs=placed, out_specs=results, check_vma=False)(*args)

    return whole
```

```python
import functools
import heapq
import math

import jax
import jax.numpy as jnp
from jax import lax
from jax.experimental import pallas as pl
from jax.experimental.pallas import tpu as pltpu
from jax.sharding import PartitionSpec as P

BF = jnp.bfloat16
F32 = jnp.float32
HEAD = 64
SEGS = 8
BLOCK = 128
EPS = 1e-5
MASKED = -1e30
MESH = pl.DeviceIdType.MESH
VMEM_LIMIT = int(63.5 * 2**20)


def nn(a, b):
    return lax.dot_general(a, b, (((1,), (0,)), ((), ())), preferred_element_type=F32)


def nt(a, b):
    return lax.dot_general(a, b, (((1,), (1,)), ((), ())), preferred_element_type=F32)


def tn(a, b):
    return lax.dot_general(a, b, (((0,), (0,)), ((), ())), preferred_element_type=F32)


def rmean(t):
    return jnp.mean(t, axis=-1, keepdims=True)


def csum(t):
    return jnp.sum(t, axis=0, keepdims=True)


def loop(count, step):
    def body(i, carry):
        step(i)
        return carry

    lax.fori_loop(0, count, body, 0)


def ds(start, size, multiple=None):
    if not isinstance(start, int):
        start = pl.multiple_of(start, multiple or size)
    return pl.ds(start, size)


def key_windows(length):
    blocks = length // BLOCK
    spans, offsets, total = [], [], 0
    for qb in range(blocks):
        span = (max(qb - 1, 0), min(qb + 2, blocks))
        spans.append(span)
        offsets.append(total)
        total += (span[1] - span[0]) * BLOCK
    return spans, offsets, total


def stack2(pair):
    lane = lax.broadcasted_iota(jnp.int32, pair.shape, 1)
    zero = jnp.zeros_like(pair)
    return jnp.concatenate(
        [jnp.where(lane < HEAD, pair, zero), jnp.where(lane < HEAD, zero, pair)], axis=0
    )


def unstack_t(both):
    return jnp.concatenate([both[:HEAD, :BLOCK], both[HEAD:, BLOCK:]], axis=0).T


def make_bias(seg, bias_at):
    rows, length = seg.shape
    spans, _, _ = key_windows(length)
    for row in range(rows):
        ids = seg[row : row + 1, :].astype(F32)
        keys = jnp.broadcast_to(ids, (BLOCK, length)).T
        for qb, (k0, k1) in enumerate(spans):
            same = keys[k0 * BLOCK : k1 * BLOCK, :] == ids[:, qb * BLOCK : (qb + 1) * BLOCK]
            bias_at(row, qb)[...] = jnp.where(same, 0.0, MASKED)


def attend_pair(row, length, q, k, v, o, probs_at, bias_at):
    spans, _, _ = key_windows(length)
    (q, cq), (k, ck), (v, cv), (o, co) = q, k, v, o
    r0 = pl.multiple_of(row * length, length)
    vt = v[pl.ds(r0, length), cv].T
    for qb, (k0, k1) in enumerate(spans):
        n = (k1 - k0) * BLOCK
        mine = pl.ds(r0 + qb * BLOCK, BLOCK)
        q2 = stack2(q[mine, cq] * BF(HEAD**-0.5))
        s = nt(k[pl.ds(r0 + k0 * BLOCK, n), ck], q2)
        b = bias_at(qb)[...]
        s = s + jnp.concatenate([b, b], axis=1)
        e = jnp.exp(s - jnp.max(s, axis=0, keepdims=True))
        p = (e * (1.0 / jnp.sum(e, axis=0, keepdims=True))).astype(BF)
        probs_at(qb)[...] = p
        o[mine, co] = unstack_t(nn(vt[:, k0 * BLOCK : k1 * BLOCK], p)).astype(BF)


def attend_back_pair(row, length, q, k, v, do, dq, probs_at, dk_sum, dv_sum):
    spans, _, _ = key_windows(length)
    last = len(spans) - 1
    (q, cq), (k, ck), (v, cv), (do, co) = q, k, v, do
    r0 = pl.multiple_of(row * length, length)
    kt = k[pl.ds(r0, length), ck].T
    for qb, (k0, k1) in enumerate(spans):
        n = (k1 - k0) * BLOCK
        mine = pl.ds(r0 + qb * BLOCK, BLOCK)
        q2 = stack2(q[mine, cq] * BF(HEAD**-0.5))
        do2 = stack2(do[mine, co])
        dp = nt(v[pl.ds(r0 + k0 * BLOCK, n), cv], do2)
        low = probs_at(qb)[...]
        p = low.astype(F32)
        d_s = (p * (dp - jnp.sum(p * dp, axis=0, keepdims=True))).astype(BF)
        dv_part = nn(low, do2)
        dk_part = nn(d_s, q2)
        for kb in range(k0, k1):
            part = slice((kb - k0) * BLOCK, (kb - k0 + 1) * BLOCK)
            held = slice(kb * BLOCK, (kb + 1) * BLOCK)
            a, b = dv_part[part], dk_part[part]
            if qb != max(kb - 1, 0):
                a, b = a + dv_sum[held, :], b + dk_sum[held, :]
            if qb == min(kb + 1, last):
                there = pl.ds(r0 + kb * BLOCK, BLOCK)
                v[there, cv] = a.astype(BF)
                k[there, ck] = b.astype(BF)
            else:
                dv_sum[held, :] = a
                dk_sum[held, :] = b
        dqt = nn(kt[:, k0 * BLOCK : k1 * BLOCK], d_s)
        dq[mine, co] = (unstack_t(dqt) * HEAD**-0.5).astype(BF)


class Place:
    def __init__(self, depth):
        self.depth = depth
        self.f = lax.axis_index("fsdp")
        self.y = lax.axis_index("rep")
        self.c = self.f % 2
        self.x = self.f // 2 % 2
        self.z = self.f // 4
        self.sib = (self.f + 1 - 2 * self.c, self.y)
        self.xn = (self.f + 2 - 4 * self.x, self.y)
        self.yn = (self.f, 1 - self.y)
        self.up = (self.f + 4, self.y)
        self.down = (self.f - 4, self.y)

    def barrier(self):
        sem = pltpu.get_barrier_semaphore()
        for who in (self.sib, self.xn, self.yn):
            pl.semaphore_signal(sem, inc=1, device_id=who, device_id_type=MESH)

        @pl.when(self.z > 0)
        def _():
            pl.semaphore_signal(sem, inc=1, device_id=self.down, device_id_type=MESH)

        @pl.when(self.z < self.depth - 1)
        def _():
            pl.semaphore_signal(sem, inc=1, device_id=self.up, device_id_type=MESH)

        inner = (self.z > 0).astype(jnp.int32) + (self.z < self.depth - 1).astype(jnp.int32)
        pl.semaphore_wait(sem, 3 + inner)


def remote(src, dst, send, recv, who):
    return pltpu.make_async_remote_copy(
        src_ref=src, dst_ref=dst, send_sem=send, recv_sem=recv, device_id=who, device_id_type=MESH
    )


def gather_sems(groups, depth):
    return [
        pltpu.SemaphoreType.DMA((groups, 2, depth - 1)),
        pltpu.SemaphoreType.DMA((groups, depth)),
        pltpu.SemaphoreType.DMA((groups, depth)),
        pltpu.SemaphoreType.DMA((groups, depth + 1)),
        pltpu.SemaphoreType.DMA((groups, depth)),
    ] * 2 + [pltpu.SemaphoreType.DMA((groups,))]


class Gather:
    def __init__(self, place, g, shard, whole, sems, halved=False):
        self.p, self.g, self.shard, self.whole = place, g, shard, whole
        self.halved = halved
        self.sz, self.sx, self.sy, self.sc, self.so, self.rz, self.rx, self.ry, self.rc, self.ro, self.own = sems
        self.rows, self.cols = whole.shape[3:]
        self.done = False

    def piece(self, z, x, half=None):
        return self.piece_of(z, x, self.p.c, half)

    def piece_of(self, z, x, c, half=None):
        if half is None:
            return self.whole.at[z, x, c]
        return self.whole.at[z, x, c, :, ds(half * (self.cols // 2), self.cols // 2)]

    def copy_z(self, direction, distance, z, src=None):
        dst = self.piece(z, self.p.x, self.p.y if self.halved else None)
        return remote(
            dst if src is None else src,
            dst,
            self.sz.at[self.g, direction, distance],
            self.rz.at[self.g, direction, distance],
            self.p.up if direction == 0 else self.p.down,
        )

    def copy_x(self, z, src=None):
        dst = self.piece(z, self.p.x, self.p.y)
        return remote(dst if src is None else src, dst, self.sx.at[self.g, z], self.rx.at[self.g, z], self.p.xn)

    def copy_y(self, z):
        at = self.piece(z, 1 - self.p.x, self.p.y)
        return remote(at, at, self.sy.at[self.g, z], self.ry.at[self.g, z], self.p.yn)

    def copy_c(self, z, src=None):
        dst = self.piece(z, self.p.x)
        return remote(dst if src is None else src, dst, self.sc.at[self.g, z], self.rc.at[self.g, z], self.p.sib)

    def copy_o(self, z):
        at = self.piece(z, self.p.x, self.p.y)
        return remote(at, at, self.so.at[self.g, z], self.ro.at[self.g, z], self.p.yn)

    def o_step(self, k):
        def act(z):
            at = self.piece(z, self.p.x, 1 - self.p.y)
            remote(at, at, self.so.at[self.g, z], self.ro.at[self.g, z], self.p.yn).wait_recv()
            self.copy_c(z).start()

        self.at_distance(k, act)

    def copy_column(self):
        at = self.whole.at[:, 1 - self.p.x, self.p.c]
        n = self.p.depth
        return remote(at, at, self.sc.at[self.g, n], self.rc.at[self.g, n], self.p.sib)

    def local(self):
        return pltpu.make_async_copy(self.shard, self.piece(self.p.z, self.p.x), self.own.at[self.g])

    def z_step(self, k):
        p = self.p
        if k == 0:
            if self.shard is None:
                shard, half = self.piece(p.z, p.x), self.piece(p.z, p.x, p.y)
            else:
                self.local().start()
                shard, half = self.shard, self.shard.at[:, ds(p.y * (self.cols // 2), self.cols // 2)]
            mine = half if self.halved else shard

            @pl.when(p.z < p.depth - 1)
            def _():
                self.copy_z(0, 0, p.z, mine).start()

            @pl.when(p.z > 0)
            def _():
                self.copy_z(1, 0, p.z, mine).start()

            self.copy_x(p.z, half).start()
            self.copy_c(p.z, shard).start()
            return

        for direction in (0, 1):
            z = p.z - k if direction == 0 else p.z + k

            @pl.when(z >= 0 if direction == 0 else z < p.depth)
            def _(direction=direction, z=z):
                self.copy_z(direction, k - 1, z).wait_recv()
                if k < p.depth - 1:

                    @pl.when(p.z < p.depth - 1 if direction == 0 else p.z > 0)
                    def _():
                        self.copy_z(direction, k, z).start()

                self.copy_x(z).start()
                if self.halved:
                    self.copy_o(z).start()
                else:
                    self.copy_c(z).start()

    def at_distance(self, k, act):
        p = self.p
        if k == 0:
            act(p.z)
            return

        @pl.when(p.z - k >= 0)
        def _():
            act(p.z - k)

        @pl.when(p.z + k < p.depth)
        def _():
            act(p.z + k)

    def x_step(self, k):
        def act(z):
            self.copy_x_in(z).wait_recv()
            self.copy_y(z).start()

        self.at_distance(k, act)

    def copy_x_in(self, z):
        at = self.piece(z, 1 - self.p.x, self.p.y)
        return remote(at, at, self.sx.at[self.g, z], self.rx.at[self.g, z], self.p.xn)

    def copy_y_in(self, z):
        at = self.piece(z, 1 - self.p.x, 1 - self.p.y)
        return remote(at, at, self.sy.at[self.g, z], self.ry.at[self.g, z], self.p.yn)

    def y_step(self, k):
        def act(z):
            self.copy_y_in(z).wait_recv()

        self.at_distance(k, act)
        if k == self.p.depth - 1:
            self.copy_column().start()

    def c_step(self):
        self.done = True
        if self.shard is not None:
            self.local().wait()
        p, n = self.p, self.p.depth
        for z in range(n):
            at = self.whole.at[z, p.x, 1 - p.c]
            remote(at, at, self.sc.at[self.g, z], self.rc.at[self.g, z], p.sib).wait_recv()
        at = self.whole.at[:, 1 - p.x, 1 - p.c]
        remote(at, at, self.sc.at[self.g, n], self.rc.at[self.g, n], p.sib).wait_recv()

    def end(self):
        p = self.p
        for k in range(p.depth - 1):
            @pl.when((p.z < p.depth - 1) & (p.z - k >= 0))
            def _():
                self.copy_z(0, k, p.z - k).wait_send()

            @pl.when((p.z > 0) & (p.z + k < p.depth))
            def _():
                self.copy_z(1, k, p.z + k).wait_send()

        for z in range(p.depth):
            self.copy_x(z).wait_send()
            self.copy_y(z).wait_send()
            self.copy_c(z).wait_send()
            if self.halved:

                @pl.when(p.z != z)
                def _(z=z):
                    self.copy_o(z).wait_send()

        self.copy_column().wait_send()


def scatter_sems(groups, depth):
    kinds = [(groups, 2, depth), (groups,), (groups,), (groups, 2, depth - 1), (groups,)]
    return [pltpu.SemaphoreType.DMA(k) for k in kinds] * 2 + [pltpu.SemaphoreType.DMA((groups, 5))]


def scatter_buffers(rows, cols, depth):
    return [
        pltpu.VMEM((2, depth, rows, cols), BF),
        pltpu.VMEM((depth, rows, cols // 2), BF),
        pltpu.VMEM((depth, rows, cols // 2), BF),
        pltpu.VMEM((2 * depth - 3, rows, cols), BF),
        pltpu.VMEM((rows, cols), BF),
    ]


def scatter_half_buffers(rows, cols, depth):
    return [
        pltpu.VMEM((2, depth, rows, cols), BF),
        pltpu.VMEM((depth, rows, cols // 2), BF),
        pltpu.VMEM((depth, rows, cols), BF),
        pltpu.VMEM((2 * depth - 3, rows, cols // 2), BF),
        pltpu.VMEM((rows, cols // 2), BF),
    ]


def add_into(depth, rows, target, other):
    piece = min(rows, 48)
    parts = rows // piece

    def step(i):
        z, at = i // parts, ds(i % parts * piece, piece, 16)
        t = target(z, at)
        t[...] = t[...] + other(z, at)[...]

    loop(depth * parts, step)


class Scatter:
    first, second, along, last = ("y", 2), ("x", 2), 1.0, 1.0
    pieces = False

    def __init__(self, place, g, grad, landing, buffers, sems):
        self.p, self.g, self.grad, self.landing = place, g, grad, landing
        self.in_c, self.in_y, self.in_x, self.in_z, self.in_f = buffers
        (self.sc, self.sy, self.sx, self.sz, self.sf, self.rc, self.ry, self.rx, self.rz, self.rf, self.out) = sems
        _, self.depth, self.rows, self.cols = self.in_c.shape

    def half(self, h):
        return ds(h * (self.cols // 2), self.cols // 2)

    def copy_c(self, x):
        p = self.p
        return remote(
            self.grad.at[:, x, 1 - p.c], self.in_c.at[x], self.sc.at[self.g, x, 0], self.rc.at[self.g, x, 0], p.sib
        )

    def copy_piece(self, z, x):
        p = self.p
        return remote(
            self.grad.at[z, x, 1 - p.c], self.in_c.at[x, z], self.sc.at[self.g, x, z], self.rc.at[self.g, x, z], p.sib
        )

    def copies_c(self, x):
        return [self.copy_piece(z, x) for z in range(self.depth)] if self.pieces else [self.copy_c(x)]

    def copy_y(self):
        p = self.p
        return remote(
            self.grad.at[:, 1 - p.x, p.c, :, self.half(1 - p.y)], self.in_y, self.sy.at[self.g], self.ry.at[self.g], p.yn
        )

    def copy_x(self):
        p = self.p
        return remote(
            self.grad.at[:, 1 - p.x, p.c, :, self.half(p.y)], self.in_x, self.sx.at[self.g], self.rx.at[self.g], p.xn
        )

    def line_slot(self, direction, slot):
        far = self.depth - 2
        return 2 * far if slot == far else 2 * slot + direction

    def copy_z(self, direction, z, slot):
        p = self.p
        return remote(
            self.line_piece(z),
            self.in_z.at[self.line_slot(direction, slot)],
            self.sz.at[self.g, direction, slot],
            self.rz.at[self.g, direction, slot],
            p.up if direction == 0 else p.down,
        )

    def copy_f(self):
        p = self.p
        return remote(self.grad.at[p.z, p.x, p.c], self.in_f, self.sf.at[self.g], self.rf.at[self.g], p.yn)

    def receive(self):
        self.copy_f().wait_recv()

    def end_y(self):
        self.copy_y().wait_send()

    def begin(self):
        self.copy_c(1 - self.p.x).start()
        self.copy_c(self.p.x).start()

    def cores(self, turn):
        p = self.p
        x = 1 - p.x if turn == 0 else p.x
        for copy in self.copies_c(x):
            copy.wait_recv()
        add_into(
            self.depth,
            self.rows,
            lambda z, at: self.grad.at[z, x, p.c, at],
            lambda z, at: self.in_c.at[x, z, at],
        )
        if turn == 0:
            self.begin_exchange()

    def begin_exchange(self):
        self.copy_y().start()

    def line_piece(self, z):
        return self.grad.at[z, self.p.x, self.p.c]

    def over_y(self):
        p = self.p
        self.copy_y().wait_recv()
        add_into(
            self.depth,
            self.rows,
            lambda z, at: self.grad.at[z, 1 - p.x, p.c, at, self.half(p.y)],
            lambda z, at: self.in_y.at[z, at],
        )
        self.copy_x().start()

    def over_x(self):
        p = self.p
        self.copy_x().wait_recv()
        add_into(
            self.depth,
            self.rows,
            lambda z, at: self.grad.at[z, p.x, p.c, at, self.half(p.y)],
            lambda z, at: self.in_x.at[z, at],
        )

    def line(self, wave):
        p, top = self.p, self.depth - 1
        for direction in (0, 1):
            place = p.z if direction == 0 else top - p.z
            if wave == 0:

                @pl.when(place == 0)
                def _(direction=direction):
                    for far in range(top, 0, -1):
                        self.copy_z(direction, far if direction == 0 else top - far, far - 1).start()

                continue

            @pl.when((place >= 1) & (place <= wave))
            def _(direction=direction, place=place):
                far = top - wave + place
                z = far if direction == 0 else top - far
                slot = top - wave
                self.copy_z(direction, z, slot).wait_recv()
                add_into(
                    1,
                    self.rows,
                    lambda _, at: self.line_piece(z).at[at],
                    lambda _, at: self.in_z.at[self.line_slot(direction, slot), at],
                )
                if slot > 0:
                    self.copy_z(direction, z, slot - 1).start()

    def share(self):
        self.copy_f().start()

    def copy_out(self, n):
        _, view, result = self.landing[n]
        return pltpu.make_async_copy(view, result, self.out.at[self.g, n])

    def finish(self):
        p = self.p
        self.receive()
        piece = min(self.rows, 48)
        c0 = 0
        for n, (cols, view, result) in enumerate(self.landing):
            if view is None:
                c0 += cols
                continue

            def step(i, view=view, c0=c0, cols=cols):
                at = ds(i * piece, piece, 16)
                cs = pl.ds(c0, cols)
                view[at, :] = self.total(at, cs)

            loop(self.rows // piece, step)
            if result is not None:
                self.copy_out(n).start()
            c0 += cols

    def total(self, at, cs):
        p = self.p
        return self.grad[p.z, p.x, p.c, at, cs].astype(F32) + self.in_f[at, cs].astype(F32)

    def end(self):
        p, top = self.p, self.depth - 1
        for x in (0, 1):
            for copy in self.copies_c(x):
                copy.wait_send()
        self.end_y()
        self.copy_x().wait_send()
        for direction in (0, 1):
            place = p.z if direction == 0 else top - p.z
            for slot in range(top):

                @pl.when(place + slot < top)
                def _(direction=direction, slot=slot):
                    self.copy_z(direction, 0, slot).wait_send()

        self.copy_f().wait_send()
        for n, (_, _, result) in enumerate(self.landing):
            if result is not None:
                self.copy_out(n).wait()

    def exchanges(self):
        return [self.over_y, self.over_x]

    def steps(self):
        one, two = self.exchanges()

        def two_and_line():
            two()
            self.line(0)

        out = [lambda: self.cores(0), lambda: self.cores(1), one, two_and_line]
        for wave in range(1, self.depth):
            out.append(functools.partial(self.line, wave))
        return out + [self.share, self.finish]


class HalfScatter(Scatter):
    first, second, along, last = ("x", 4), ("y", 2), 0.5, 0.5

    def copy_x(self):
        p = self.p
        return remote(self.grad.at[:, 1 - p.x, p.c], self.in_x, self.sx.at[self.g], self.rx.at[self.g], p.xn)

    def copy_y(self):
        p = self.p
        return remote(
            self.grad.at[:, p.x, p.c, :, self.half(1 - p.y)], self.in_y, self.sy.at[self.g], self.ry.at[self.g], p.yn
        )

    def begin_exchange(self):
        self.copy_x().start()

    def exchanges(self):
        return [self.over_x, self.over_y]

    def over_x(self):
        p = self.p
        self.copy_x().wait_recv()
        add_into(
            self.depth,
            self.rows,
            lambda z, at: self.grad.at[z, p.x, p.c, at],
            lambda z, at: self.in_x.at[z, at],
        )
        self.copy_y().start()

    def over_y(self):
        p = self.p
        self.copy_y().wait_recv()
        add_into(
            self.depth,
            self.rows,
            lambda z, at: self.line_piece(z).at[at],
            lambda z, at: self.in_y.at[z, at],
        )

    def line_piece(self, z):
        return self.grad.at[z, self.p.x, self.p.c, :, self.half(self.p.y)]

    def copy_f(self):
        return remote(self.line_piece(self.p.z), self.in_f, self.sf.at[self.g], self.rf.at[self.g], self.p.yn)

    def receive(self):
        p = self.p
        self.copy_f().wait_recv()
        self.copy_y().wait_send()
        self.grad[p.z, p.x, p.c, :, self.half(1 - p.y)] = self.in_f[...]

    def end_y(self):
        pass

    def total(self, at, cs):
        p = self.p
        return self.grad[p.z, p.x, p.c, at, cs].astype(F32)


def spread(place, owners_rows, parts):
    width = place.shape[0]
    row = lax.broadcasted_iota(jnp.int32, (width, 1), 0)
    target = row
    for owner in range(1, width // owners_rows):
        target = target + jnp.where(row >= owner * owners_rows, (parts - 1) * owners_rows, 0)
    lane = lax.broadcasted_iota(jnp.int32, (width, width * parts), 1)
    place[...] = (lane == target).astype(BF)


def unpack_small(columns, shard, parts, vec, bup, room):
    rows = columns.astype(F32).T
    vec[...] = rows[:8, :]
    low = rows[8:16, :].astype(BF)
    width = 8 * shard
    place = room.at[:width, : width * parts]
    spread(place, shard, parts)
    for t in range(columns.shape[0] // width):
        wide = nn(low[:, t * width : (t + 1) * width], place[...])
        total = wide[0:1]
        for i in range(1, parts):
            total = total + pltpu.roll(wide, i * shard, 1)[i : i + 1]
        bup[:, t * width * parts : (t + 1) * width * parts] = total


def pack_small(gv, gbu, shard, parts, room):
    width = 8 * shard
    wide = width * parts
    model = gv.shape[1]
    place = room.at[:width, :wide]
    spread(place, shard, parts)
    columns = jnp.concatenate([gv, jnp.zeros((BLOCK - 8, model), F32)], axis=0).T
    found = []
    for t in range(model // width):
        piece = jnp.broadcast_to(gbu[:, t * wide : (t + 1) * wide], (8, wide))
        rows = [jnp.zeros((8, wide), F32)]
        for i in range(parts):
            rows.append((pltpu.roll(piece, wide - i * shard, 1) if i else piece)[0:1])
        rows.append(jnp.zeros((BLOCK - 8 - parts, wide), F32))
        found.append(nt(place[...], jnp.concatenate(rows, axis=0).astype(BF)))
    return (columns + jnp.concatenate(found, axis=0)).astype(BF)


ROWS = 256
CHUNK = 512


def phi_parts(u):
    cdf = 0.5 * (1.0 + lax.erf(u * math.sqrt(0.5)))
    pdf = jnp.exp(-0.5 * u * u) * (1.0 / math.sqrt(2.0 * math.pi))
    return cdf, pdf


V = pl.BlockSpec(memory_space=pltpu.VMEM)
ANY = pl.BlockSpec(memory_space=pl.ANY)
sds = jax.ShapeDtypeStruct


def params(collective_id=None):
    if collective_id is None:
        return pltpu.CompilerParams(vmem_limit_bytes=VMEM_LIMIT)
    return pltpu.CompilerParams(
        vmem_limit_bytes=VMEM_LIMIT, collective_id=collective_id, has_side_effects=True
    )


class Links:
    core_rate = 350.0

    def __init__(self):
        self.free = dict.fromkeys("cxyz", 0.0)
        self.heap = []
        self.count = 0
        self.rate, self.lag = GATHER

    def send(self, link, at, size):
        rate = self.core_rate if link == "c" else self.rate
        self.free[link] = max(at, self.free[link]) + size / rate * 1e-3
        return self.free[link] + self.lag

    def push(self, at, task, then=None):
        self.count += 1
        heapq.heappush(self.heap, (at, self.count, task, then))

    def gather(self, gather, at):
        size = gather.rows * gather.cols * 2
        part = size / 2 if gather.halved else size
        depth = gather.p.depth

        def zed(k):
            def then(now):
                if k < depth - 1:
                    self.push(self.send("z", now, part), lambda: gather.z_step(k + 1), zed(k + 1))
                self.push(self.send("x", now, size / 2), lambda: gather.x_step(k), ex(k))
                if k and gather.halved:
                    self.push(self.send("y", now, size / 2), lambda: gather.o_step(k))

            return then

        def ex(k):
            return lambda now: self.push(
                self.send("y", now, size / 2), lambda: gather.y_step(k), lambda now: None if k < depth - 1
                else self.push(now + 2.0, gather.c_step)
            )

        self.push(at, lambda: gather.z_step(0), zed(0))

    def scatter(self, scatter, at):
        size = scatter.rows * scatter.cols * 2
        steps = scatter.steps()
        last = len(steps) - 1

        def after(n):
            def then(now):
                now = now + 0.3
                if n == 0:
                    link, count = scatter.first
                    self.push(self.send(link, now, count * size), steps[2], after(2))
                elif n == 2:
                    link, count = scatter.second
                    self.push(self.send(link, now, count * size), steps[3], after(3))
                elif 3 <= n < last - 2:
                    self.push(self.send("z", now, scatter.along * size), steps[n + 1], after(n + 1))
                elif n == last - 2:
                    self.push(now, steps[last - 1], after(last - 1))
                elif n == last - 1:
                    self.push(self.send("y", now, scatter.last * size), steps[last])

            return then

        part = 0 if scatter.pieces else 4
        self.push(self.send("c", at, part * size), steps[0], after(0))
        self.push(self.send("c", at, part * size), steps[1])

    def due(self, now):
        found = []
        while self.heap and self.heap[0][0] <= now:
            at, _, task, then = heapq.heappop(self.heap)
            found.append(task)
            if then:
                then(at)
        return found

    def all(self):
        return self.due(float("inf"))

    def next(self):
        return self.heap[0][0]


class Clock:
    def __init__(self, links):
        self.links, self.now = links, 0.0

    def run(self, tasks):
        for task in tasks:
            task()

    def spend(self, time):
        self.now += time
        self.run(self.links.due(self.now))

    def until(self, gather):
        while not gather.done:
            self.now = max(self.now, self.links.next())
            self.run(self.links.due(self.now))

    def loop(self, count, step, time):
        ticks = []
        for _ in range(count):
            self.now += time
            ticks.append(self.links.due(self.now))

        def body(i):
            step(i)
            for n, tasks in enumerate(ticks):
                if tasks:

                    @pl.when(i == n)
                    def _(tasks=tasks):
                        self.run(tasks)

        loop(count, body)


def head_groups(pairs):
    few = pairs // 3
    return [(0, few), (few, pairs - few)]


def group_columns(pairs):
    groups = head_groups(pairs)
    blank = 2 * BLOCK
    return [(0, blank), (3 * groups[0][1] * BLOCK + blank, 0)]


LIGHT = ("o", 0, 1)


def column_cuts(model):
    third = model // 3
    return [(0, third), (third, model - third)]


def layer_kernel(depth, parts, cuts, *refs):
    it = iter(refs)

    def take(n):
        return [next(it) for _ in range(n)]

    x_in, seg, sq, sk, sv, small_in, so, su, sd, og_in = take(10)
    out, pooled, gtok, gq, gk, gv_w, go_w, gu_w, gd_w, small, p_main, p_last = take(12)
    x, q, k, v, o, z_low, df, n1s, dh, r1s, g, sl, stage = take(13)
    wa, wo, wu, wd, gv, gbu, vec, bup = take(8)
    sets = [take(5) for _ in cuts]
    gsems, ssems, msem, osem, psem, asem = take(11), take(11), *take(4)

    seqs, length = seg.shape
    tokens, model = x.shape
    hidden = g.shape[1]
    dk_sum, dv_sum = r1s.at[:length], r1s.at[length : 2 * length]
    shard = so.shape[0]
    pairs = model // BLOCK
    spans, offsets, _ = key_windows(length)
    final = len(spans) - 1
    tiles = tokens // ROWS

    def span_rows(qb):
        return (spans[qb][1] - spans[qb][0]) * BLOCK

    def bias_at(row, qb):
        at = 0 if qb == final else offsets[qb]
        lane = (row * 2 + (1 if qb == final else 0)) * BLOCK
        return dh.at[at : at + span_rows(qb), ds(lane, BLOCK)]

    def probs_of(i):
        def at(qb):
            held, at = (sl, 0) if qb == final else (g, offsets[qb])
            return held.at[at : at + span_rows(qb), ds(i * 2 * BLOCK, 2 * BLOCK)]

        return at

    groups = head_groups(pairs)
    packed = group_columns(pairs)

    def group_span(n):
        first, size = groups[n]
        return slice(first * BLOCK, (first + size) * BLOCK)

    def weight_span(n, part):
        width = groups[n][1] * BLOCK
        return slice(packed[n][0] + part * width, packed[n][0] + (part + 1) * width)

    def weight_of(span):
        return wa[:, :, :, :, span].reshape(model, span.stop - span.start)

    place = Place(depth)
    links = Links()
    clock = Clock(links)
    loads = [pltpu.make_async_copy(x_in, x, msem.at[0]), pltpu.make_async_copy(og_in, df, msem.at[1])]
    mine = wa.at[place.z, place.x, place.c]
    packs = [pltpu.make_async_copy(small_in, mine.at[:, 3 * groups[0][1] * BLOCK : packed[1][0]], asem.at[0])]
    for n in range(len(groups)):
        for part, source in enumerate((sq, sk, sv)):
            there = mine.at[:, weight_span(n, part)]
            packs.append(pltpu.make_async_copy(source.at[:, group_span(n)], there, asem.at[len(packs)]))
    for load in packs + loads:
        load.start()
    early = packed[1][0]
    sources = (
        (None, wa.at[:, :, :, :, :early]),
        (None, wa.at[:, :, :, :, early:]),
        (so, wo), (su, wu), (sd, wd),
    )
    gathers = [Gather(place, n, s, w, gsems, n in HALVED) for n, (s, w) in enumerate(sources)]
    for gather, at in zip(gathers, BEGINS):
        links.gather(gather, at)
    for load in packs:
        load.wait()
    place.barrier()
    clock.spend(1.0)
    make_bias(seg, bias_at)
    loads[0].wait()
    clock.until(gathers[0])
    at = packed[0][0] + 3 * groups[0][1] * BLOCK
    unpack_small(wa[:, :, :, :, at : at + BLOCK].reshape(model, BLOCK), shard, parts, vec, bup, g)

    def vrow(i):
        return vec[i : i + 1, :]

    def project(n):
        here = group_span(n)

        def step(rt):
            rows = ds(rt * ROWS, ROWS)
            for part, (to, bias) in enumerate(((q, 0), (k, None), (v, 1))):
                value = nn(x[rows, :], weight_of(weight_span(n, part)))
                to[rows, here] = (value if bias is None else value + vec[bias : bias + 1, here]).astype(BF)

        clock.loop(tiles, step, 0.25 * groups[n][1])

    def copy_probs(i, which, back=False):
        lanes = ds(i * 2 * BLOCK, 2 * BLOCK)
        here = g.at[:, lanes] if which == 0 else sl.at[: span_rows(final), lanes]
        there = (p_main if which == 0 else p_last).at[:, lanes]
        return pltpu.make_async_copy(here, there, psem.at[which, i])

    def attend(n):
        first, size = groups[n]

        def step(j):
            row, local = j // size, j % size
            i = row * pairs + first + local
            c = ds((first + local) * BLOCK, BLOCK)
            attend_pair(row, length, (q, c), (k, c), (v, c), (o, c), probs_of(i), functools.partial(bias_at, row))
            copy_probs(i, 0).start()
            copy_probs(i, 1).start()

        clock.loop(seqs * size, step, ATTEND)

    for n in range(len(groups)):
        clock.until(gathers[min(n, 1)])
        project(n)
        attend(n)
    for i in range(seqs * pairs):
        copy_probs(i, 0).wait()
        copy_probs(i, 1).wait()

    chunks = hidden // CHUNK

    def up(i):
        rows = ds(i // chunks * ROWS, ROWS)

        @pl.when(i % chunks == 0)
        def _():
            h = x[rows, :].astype(F32) + (nn(o[rows, :], wo[...].reshape(model, model)) + vrow(2))
            c = h - rmean(h)
            r = lax.rsqrt(rmean(c * c) + EPS)
            n = c * r
            n1s[rows, :] = n
            r1s[rows, :] = jnp.broadcast_to(r, (ROWS, BLOCK))
            z_low[rows, :] = (n * vrow(3) + vrow(4)).astype(BF)

        cs = ds(i % chunks * CHUNK, CHUNK)
        u = nn(z_low[rows, :], wu[:, :, :, :, cs].reshape(model, CHUNK)) + bup[:, cs]
        cdf, pdf = phi_parts(u)
        g[rows, cs] = (u * cdf).astype(BF)
        sl[rows, cs] = (cdf + u * pdf).astype(BF)

    clock.until(gathers[2])
    clock.until(gathers[3])
    clock.loop(tiles * chunks, up, 22.0 / (tiles * chunks))
    clock.until(gathers[4])
    for gather in gathers:
        gather.end()
    loads[1].wait()
    gv[...] = jnp.zeros_like(gv)
    pooled[...] = jnp.zeros_like(pooled)

    def copy_tile(rt):
        return pltpu.make_async_copy(stage, out.at[ds(rt * ROWS, ROWS)], osem.at[0])

    def down(rt):
        rows = ds(rt * ROWS, ROWS)
        h = (n1s[rows, :] * vrow(3) + vrow(4)) + (nn(g[rows, :], wd[...].reshape(hidden, model)) + vrow(5))
        c = h - rmean(h)
        r = lax.rsqrt(rmean(c * c) + EPS)
        n2 = c * r
        y = n2 * vrow(6) + vrow(7)
        y_low = y.astype(BF)

        @pl.when(rt > 0)
        def _():
            copy_tile(rt - 1).wait()

        stage[...] = y_low
        copy_tile(rt).start()
        row = rt * ROWS // length
        ids = seg[pl.ds(row, 1), ds(rt * ROWS % length, ROWS)]
        onehot = (ids == lax.broadcasted_iota(jnp.int32, (SEGS, ROWS), 0)).astype(BF)
        pooled[row] = pooled[row] + (nn(onehot, y_low) + nn(onehot, (y - y_low.astype(F32)).astype(BF)))
        dy = df[rows, :].astype(F32)
        gv[6:7, :] += csum(dy * n2)
        gv[7:8, :] += csum(dy)
        e = dy * vrow(6)
        d = r * (e - rmean(e) - n2 * rmean(e * n2))
        dh[rows, :] = d
        low = d.astype(BF)
        df[rows, :] = low
        gv[5:6, :] += csum(low.astype(F32))

    clock.loop(tiles, down, 3.0)
    copy_tile(tiles - 1).wait()
    for row in range(seqs):
        onehot = (seg[row : row + 1, :] == lax.broadcasted_iota(jnp.int32, (SEGS, length), 0)).astype(F32)
        pooled[row] = pooled[row] / jnp.sum(onehot, axis=1, keepdims=True)

    base = {}
    at = 0
    for name, rows in (("d", sd.shape[0]), ("o", shard), ("u", shard * (hidden // model)), ("q", shard), ("k", shard),
                       ("v", shard), ("small", shard)):
        base[name] = at
        at += rows
    results = {"d": gd_w, "o": go_w, "u": gu_w, "q": gq, "k": gk, "v": gv_w}
    weights = {"d": wd, "o": wo, "u": wu}
    scatters = {}
    for n, (name, r0, rows, c0, cols) in enumerate(cuts):
        landing = []
        if isinstance(name, int):
            first, size = groups[name]
            cs = slice(first * BLOCK, (first + size) * BLOCK)
            spans_of = [(weight, cs.start + at, part * size * BLOCK + at) for part, weight in enumerate("qkv")
                        for at in range(0, size * BLOCK, 2 * BLOCK)]
            for weight, to, at in spans_of:
                if c0 <= at < c0 + cols:
                    ends = slice(to, to + 2 * BLOCK)
                    landing.append((2 * BLOCK, n1s.at[base[weight] : base[weight] + shard, ends], results[weight].at[:, ends]))
            if packed[name][1] and c0 + cols > 3 * size * BLOCK:
                landing.append((BLOCK, n1s.at[base["small"] : base["small"] + shard, :BLOCK], None))
            grad = wa.at[:, :, :, :, packed[name][0] + c0 : packed[name][0] + c0 + cols]
        else:
            for c in range(c0, c0 + cols, model):
                top = base[name] + c // model * shard + r0
                width = min(model, c0 + cols - c)
                at = c % model
                landing.append((width, n1s.at[top : top + rows, at : at + width],
                                results[name].at[r0 : r0 + rows, c : c + width]))
            grad = weights[name].at[:, :, :, r0 : r0 + rows, c0 : c0 + cols]
        kind = HalfScatter if name in LIGHT else Scatter
        scatters.setdefault(name, []).append(kind(place, n, grad, landing, sets[n], ssems))

    for s in scatters["d"]:
        s.pieces = True
    pair_rows = 2 * sd.shape[0]

    def up_back(cc):
        cs = ds(cc * pair_rows, pair_rows, BLOCK)
        weight = wd[cc // 2, cc % 2].reshape(pair_rows, model)
        total = jnp.zeros((1, pair_rows), F32)
        for rt in range(tiles):
            rows = slice(rt * ROWS, (rt + 1) * ROWS)
            du = (nt(df[rows, :], weight) * sl[rows, cs].astype(F32)).astype(BF)
            sl[rows, cs] = du
            total += csum(du.astype(F32))
        gbu[:, cs] = total
        wd[cc // 2, cc % 2] = tn(g[:, cs], df[...]).astype(BF).reshape(2, sd.shape[0], model)
        for s in scatters["d"]:
            s.copy_piece(cc // 2, cc % 2).start()

    clock.loop(hidden // pair_rows, up_back, 1.7)
    links.rate, links.lag = SCATTER

    def send_home(name, number=None):
        for n, s in enumerate(scatters[name]):
            if number is None or n == number:
                if not s.pieces:
                    s.begin()
                links.scatter(s, clock.now)

    send_home("d")
    bring = [
        pltpu.make_async_copy(p_main, g, msem.at[2]),
        pltpu.make_async_copy(p_last, sl.at[: span_rows(final)], msem.at[3]),
    ]
    bring[0].start()

    def first_back(rt):
        rows = ds(rt * ROWS, ROWS)
        dz = dh[rows, :] + nt(sl[rows, :], wu[...].reshape(model, hidden))
        n1 = n1s[rows, :]
        gv[3:4, :] += csum(dz * n1)
        gv[4:5, :] += csum(dz)
        e = dz * vrow(3)
        d = r1s[rows, 0:1] * (e - rmean(e) - n1 * rmean(e * n1))
        dh[rows, :] = d
        da = d.astype(BF)
        df[rows, :] = da
        gv[2:3, :] += csum(da.astype(F32))

    clock.loop(tiles, first_back, 2.0)

    quarter = hidden // 4
    for n in range(2):

        def up_grad(cc, n=n):
            cs = ds((2 * n + cc) * quarter, quarter, BLOCK)
            wu[:, :, :, :, cs] = tn(z_low[...], sl[:, cs]).astype(BF).reshape(depth, 2, 2, shard, quarter)

        clock.loop(2, up_grad, 1.5)
        send_home("u", n)

    bring[1].start()
    do = z_low

    def out_back(rt):
        rows = ds(rt * ROWS, ROWS)
        do[rows, :] = nt(df[rows, :], wo[...].reshape(model, model)).astype(BF)

    clock.loop(tiles, out_back, 0.4)
    half = model // 2

    def halves(left, right, columns, to, at, time):
        width = columns.stop - columns.start

        def step(t):
            value = tn(left[:, ds(t * half, half, BLOCK)], right[:, columns]).astype(BF)
            shaped = value.reshape(depth // 2, 2, 2, shard, width)
            to[pl.ds(t * (depth // 2), depth // 2), :, :, :, at : at + width] = shaped

        clock.loop(2, step, time)

    halves(o, df, slice(0, model), wo, 0, 0.8)
    send_home("o")
    bring[0].wait()
    bring[1].wait()

    dq = o

    def copy_tokens(rt):
        rows = ds(rt * ROWS, ROWS)
        return pltpu.make_async_copy(x.at[rows], gtok.at[rows], psem.at[0, rt])

    for n in reversed(range(len(groups))):
        first, size = groups[n]
        here = group_span(n)

        def back(j, first=first, size=size):
            row, local = j // size, j % size
            c = ds((first + local) * BLOCK, BLOCK)
            attend_back_pair(row, length, (q, c), (k, c), (v, c), (do, c), dq, probs_of(row * pairs + first + local),
                             dk_sum, dv_sum)

        clock.loop(seqs * size, back, BACK)

        def token_step(rt, n=n, here=here):
            rows = ds(rt * ROWS, ROWS)
            total = dh[rows, :]
            for part, d in enumerate((dq, k, v)):
                total = total + nt(d[rows, here], weight_of(weight_span(n, part)))
            dh[rows, :] = total
            gv[0:1, here] += csum(dq[rows, here].astype(F32))
            gv[1:2, here] += csum(v[rows, here].astype(F32))

        clock.loop(tiles, token_step, 0.25 * size)
        for part, d in enumerate((dq, k, v)):
            span = weight_span(n, part)
            halves(x, d, here, wa, span.start, 0.15 * size)
        if n == 0:
            blank = packed[0][0] + 3 * size * BLOCK

            @pl.when(place.z >= 0)
            def _(blank=blank):
                columns = pack_small(gv[...], gbu[...], shard, parts, g).reshape(depth, 2, 2, shard, BLOCK)
                wa[:, :, :, :, blank : blank + BLOCK] = columns

        send_home(n)

    def token_out(rt):
        rows = ds(rt * ROWS, ROWS)
        x[rows, :] = dh[rows, :].astype(BF)
        copy_tokens(rt).start()

    clock.loop(tiles, token_out, 0.2)
    clock.run(links.all())
    for group in scatters.values():
        for s in group:
            s.end()
    for rt in range(tiles):
        copy_tokens(rt).wait()
    last = n1s[base["small"] : base["small"] + shard, :BLOCK]
    square = jnp.concatenate([last, jnp.zeros((BLOCK - shard, BLOCK), F32)], axis=0).T
    small[...] = square[:16, :]


BEGINS = (0.0, 5.0, 13.0, 16.0, 24.0)
HALVED = ()
GATHER, SCATTER = (52.0, 3.0), (50.0, 2.0)
ATTEND, BACK = 1.6, 1.7


def run_layer(depth, x, seg, sq, sk, sv, small, so, su, sd, og):
    tokens, model = x.shape
    hidden = su.shape[1]
    parts = hidden // model
    seqs, length = seg.shape
    spans, offsets, band = key_windows(length)
    final_rows = band - offsets[-1]
    shard = so.shape[0]
    cuts = []
    for at, width in column_cuts(model):
        cuts.append(("d", 0, sd.shape[0], at, width))
    for part in range(2):
        cuts.append(("u", 0, shard, part * (hidden // 2), hidden // 2))
    cuts.append(("o", 0, shard, 0, model))
    groups = head_groups(model // BLOCK)
    for n, (_, blank) in enumerate(group_columns(model // BLOCK)):
        width = 3 * groups[n][1] * BLOCK + blank
        cuts += [(n, 0, shard, part * (width // 2), width // 2) for part in range(2)]
    buffers = []
    for name, _, rows, _, cols in cuts:
        buffers += (scatter_half_buffers if name in LIGHT else scatter_buffers)(rows, cols, depth)

    def own(s):
        return pltpu.VMEM((depth, 2, 2, *s), BF)

    act, wide = pltpu.VMEM((tokens, model), BF), pltpu.VMEM((tokens, hidden), BF)
    full = pltpu.VMEM((tokens, model), F32)
    weight = sds((shard, model), F32)
    iterations = seqs * model // BLOCK
    return pl.pallas_call(
        functools.partial(layer_kernel, depth, parts, tuple(cuts)),
        out_shape=(sds((tokens, model), BF), sds((seqs, SEGS, model), F32), sds((tokens, model), BF),
                   weight, weight, weight, weight, sds(su.shape, F32), sds(sd.shape, F32), sds((16, BLOCK), F32),
                   sds((tokens, hidden), BF), sds((final_rows, hidden), BF)),
        in_specs=[ANY, V] + [ANY] * 8,
        out_specs=(ANY, V, ANY) + (ANY,) * 6 + (V, ANY, ANY),
        scratch_shapes=[act] * 7 + [full, full, pltpu.VMEM((max(tokens, 2 * length), BLOCK), F32), wide, wide,
                        pltpu.VMEM((ROWS, model), BF), own((shard, 3 * model + small.shape[1])), own(so.shape), own(su.shape), own(sd.shape),
                        pltpu.VMEM((8, model), F32), pltpu.VMEM((1, hidden), F32), pltpu.VMEM((8, model), F32),
                        pltpu.VMEM((1, hidden), F32), *buffers, *gather_sems(5, depth),
                        *scatter_sems(len(cuts), depth), pltpu.SemaphoreType.DMA((4,)), pltpu.SemaphoreType.DMA((1,)),
                        pltpu.SemaphoreType.DMA((2, iterations)),
                        pltpu.SemaphoreType.DMA((1 + 3 * len(groups),))],
        compiler_params=params(0),
        name="layer",
    )(x, seg, sq, sk, sv, small, so, su, sd, og)


def hand_over_kernel(count, shard, parts, *refs):
    ins, small = refs[:count], refs[count]
    outs, vectors = refs[count + 1 : 2 * count + 1], refs[2 * count + 1 : 2 * count + 10]
    rooms, sems = refs[2 * count + 10 : -1], refs[-1]
    fetches = [pltpu.make_async_copy(a, b, sems.at[0, n]) for n, (a, b) in enumerate(zip(ins, rooms))]
    copies = [pltpu.make_async_copy(a, b, sems.at[1, n]) for n, (a, b) in enumerate(zip(rooms, outs))]
    for copy in fetches:
        copy.start()
    for n in range(8):
        vectors[n][...] = small[n, :shard]
    rows = jnp.concatenate([small[8:16, :], jnp.zeros((8, BLOCK), F32)], axis=1)
    total = rows[0]
    for i in range(1, parts):
        total = total + pltpu.roll(rows, i * shard, 1)[i]
    vectors[8][...] = total[: parts * shard]
    for fetch, copy in zip(fetches, copies):
        fetch.wait()
        copy.start()
    for copy in copies:
        copy.wait()


def hand_over(results, small, shard, parts):
    count = len(results)
    return pl.pallas_call(
        functools.partial(hand_over_kernel, count, shard, parts),
        out_shape=[sds(r.shape, r.dtype) for r in results] + [sds((shard,), F32)] * 8 + [sds((parts * shard,), F32)],
        in_specs=[ANY] * count + [V],
        out_specs=[ANY] * count + [V] * 9,
        scratch_shapes=[pltpu.VMEM(r.shape, r.dtype) for r in results] + [pltpu.SemaphoreType.DMA((2, count))],
        name="hand_over",
    )(*results, small)


def local_ring(depth, *args):
    (tokens, segments, w_query, b_query, w_key, w_value, b_value, w_out, b_out, gain1, shift1, w_up, b_up, w_down,
     b_down, gain2, shift2, out_grad) = args
    seqs, length, model = tokens.shape
    shard = w_query.shape[0]
    parts = w_up.shape[1] // model
    x = tokens.reshape(seqs * length, model)
    og = out_grad.reshape(seqs * length, model)
    small = jnp.stack([b_query, b_value, b_out, gain1, shift1, b_down, gain2, shift2] + [
        b_up[i * shard : (i + 1) * shard] for i in range(parts)
    ], axis=1)
    small = jnp.pad(small, ((0, 0), (0, 2 * BLOCK - 8 - parts)))
    *results, gs, _, _ = run_layer(depth, x, segments, w_query, w_key, w_value, small, w_out, w_up, w_down, og)
    out, pooled, gtok, gq, gk, gv, go, gu, gd, gbq, gbv, gbo, gg1, gs1, gbd, gg2, gs2, gb_up = hand_over(
        results, gs, shard, parts
    )
    return (
        out.reshape(tokens.shape), pooled, gtok.reshape(tokens.shape),
        gq, gbq, gk, gv, gbv, go, gbo, gg1, gs1, gu, gb_up, gd, gbd, gg2, gs2,
    )


def mid_kernel(*refs):
    (x, o, og, seg, wo, wu, wd, vec, bup, out, pooled, g_down, g_up, g_out, do, dh1, gv, gbu,
     n1s, r1s, z_low, g, sl, df, dh2) = refs
    tokens, model = x.shape
    hidden = wu.shape[1]
    seqs, length = seg.shape
    gv[...] = jnp.zeros_like(gv)
    pooled[...] = jnp.zeros_like(pooled)

    def vrow(i):
        return vec[i : i + 1, :]

    def up(rt):
        rows = ds(rt * ROWS, ROWS)
        h = x[rows, :].astype(F32) + (nn(o[rows, :], wo[...]) + vrow(2))
        c = h - rmean(h)
        r = lax.rsqrt(rmean(c * c) + EPS)
        n = c * r
        n1s[rows, :] = n
        r1s[rows, :] = jnp.broadcast_to(r, (ROWS, BLOCK))
        z_low[rows, :] = (n * vrow(3) + vrow(4)).astype(BF)
        for cc in range(hidden // CHUNK):
            cs = slice(cc * CHUNK, (cc + 1) * CHUNK)
            u = nn(z_low[rows, :], wu[:, cs]) + bup[:, cs]
            cdf, pdf = phi_parts(u)
            g[rows, cs] = (u * cdf).astype(BF)
            sl[rows, cs] = (cdf + u * pdf).astype(BF)

    loop(tokens // ROWS, up)

    def down(rt):
        rows = ds(rt * ROWS, ROWS)
        h = (n1s[rows, :] * vrow(3) + vrow(4)) + (nn(g[rows, :], wd[...]) + vrow(5))
        c = h - rmean(h)
        r = lax.rsqrt(rmean(c * c) + EPS)
        n2 = c * r
        y = n2 * vrow(6) + vrow(7)
        y_low = y.astype(BF)
        out[rows, :] = y_low
        row = rt * ROWS // length
        ids = seg[pl.ds(row, 1), ds(rt * ROWS % length, ROWS)]
        onehot = (ids == lax.broadcasted_iota(jnp.int32, (SEGS, ROWS), 0)).astype(BF)
        pooled[row] = pooled[row] + (nn(onehot, y_low) + nn(onehot, (y - y_low.astype(F32)).astype(BF)))
        dy = og[rows, :].astype(F32)
        gv[6:7, :] += csum(dy * n2)
        gv[7:8, :] += csum(dy)
        e = dy * vrow(6)
        d = r * (e - rmean(e) - n2 * rmean(e * n2))
        dh2[rows, :] = d
        low = d.astype(BF)
        df[rows, :] = low
        gv[5:6, :] += csum(low.astype(F32))

    loop(tokens // ROWS, down)
    for row in range(seqs):
        onehot = (seg[row : row + 1, :] == lax.broadcasted_iota(jnp.int32, (SEGS, length), 0)).astype(F32)
        pooled[row] = pooled[row] / jnp.sum(onehot, axis=1, keepdims=True)

    def down_grad(cc):
        cs = ds(cc * CHUNK, CHUNK)
        g_down[cs, :] = tn(g[:, cs], df[...]).astype(BF)

    loop(hidden // CHUNK, down_grad)

    def up_back(cc):
        cs = ds(cc * CHUNK, CHUNK)
        total = jnp.zeros((1, CHUNK), F32)
        for rt in range(tokens // ROWS):
            rows = slice(rt * ROWS, (rt + 1) * ROWS)
            du = (nt(df[rows, :], wd[cs, :]) * sl[rows, cs].astype(F32)).astype(BF)
            sl[rows, cs] = du
            total += csum(du.astype(F32))
        gbu[:, cs] = total
        g_up[:, cs] = tn(z_low[...], sl[:, cs]).astype(BF)

    loop(hidden // CHUNK, up_back)

    def first_back(rt):
        rows = ds(rt * ROWS, ROWS)
        dz = dh2[rows, :] + nt(sl[rows, :], wu[...])
        n1 = n1s[rows, :]
        gv[3:4, :] += csum(dz * n1)
        gv[4:5, :] += csum(dz)
        e = dz * vrow(3)
        d = r1s[rows, 0:1] * (e - rmean(e) - n1 * rmean(e * n1))
        dh1[rows, :] = d
        da = d.astype(BF)
        df[rows, :] = da
        gv[2:3, :] += csum(da.astype(F32))
        do[rows, :] = nt(da, wo[...]).astype(BF)

    loop(tokens // ROWS, first_back)

    def out_grad_step(cc):
        cs = ds(cc * (model // 2), model // 2)
        g_out[cs, :] = tn(o[:, cs], df[...]).astype(BF)

    loop(2, out_grad_step)


def qkv_grads(x, dqkv, store):
    model = x.shape[1]
    part = model // 2
    for n, d in enumerate(dqkv):

        def step(t, n=n, d=d):
            store(n, t, tn(x[:, ds(t * part, part, BLOCK)], d[...]).astype(BF))

        loop(2, step)


def token_grads(dh1, dqkv, wa, out):
    model = dh1.shape[1]

    def step(rt):
        rows = ds(rt * ROWS, ROWS)
        total = dh1[rows, :]
        for n, d in enumerate(dqkv):
            total = total + nt(d[rows, :], wa[:, n * model : (n + 1) * model])
        out[rows, :] = total.astype(BF)

    loop(dh1.shape[0] // ROWS, step)


def run_mid(x, o, og, seg, wo, wu, wd, vec, bup):
    tokens, model = x.shape
    hidden = wu.shape[1]
    wide = pltpu.VMEM((tokens, hidden), BF)
    act = sds((tokens, model), BF)
    return pl.pallas_call(
        mid_kernel,
        out_shape=(act, sds((seg.shape[0], SEGS, model), F32), sds(wd.shape, BF), sds(wu.shape, BF), sds(wo.shape, BF),
                   act, sds((tokens, model), F32), sds((8, model), F32), sds((1, hidden), F32)),
        in_specs=[V] * 9,
        out_specs=(V,) * 9,
        scratch_shapes=[pltpu.VMEM((tokens, model), F32), pltpu.VMEM((tokens, BLOCK), F32), pltpu.VMEM((tokens, model), BF),
                        wide, wide, pltpu.VMEM((tokens, model), BF), pltpu.VMEM((tokens, model), F32)],
        compiler_params=params(),
        name="middle",
    )(x, o, og, seg, wo, wu, wd, vec, bup)


def plain_views(length, bias, probs):
    spans, offsets, _ = key_windows(length)

    def rows(held, i):
        return lambda qb: held.at[i, pl.ds(offsets[qb], (spans[qb][1] - spans[qb][0]) * BLOCK)]

    return functools.partial(rows, bias), functools.partial(rows, probs)


def pair_columns(pairs, pair):
    return [ds((part * pairs + pair) * BLOCK, BLOCK) for part in range(3)] + [ds(pair * BLOCK, BLOCK)]


def qkv_kernel(x, wa, vec, seg, qkv, o, probs, bias):
    length, model = seg.shape[1], x.shape[1]
    pairs = model // BLOCK
    bias_of, probs_of = plain_views(length, bias, probs)
    make_bias(seg, lambda row, qb: bias_of(row)(qb))
    for n, row in enumerate((0, None, 1)):
        cs = slice(n * model, (n + 1) * model)

        def project(rt, cs=cs, row=row):
            rows = ds(rt * ROWS, ROWS)
            value = nn(x[rows, :], wa[:, cs])
            qkv[rows, cs] = (value if row is None else value + vec[row : row + 1, :]).astype(BF)

        loop(x.shape[0] // ROWS, project)

    def step(i):
        row = i // pairs
        cq, ck, cv, co = pair_columns(pairs, i % pairs)
        attend_pair(row, length, (qkv, cq), (qkv, ck), (qkv, cv), (o, co), probs_of(i), bias_of(row))

    loop(seg.shape[0] * pairs, step)


def back_kernel(length, qkv_in, do, probs, x, dh1, wa, gtok, g_qkv, gb, qkv, dq, dk_sum, dv_sum):
    model = x.shape[1]
    pairs = model // BLOCK
    qkv[...] = qkv_in[...]
    probs_of = plain_views(length, None, probs)[1]

    def step(i):
        row = i // pairs
        cq, ck, cv, co = pair_columns(pairs, i % pairs)
        attend_back_pair(row, length, (qkv, cq), (qkv, ck), (qkv, cv), (do, co), dq, probs_of(i), dk_sum, dv_sum)

    loop(x.shape[0] // length * pairs, step)
    qkv[:, :model] = dq[...]

    def weight_step(t):
        rows = ds(t * (model // 2), model // 2)
        for n in range(3):
            cs = slice(n * model, (n + 1) * model)
            g_qkv[rows, cs] = tn(x[:, rows], qkv[:, cs]).astype(BF)

    loop(2, weight_step)

    def token_step(rt):
        rows = ds(rt * ROWS, ROWS)
        gtok[rows, :] = (dh1[rows, :] + nt(qkv[rows, :], wa[...])).astype(BF)

    loop(x.shape[0] // ROWS, token_step)
    gb[...] = jnp.concatenate(
        [csum(qkv[:, :model].astype(F32)), csum(qkv[:, 2 * model :].astype(F32)), jnp.zeros((6, model), F32)], axis=0
    )


def local_plain(*args):
    (tokens, segments, w_query, b_query, w_key, w_value, b_value, w_out, b_out, gain1, shift1, w_up, b_up, w_down,
     b_down, gain2, shift2, out_grad) = args
    seqs, length, model = tokens.shape
    count = seqs * length
    band = key_windows(length)[2]
    x = tokens.reshape(count, model)
    og = out_grad.reshape(count, model)

    def gathered(t):
        return lax.all_gather(t, "fsdp", axis=0, tiled=True)

    wa = gathered(jnp.concatenate([w_query, w_key, w_value], axis=1))
    small = gathered(jnp.stack([b_query, b_value, b_out, gain1, shift1, b_down, gain2, shift2], axis=1))
    vec = small.T.astype(F32)
    bup = gathered(b_up).astype(F32)[None]
    wo, wu, wd = gathered(w_out), gathered(w_up), gathered(w_down)
    act = sds((count, model), BF)
    wide = sds((count, 3 * model), BF)
    qkv, o, probs = pl.pallas_call(
        qkv_kernel,
        out_shape=(wide, act, sds((seqs * model // BLOCK, band, 2 * BLOCK), BF)),
        in_specs=[V] * 4,
        out_specs=(V,) * 3,
        scratch_shapes=[pltpu.VMEM((seqs, band, BLOCK), F32)],
        compiler_params=params(),
        name="attention",
    )(x, wa, vec, segments)
    out, pooled, g_down, g_up, g_out, do, dh1, gv, gbu = run_mid(x, o, og, segments, wo, wu, wd, vec, bup)
    part = pltpu.VMEM((length, BLOCK), F32)
    gtok, g_qkv, gb = pl.pallas_call(
        functools.partial(back_kernel, length),
        out_shape=(act, sds((model, 3 * model), BF), sds((8, model), F32)),
        in_specs=[V] * 6,
        out_specs=(V,) * 3,
        scratch_shapes=[pltpu.VMEM((count, 3 * model), BF), pltpu.VMEM((count, model), BF), part, part],
        compiler_params=params(),
        name="attention_back",
    )(qkv, do, probs, x, dh1, wa)
    vectors = jnp.concatenate([gb[:2], gv[2:8]], axis=0).T

    def shared(t):
        mine = lax.psum_scatter(t.astype(F32), "fsdp", scatter_dimension=0, tiled=True)
        return lax.psum(mine.astype(BF), "rep").astype(F32)

    ga, gs = shared(g_qkv), shared(vectors)
    go, gu, gd, gb_up = shared(g_out), shared(g_up), shared(g_down), shared(gbu[0])
    gbq, gbv, gbo, gg1, gs1, gbd, gg2, gs2 = [gs[:, i] for i in range(8)]
    return (
        out.reshape(tokens.shape), pooled, gtok.reshape(tokens.shape),
        ga[:, :model], gbq, ga[:, model : 2 * model], ga[:, 2 * model :], gbv,
        go, gbo, gg1, gs1, gu, gb_up, gd, gbd, gg2, gs2,
    )


def solution(mesh):
    rows = P(("fsdp", "rep"))
    split = P("fsdp")
    placed = (rows, rows) + (split,) * 15 + (rows,)
    results = (rows,) * 3 + (split,) * 15
    owners = mesh.shape["fsdp"]

    def whole(*args):
        shard = args[2].shape[0] // owners
        ring = owners % 8 == 0 and mesh.shape["rep"] == 2 and shard % 16 == 0
        body = functools.partial(local_ring, owners // 4) if ring else local_plain
        return jax.shard_map(body, mesh=mesh, in_specs=placed, out_specs=results, check_vma=False)(*args)

    return whole
```

```python
import functools
import heapq
import math

import jax
import jax.numpy as jnp
from jax import lax
from jax.experimental import pallas as pl
from jax.experimental.pallas import tpu as pltpu
from jax.sharding import PartitionSpec as P

BF = jnp.bfloat16
F32 = jnp.float32
HEAD = 64
SEGS = 8
BLOCK = 128
EPS = 1e-5
MASKED = -1e30
MESH = pl.DeviceIdType.MESH
VMEM_LIMIT = int(63.5 * 2**20)


def nn(a, b):
    return lax.dot_general(a, b, (((1,), (0,)), ((), ())), preferred_element_type=F32)


def nt(a, b):
    return lax.dot_general(a, b, (((1,), (1,)), ((), ())), preferred_element_type=F32)


def tn(a, b):
    return lax.dot_general(a, b, (((0,), (0,)), ((), ())), preferred_element_type=F32)


def rmean(t):
    return jnp.mean(t, axis=-1, keepdims=True)


def csum(t):
    return jnp.sum(t, axis=0, keepdims=True)


def loop(count, step):
    def body(i, carry):
        step(i)
        return carry

    lax.fori_loop(0, count, body, 0)


def ds(start, size, multiple=None):
    if not isinstance(start, int):
        start = pl.multiple_of(start, multiple or size)
    return pl.ds(start, size)


def key_windows(length):
    blocks = length // BLOCK
    spans, offsets, total = [], [], 0
    for qb in range(blocks):
        span = (max(qb - 1, 0), min(qb + 2, blocks))
        spans.append(span)
        offsets.append(total)
        total += (span[1] - span[0]) * BLOCK
    return spans, offsets, total


def stack2(pair):
    lane = lax.broadcasted_iota(jnp.int32, pair.shape, 1)
    zero = jnp.zeros_like(pair)
    return jnp.concatenate(
        [jnp.where(lane < HEAD, pair, zero), jnp.where(lane < HEAD, zero, pair)], axis=0
    )


def unstack_t(both):
    return jnp.concatenate([both[:HEAD, :BLOCK], both[HEAD:, BLOCK:]], axis=0).T


def make_bias(seg, bias_at):
    rows, length = seg.shape
    spans, _, _ = key_windows(length)
    for row in range(rows):
        ids = seg[row : row + 1, :].astype(F32)
        keys = jnp.broadcast_to(ids, (BLOCK, length)).T
        for qb, (k0, k1) in enumerate(spans):
            same = keys[k0 * BLOCK : k1 * BLOCK, :] == ids[:, qb * BLOCK : (qb + 1) * BLOCK]
            bias_at(row, qb)[...] = jnp.where(same, 0.0, MASKED)


def attend_pair(row, length, q, k, v, o, probs_at, bias_at):
    spans, _, _ = key_windows(length)
    (q, cq), (k, ck), (v, cv), (o, co) = q, k, v, o
    r0 = pl.multiple_of(row * length, length)
    vt = v[pl.ds(r0, length), cv].T
    for qb, (k0, k1) in enumerate(spans):
        n = (k1 - k0) * BLOCK
        mine = pl.ds(r0 + qb * BLOCK, BLOCK)
        q2 = stack2(q[mine, cq] * BF(HEAD**-0.5))
        s = nt(k[pl.ds(r0 + k0 * BLOCK, n), ck], q2)
        b = bias_at(qb)[...]
        s = s + jnp.concatenate([b, b], axis=1)
        e = jnp.exp(s - jnp.max(s, axis=0, keepdims=True))
        p = (e * (1.0 / jnp.sum(e, axis=0, keepdims=True))).astype(BF)
        probs_at(qb)[...] = p
        o[mine, co] = unstack_t(nn(vt[:, k0 * BLOCK : k1 * BLOCK], p)).astype(BF)


def attend_back_pair(row, length, q, k, v, do, dq, probs_at, dk_sum, dv_sum):
    spans, _, _ = key_windows(length)
    last = len(spans) - 1
    (q, cq), (k, ck), (v, cv), (do, co) = q, k, v, do
    r0 = pl.multiple_of(row * length, length)
    kt = k[pl.ds(r0, length), ck].T
    for qb, (k0, k1) in enumerate(spans):
        n = (k1 - k0) * BLOCK
        mine = pl.ds(r0 + qb * BLOCK, BLOCK)
        q2 = stack2(q[mine, cq] * BF(HEAD**-0.5))
        do2 = stack2(do[mine, co])
        dp = nt(v[pl.ds(r0 + k0 * BLOCK, n), cv], do2)
        low = probs_at(qb)[...]
        p = low.astype(F32)
        d_s = (p * (dp - jnp.sum(p * dp, axis=0, keepdims=True))).astype(BF)
        dv_part = nn(low, do2)
        dk_part = nn(d_s, q2)
        for kb in range(k0, k1):
            part = slice((kb - k0) * BLOCK, (kb - k0 + 1) * BLOCK)
            held = slice(kb * BLOCK, (kb + 1) * BLOCK)
            a, b = dv_part[part], dk_part[part]
            if qb != max(kb - 1, 0):
                a, b = a + dv_sum[held, :], b + dk_sum[held, :]
            if qb == min(kb + 1, last):
                there = pl.ds(r0 + kb * BLOCK, BLOCK)
                v[there, cv] = a.astype(BF)
                k[there, ck] = b.astype(BF)
            else:
                dv_sum[held, :] = a
                dk_sum[held, :] = b
        dqt = nn(kt[:, k0 * BLOCK : k1 * BLOCK], d_s)
        dq[mine, co] = (unstack_t(dqt) * HEAD**-0.5).astype(BF)


class Place:
    def __init__(self, depth):
        self.depth = depth
        self.f = lax.axis_index("fsdp")
        self.y = lax.axis_index("rep")
        self.c = self.f % 2
        self.x = self.f // 2 % 2
        self.z = self.f // 4
        self.sib = (self.f + 1 - 2 * self.c, self.y)
        self.xn = (self.f + 2 - 4 * self.x, self.y)
        self.yn = (self.f, 1 - self.y)
        self.up = (self.f + 4, self.y)
        self.down = (self.f - 4, self.y)

    def barrier(self):
        sem = pltpu.get_barrier_semaphore()
        for who in (self.sib, self.xn, self.yn):
            pl.semaphore_signal(sem, inc=1, device_id=who, device_id_type=MESH)

        @pl.when(self.z > 0)
        def _():
            pl.semaphore_signal(sem, inc=1, device_id=self.down, device_id_type=MESH)

        @pl.when(self.z < self.depth - 1)
        def _():
            pl.semaphore_signal(sem, inc=1, device_id=self.up, device_id_type=MESH)

        inner = (self.z > 0).astype(jnp.int32) + (self.z < self.depth - 1).astype(jnp.int32)
        pl.semaphore_wait(sem, 3 + inner)


def remote(src, dst, send, recv, who):
    return pltpu.make_async_remote_copy(
        src_ref=src, dst_ref=dst, send_sem=send, recv_sem=recv, device_id=who, device_id_type=MESH
    )


def gather_sems(groups, depth):
    return [
        pltpu.SemaphoreType.DMA((groups, 2, depth - 1)),
        pltpu.SemaphoreType.DMA((groups, depth)),
        pltpu.SemaphoreType.DMA((groups, depth)),
        pltpu.SemaphoreType.DMA((groups, depth + 1)),
        pltpu.SemaphoreType.DMA((groups, depth)),
    ] * 2 + [pltpu.SemaphoreType.DMA((groups,))]


class Gather:
    def __init__(self, place, g, shard, whole, sems, halved=False):
        self.p, self.g, self.shard, self.whole = place, g, shard, whole
        self.halved = halved
        self.sz, self.sx, self.sy, self.sc, self.so, self.rz, self.rx, self.ry, self.rc, self.ro, self.own = sems
        self.rows, self.cols = whole.shape[3:]
        self.done = False

    def piece(self, z, x, half=None):
        return self.piece_of(z, x, self.p.c, half)

    def piece_of(self, z, x, c, half=None):
        if half is None:
            return self.whole.at[z, x, c]
        return self.whole.at[z, x, c, :, ds(half * (self.cols // 2), self.cols // 2)]

    def copy_z(self, direction, distance, z, src=None):
        dst = self.piece(z, self.p.x, self.p.y if self.halved else None)
        return remote(
            dst if src is None else src,
            dst,
            self.sz.at[self.g, direction, distance],
            self.rz.at[self.g, direction, distance],
            self.p.up if direction == 0 else self.p.down,
        )

    def copy_x(self, z, src=None):
        dst = self.piece(z, self.p.x, self.p.y)
        return remote(dst if src is None else src, dst, self.sx.at[self.g, z], self.rx.at[self.g, z], self.p.xn)

    def copy_y(self, z):
        at = self.piece(z, 1 - self.p.x, self.p.y)
        return remote(at, at, self.sy.at[self.g, z], self.ry.at[self.g, z], self.p.yn)

    def copy_c(self, z, src=None):
        dst = self.piece(z, self.p.x)
        return remote(dst if src is None else src, dst, self.sc.at[self.g, z], self.rc.at[self.g, z], self.p.sib)

    def copy_o(self, z):
        at = self.piece(z, self.p.x, self.p.y)
        return remote(at, at, self.so.at[self.g, z], self.ro.at[self.g, z], self.p.yn)

    def o_step(self, k):
        def act(z):
            at = self.piece(z, self.p.x, 1 - self.p.y)
            remote(at, at, self.so.at[self.g, z], self.ro.at[self.g, z], self.p.yn).wait_recv()
            self.copy_c(z).start()

        self.at_distance(k, act)

    def copy_column(self):
        at = self.whole.at[:, 1 - self.p.x, self.p.c]
        n = self.p.depth
        return remote(at, at, self.sc.at[self.g, n], self.rc.at[self.g, n], self.p.sib)

    def local(self):
        return pltpu.make_async_copy(self.shard, self.piece(self.p.z, self.p.x), self.own.at[self.g])

    def z_step(self, k):
        p = self.p
        if k == 0:
            if self.shard is None:
                shard, half = self.piece(p.z, p.x), self.piece(p.z, p.x, p.y)
            else:
                self.local().start()
                shard, half = self.shard, self.shard.at[:, ds(p.y * (self.cols // 2), self.cols // 2)]
            mine = half if self.halved else shard

            @pl.when(p.z < p.depth - 1)
            def _():
                self.copy_z(0, 0, p.z, mine).start()

            @pl.when(p.z > 0)
            def _():
                self.copy_z(1, 0, p.z, mine).start()

            self.copy_x(p.z, half).start()
            self.copy_c(p.z, shard).start()
            return

        for direction in (0, 1):
            z = p.z - k if direction == 0 else p.z + k

            @pl.when(z >= 0 if direction == 0 else z < p.depth)
            def _(direction=direction, z=z):
                self.copy_z(direction, k - 1, z).wait_recv()
                if k < p.depth - 1:

                    @pl.when(p.z < p.depth - 1 if direction == 0 else p.z > 0)
                    def _():
                        self.copy_z(direction, k, z).start()

                self.copy_x(z).start()
                if self.halved:
                    self.copy_o(z).start()
                else:
                    self.copy_c(z).start()

    def at_distance(self, k, act):
        p = self.p
        if k == 0:
            act(p.z)
            return

        @pl.when(p.z - k >= 0)
        def _():
            act(p.z - k)

        @pl.when(p.z + k < p.depth)
        def _():
            act(p.z + k)

    def x_step(self, k):
        def act(z):
            self.copy_x_in(z).wait_recv()
            self.copy_y(z).start()

        self.at_distance(k, act)

    def copy_x_in(self, z):
        at = self.piece(z, 1 - self.p.x, self.p.y)
        return remote(at, at, self.sx.at[self.g, z], self.rx.at[self.g, z], self.p.xn)

    def copy_y_in(self, z):
        at = self.piece(z, 1 - self.p.x, 1 - self.p.y)
        return remote(at, at, self.sy.at[self.g, z], self.ry.at[self.g, z], self.p.yn)

    def y_step(self, k):
        def act(z):
            self.copy_y_in(z).wait_recv()

        self.at_distance(k, act)
        if k == self.p.depth - 1:
            self.copy_column().start()

    def c_step(self):
        self.done = True
        if self.shard is not None:
            self.local().wait()
        p, n = self.p, self.p.depth
        for z in range(n):
            at = self.whole.at[z, p.x, 1 - p.c]
            remote(at, at, self.sc.at[self.g, z], self.rc.at[self.g, z], p.sib).wait_recv()
        at = self.whole.at[:, 1 - p.x, 1 - p.c]
        remote(at, at, self.sc.at[self.g, n], self.rc.at[self.g, n], p.sib).wait_recv()

    def end(self):
        p = self.p
        for k in range(p.depth - 1):
            @pl.when((p.z < p.depth - 1) & (p.z - k >= 0))
            def _():
                self.copy_z(0, k, p.z - k).wait_send()

            @pl.when((p.z > 0) & (p.z + k < p.depth))
            def _():
                self.copy_z(1, k, p.z + k).wait_send()

        for z in range(p.depth):
            self.copy_x(z).wait_send()
            self.copy_y(z).wait_send()
            self.copy_c(z).wait_send()
            if self.halved:

                @pl.when(p.z != z)
                def _(z=z):
                    self.copy_o(z).wait_send()

        self.copy_column().wait_send()


def scatter_sems(groups, depth):
    kinds = [(groups, 2, depth), (groups,), (groups,), (groups, 2, depth - 1), (groups,)]
    return [pltpu.SemaphoreType.DMA(k) for k in kinds] * 2 + [pltpu.SemaphoreType.DMA((groups, 5))]


def scatter_buffers(rows, cols, depth):
    return [
        pltpu.VMEM((2, depth, rows, cols), BF),
        pltpu.VMEM((depth, rows, cols // 2), BF),
        pltpu.VMEM((depth, rows, cols // 2), BF),
        pltpu.VMEM((2 * depth - 3, rows, cols), BF),
        pltpu.VMEM((rows, cols), BF),
    ]


def scatter_half_buffers(rows, cols, depth):
    return [
        pltpu.VMEM((2, depth, rows, cols), BF),
        pltpu.VMEM((depth, rows, cols // 2), BF),
        pltpu.VMEM((depth, rows, cols), BF),
        pltpu.VMEM((2 * depth - 3, rows, cols // 2), BF),
        pltpu.VMEM((rows, cols // 2), BF),
    ]


def add_into(depth, rows, target, other):
    piece = min(rows, 48)
    parts = rows // piece

    def step(i):
        z, at = i // parts, ds(i % parts * piece, piece, 16)
        t = target(z, at)
        t[...] = t[...] + other(z, at)[...]

    loop(depth * parts, step)


class Scatter:
    first, second, along, last = ("y", 2), ("x", 2), 1.0, 1.0
    pieces = False

    def __init__(self, place, g, grad, landing, buffers, sems):
        self.p, self.g, self.grad, self.landing = place, g, grad, landing
        self.in_c, self.in_y, self.in_x, self.in_z, self.in_f = buffers
        (self.sc, self.sy, self.sx, self.sz, self.sf, self.rc, self.ry, self.rx, self.rz, self.rf, self.out) = sems
        _, self.depth, self.rows, self.cols = self.in_c.shape

    def half(self, h):
        return ds(h * (self.cols // 2), self.cols // 2)

    def copy_c(self, x):
        p = self.p
        return remote(
            self.grad.at[:, x, 1 - p.c], self.in_c.at[x], self.sc.at[self.g, x, 0], self.rc.at[self.g, x, 0], p.sib
        )

    def copy_piece(self, z, x):
        p = self.p
        return remote(
            self.grad.at[z, x, 1 - p.c], self.in_c.at[x, z], self.sc.at[self.g, x, z], self.rc.at[self.g, x, z], p.sib
        )

    def copies_c(self, x):
        return [self.copy_piece(z, x) for z in range(self.depth)] if self.pieces else [self.copy_c(x)]

    def copy_y(self):
        p = self.p
        return remote(
            self.grad.at[:, 1 - p.x, p.c, :, self.half(1 - p.y)], self.in_y, self.sy.at[self.g], self.ry.at[self.g], p.yn
        )

    def copy_x(self):
        p = self.p
        return remote(
            self.grad.at[:, 1 - p.x, p.c, :, self.half(p.y)], self.in_x, self.sx.at[self.g], self.rx.at[self.g], p.xn
        )

    def line_slot(self, direction, slot):
        far = self.depth - 2
        return 2 * far if slot == far else 2 * slot + direction

    def copy_z(self, direction, z, slot):
        p = self.p
        return remote(
            self.line_piece(z),
            self.in_z.at[self.line_slot(direction, slot)],
            self.sz.at[self.g, direction, slot],
            self.rz.at[self.g, direction, slot],
            p.up if direction == 0 else p.down,
        )

    def copy_f(self):
        p = self.p
        return remote(self.grad.at[p.z, p.x, p.c], self.in_f, self.sf.at[self.g], self.rf.at[self.g], p.yn)

    def receive(self):
        self.copy_f().wait_recv()

    def end_y(self):
        self.copy_y().wait_send()

    def begin(self):
        self.copy_c(1 - self.p.x).start()
        self.copy_c(self.p.x).start()

    def cores(self, turn):
        p = self.p
        x = 1 - p.x if turn == 0 else p.x
        for copy in self.copies_c(x):
            copy.wait_recv()
        add_into(
            self.depth,
            self.rows,
            lambda z, at: self.grad.at[z, x, p.c, at],
            lambda z, at: self.in_c.at[x, z, at],
        )
        if turn == 0:
            self.begin_exchange()

    def begin_exchange(self):
        self.copy_y().start()

    def line_piece(self, z):
        return self.grad.at[z, self.p.x, self.p.c]

    def over_y(self):
        p = self.p
        self.copy_y().wait_recv()
        add_into(
            self.depth,
            self.rows,
            lambda z, at: self.grad.at[z, 1 - p.x, p.c, at, self.half(p.y)],
            lambda z, at: self.in_y.at[z, at],
        )
        self.copy_x().start()

    def over_x(self):
        p = self.p
        self.copy_x().wait_recv()
        add_into(
            self.depth,
            self.rows,
            lambda z, at: self.grad.at[z, p.x, p.c, at, self.half(p.y)],
            lambda z, at: self.in_x.at[z, at],
        )

    def line(self, wave):
        p, top = self.p, self.depth - 1
        for direction in (0, 1):
            place = p.z if direction == 0 else top - p.z
            if wave == 0:

                @pl.when(place == 0)
                def _(direction=direction):
                    for far in range(top, 0, -1):
                        self.copy_z(direction, far if direction == 0 else top - far, far - 1).start()

                continue

            @pl.when((place >= 1) & (place <= wave))
            def _(direction=direction, place=place):
                far = top - wave + place
                z = far if direction == 0 else top - far
                slot = top - wave
                self.copy_z(direction, z, slot).wait_recv()
                add_into(
                    1,
                    self.rows,
                    lambda _, at: self.line_piece(z).at[at],
                    lambda _, at: self.in_z.at[self.line_slot(direction, slot), at],
                )
                if slot > 0:
                    self.copy_z(direction, z, slot - 1).start()

    def share(self):
        self.copy_f().start()

    def copy_out(self, n):
        _, view, result = self.landing[n]
        return pltpu.make_async_copy(view, result, self.out.at[self.g, n])

    def finish(self):
        p = self.p
        self.receive()
        piece = min(self.rows, 48)
        c0 = 0
        for n, (cols, view, result) in enumerate(self.landing):
            if view is None:
                c0 += cols
                continue

            def step(i, view=view, c0=c0, cols=cols):
                at = ds(i * piece, piece, 16)
                cs = pl.ds(c0, cols)
                view[at, :] = self.total(at, cs)

            loop(self.rows // piece, step)
            if result is not None:
                self.copy_out(n).start()
            c0 += cols

    def total(self, at, cs):
        p = self.p
        return self.grad[p.z, p.x, p.c, at, cs].astype(F32) + self.in_f[at, cs].astype(F32)

    def end(self):
        p, top = self.p, self.depth - 1
        for x in (0, 1):
            for copy in self.copies_c(x):
                copy.wait_send()
        self.end_y()
        self.copy_x().wait_send()
        for direction in (0, 1):
            place = p.z if direction == 0 else top - p.z
            for slot in range(top):

                @pl.when(place + slot < top)
                def _(direction=direction, slot=slot):
                    self.copy_z(direction, 0, slot).wait_send()

        self.copy_f().wait_send()
        for n, (_, _, result) in enumerate(self.landing):
            if result is not None:
                self.copy_out(n).wait()

    def exchanges(self):
        return [self.over_y, self.over_x]

    def steps(self):
        one, two = self.exchanges()

        def two_and_line():
            two()
            self.line(0)

        out = [lambda: self.cores(0), lambda: self.cores(1), one, two_and_line]
        for wave in range(1, self.depth):
            out.append(functools.partial(self.line, wave))
        return out + [self.share, self.finish]


class HalfScatter(Scatter):
    first, second, along, last = ("x", 4), ("y", 2), 0.5, 0.5

    def copy_x(self):
        p = self.p
        return remote(self.grad.at[:, 1 - p.x, p.c], self.in_x, self.sx.at[self.g], self.rx.at[self.g], p.xn)

    def copy_y(self):
        p = self.p
        return remote(
            self.grad.at[:, p.x, p.c, :, self.half(1 - p.y)], self.in_y, self.sy.at[self.g], self.ry.at[self.g], p.yn
        )

    def begin_exchange(self):
        self.copy_x().start()

    def exchanges(self):
        return [self.over_x, self.over_y]

    def over_x(self):
        p = self.p
        self.copy_x().wait_recv()
        add_into(
            self.depth,
            self.rows,
            lambda z, at: self.grad.at[z, p.x, p.c, at],
            lambda z, at: self.in_x.at[z, at],
        )
        self.copy_y().start()

    def over_y(self):
        p = self.p
        self.copy_y().wait_recv()
        add_into(
            self.depth,
            self.rows,
            lambda z, at: self.line_piece(z).at[at],
            lambda z, at: self.in_y.at[z, at],
        )

    def line_piece(self, z):
        return self.grad.at[z, self.p.x, self.p.c, :, self.half(self.p.y)]

    def copy_f(self):
        return remote(self.line_piece(self.p.z), self.in_f, self.sf.at[self.g], self.rf.at[self.g], self.p.yn)

    def receive(self):
        p = self.p
        self.copy_f().wait_recv()
        self.copy_y().wait_send()
        self.grad[p.z, p.x, p.c, :, self.half(1 - p.y)] = self.in_f[...]

    def end_y(self):
        pass

    def total(self, at, cs):
        p = self.p
        return self.grad[p.z, p.x, p.c, at, cs].astype(F32)


def spread(place, owners_rows, parts):
    width = place.shape[0]
    row = lax.broadcasted_iota(jnp.int32, (width, 1), 0)
    target = row
    for owner in range(1, width // owners_rows):
        target = target + jnp.where(row >= owner * owners_rows, (parts - 1) * owners_rows, 0)
    lane = lax.broadcasted_iota(jnp.int32, (width, width * parts), 1)
    place[...] = (lane == target).astype(BF)


def unpack_small(columns, shard, parts, vec, bup, room):
    rows = columns.astype(F32).T
    vec[...] = rows[:8, :]
    low = rows[8:16, :].astype(BF)
    width = 8 * shard
    place = room.at[:width, : width * parts]
    spread(place, shard, parts)
    for t in range(columns.shape[0] // width):
        wide = nn(low[:, t * width : (t + 1) * width], place[...])
        total = wide[0:1]
        for i in range(1, parts):
            total = total + pltpu.roll(wide, i * shard, 1)[i : i + 1]
        bup[:, t * width * parts : (t + 1) * width * parts] = total


def pack_small(gv, gbu, shard, parts, room):
    width = 8 * shard
    wide = width * parts
    model = gv.shape[1]
    place = room.at[:width, :wide]
    spread(place, shard, parts)
    columns = jnp.concatenate([gv, jnp.zeros((BLOCK - 8, model), F32)], axis=0).T
    found = []
    for t in range(model // width):
        piece = jnp.broadcast_to(gbu[:, t * wide : (t + 1) * wide], (8, wide))
        rows = [jnp.zeros((8, wide), F32)]
        for i in range(parts):
            rows.append((pltpu.roll(piece, wide - i * shard, 1) if i else piece)[0:1])
        rows.append(jnp.zeros((BLOCK - 8 - parts, wide), F32))
        found.append(nt(place[...], jnp.concatenate(rows, axis=0).astype(BF)))
    return (columns + jnp.concatenate(found, axis=0)).astype(BF)


ROWS = 256
CHUNK = 768


def phi_parts(u):
    cdf = 0.5 * (1.0 + lax.erf(u * math.sqrt(0.5)))
    pdf = jnp.exp(-0.5 * u * u) * (1.0 / math.sqrt(2.0 * math.pi))
    return cdf, pdf


V = pl.BlockSpec(memory_space=pltpu.VMEM)
ANY = pl.BlockSpec(memory_space=pl.ANY)
sds = jax.ShapeDtypeStruct


def params(collective_id=None):
    if collective_id is None:
        return pltpu.CompilerParams(vmem_limit_bytes=VMEM_LIMIT)
    return pltpu.CompilerParams(
        vmem_limit_bytes=VMEM_LIMIT, collective_id=collective_id, has_side_effects=True
    )


class Links:
    core_rate = 350.0

    def __init__(self):
        self.free = dict.fromkeys("cxyz", 0.0)
        self.heap = []
        self.count = 0
        self.rate, self.lag = GATHER

    def send(self, link, at, size):
        rate = self.core_rate if link == "c" else self.rate
        self.free[link] = max(at, self.free[link]) + size / rate * 1e-3
        return self.free[link] + self.lag

    def push(self, at, task, then=None):
        self.count += 1
        heapq.heappush(self.heap, (at, self.count, task, then))

    def gather(self, gather, at):
        size = gather.rows * gather.cols * 2
        part = size / 2 if gather.halved else size
        depth = gather.p.depth

        def zed(k):
            def then(now):
                if k < depth - 1:
                    self.push(self.send("z", now, part), lambda: gather.z_step(k + 1), zed(k + 1))
                self.push(self.send("x", now, size / 2), lambda: gather.x_step(k), ex(k))
                if k and gather.halved:
                    self.push(self.send("y", now, size / 2), lambda: gather.o_step(k))

            return then

        def ex(k):
            return lambda now: self.push(
                self.send("y", now, size / 2), lambda: gather.y_step(k), lambda now: None if k < depth - 1
                else self.push(now + 2.0, gather.c_step)
            )

        self.push(at, lambda: gather.z_step(0), zed(0))

    def scatter(self, scatter, at):
        size = scatter.rows * scatter.cols * 2
        steps = scatter.steps()
        last = len(steps) - 1

        def after(n):
            def then(now):
                now = now + 0.3
                if n == 0:
                    link, count = scatter.first
                    self.push(self.send(link, now, count * size), steps[2], after(2))
                elif n == 2:
                    link, count = scatter.second
                    self.push(self.send(link, now, count * size), steps[3], after(3))
                elif 3 <= n < last - 2:
                    self.push(self.send("z", now, scatter.along * size), steps[n + 1], after(n + 1))
                elif n == last - 2:
                    self.push(now, steps[last - 1], after(last - 1))
                elif n == last - 1:
                    self.push(self.send("y", now, scatter.last * size), steps[last])

            return then

        part = 0 if scatter.pieces else 4
        self.push(self.send("c", at, part * size), steps[0], after(0))
        self.push(self.send("c", at, part * size), steps[1])

    def due(self, now):
        found = []
        while self.heap and self.heap[0][0] <= now:
            at, _, task, then = heapq.heappop(self.heap)
            found.append(task)
            if then:
                then(at)
        return found

    def all(self):
        return self.due(float("inf"))

    def next(self):
        return self.heap[0][0]


class Clock:
    def __init__(self, links):
        self.links, self.now = links, 0.0

    def run(self, tasks):
        for task in tasks:
            task()

    def spend(self, time):
        self.now += time
        self.run(self.links.due(self.now))

    def until(self, gather):
        while not gather.done:
            self.now = max(self.now, self.links.next())
            self.run(self.links.due(self.now))

    def loop(self, count, step, time):
        ticks = []
        for _ in range(count):
            self.now += time
            ticks.append(self.links.due(self.now))

        def body(i):
            step(i)
            for n, tasks in enumerate(ticks):
                if tasks:

                    @pl.when(i == n)
                    def _(tasks=tasks):
                        self.run(tasks)

        loop(count, body)


def head_groups(pairs):
    few = pairs // 3
    return [(0, few), (few, pairs - few)]


def group_columns(pairs):
    groups = head_groups(pairs)
    blank = 2 * BLOCK
    return [(0, blank), (3 * groups[0][1] * BLOCK + blank, 0)]


LIGHT = ("o", 0, 1)


def column_cuts(model):
    third = model // 3
    return [(0, third), (third, model - third)]


def layer_kernel(depth, parts, cuts, *refs):
    it = iter(refs)

    def take(n):
        return [next(it) for _ in range(n)]

    x_in, seg, sq, sk, sv, small_in, so, su, sd, og_in = take(10)
    out, pooled, gtok, gq, gk, gv_w, go_w, gu_w, gd_w, small, p_main, p_last = take(12)
    x, q, k, v, o, z_low, df, n1s, dh, r1s, g, sl, stage = take(13)
    wa, wo, wu, wd, gv, gbu, vec, bup = take(8)
    sets = [take(5) for _ in cuts]
    gsems, ssems, msem, osem, psem, asem = take(11), take(11), *take(4)

    seqs, length = seg.shape
    tokens, model = x.shape
    hidden = g.shape[1]
    dk_sum, dv_sum = r1s.at[:length], r1s.at[length : 2 * length]
    shard = so.shape[0]
    pairs = model // BLOCK
    spans, offsets, _ = key_windows(length)
    final = len(spans) - 1
    tiles = tokens // ROWS

    def span_rows(qb):
        return (spans[qb][1] - spans[qb][0]) * BLOCK

    def bias_at(row, qb):
        at = 0 if qb == final else offsets[qb]
        lane = (row * 2 + (1 if qb == final else 0)) * BLOCK
        return dh.at[at : at + span_rows(qb), ds(lane, BLOCK)]

    def probs_of(i):
        def at(qb):
            held, at = (sl, 0) if qb == final else (g, offsets[qb])
            return held.at[at : at + span_rows(qb), ds(i * 2 * BLOCK, 2 * BLOCK)]

        return at

    groups = head_groups(pairs)
    packed = group_columns(pairs)

    def group_span(n):
        first, size = groups[n]
        return slice(first * BLOCK, (first + size) * BLOCK)

    def weight_span(n, part):
        width = groups[n][1] * BLOCK
        return slice(packed[n][0] + part * width, packed[n][0] + (part + 1) * width)

    def weight_of(span):
        return wa[:, :, :, :, span].reshape(model, span.stop - span.start)

    place = Place(depth)
    links = Links()
    clock = Clock(links)
    loads = [pltpu.make_async_copy(x_in, x, msem.at[0]), pltpu.make_async_copy(og_in, df, msem.at[1])]
    mine = wa.at[place.z, place.x, place.c]
    packs = [pltpu.make_async_copy(small_in, mine.at[:, 3 * groups[0][1] * BLOCK : packed[1][0]], asem.at[0])]
    for n in range(len(groups)):
        for part, source in enumerate((sq, sk, sv)):
            there = mine.at[:, weight_span(n, part)]
            packs.append(pltpu.make_async_copy(source.at[:, group_span(n)], there, asem.at[len(packs)]))
    for load in packs + loads:
        load.start()
    early = packed[1][0]
    sources = (
        (None, wa.at[:, :, :, :, :early]),
        (None, wa.at[:, :, :, :, early:]),
        (so, wo), (su, wu), (sd, wd),
    )
    gathers = [Gather(place, n, s, w, gsems, n in HALVED) for n, (s, w) in enumerate(sources)]
    for gather, at in zip(gathers, BEGINS):
        links.gather(gather, at)
    for load in packs:
        load.wait()
    place.barrier()
    clock.spend(1.0)
    make_bias(seg, bias_at)
    loads[0].wait()
    clock.until(gathers[0])
    at = packed[0][0] + 3 * groups[0][1] * BLOCK
    unpack_small(wa[:, :, :, :, at : at + BLOCK].reshape(model, BLOCK), shard, parts, vec, bup, g)

    def vrow(i):
        return vec[i : i + 1, :]

    def project(n):
        here = group_span(n)

        def step(rt):
            rows = ds(rt * ROWS, ROWS)
            for part, (to, bias) in enumerate(((q, 0), (k, None), (v, 1))):
                value = nn(x[rows, :], weight_of(weight_span(n, part)))
                to[rows, here] = (value if bias is None else value + vec[bias : bias + 1, here]).astype(BF)

        clock.loop(tiles, step, 0.25 * groups[n][1])

    def copy_probs(i, which, back=False):
        lanes = ds(i * 2 * BLOCK, 2 * BLOCK)
        here = g.at[:, lanes] if which == 0 else sl.at[: span_rows(final), lanes]
        there = (p_main if which == 0 else p_last).at[:, lanes]
        return pltpu.make_async_copy(here, there, psem.at[which, i])

    def attend(n):
        first, size = groups[n]

        def step(j):
            row, local = j // size, j % size
            i = row * pairs + first + local
            c = ds((first + local) * BLOCK, BLOCK)
            attend_pair(row, length, (q, c), (k, c), (v, c), (o, c), probs_of(i), functools.partial(bias_at, row))
            copy_probs(i, 0).start()
            copy_probs(i, 1).start()

        clock.loop(seqs * size, step, ATTEND)

    for n in range(len(groups)):
        clock.until(gathers[min(n, 1)])
        project(n)
        attend(n)
    for i in range(seqs * pairs):
        copy_probs(i, 0).wait()
        copy_probs(i, 1).wait()

    chunks = hidden // CHUNK

    def up(i):
        rows = ds(i // chunks * ROWS, ROWS)

        @pl.when(i % chunks == 0)
        def _():
            h = x[rows, :].astype(F32) + (nn(o[rows, :], wo[...].reshape(model, model)) + vrow(2))
            c = h - rmean(h)
            r = lax.rsqrt(rmean(c * c) + EPS)
            n = c * r
            n1s[rows, :] = n
            r1s[rows, :] = jnp.broadcast_to(r, (ROWS, BLOCK))
            z_low[rows, :] = (n * vrow(3) + vrow(4)).astype(BF)

        cs = ds(i % chunks * CHUNK, CHUNK)
        u = nn(z_low[rows, :], wu[:, :, :, :, cs].reshape(model, CHUNK)) + bup[:, cs]
        cdf, pdf = phi_parts(u)
        g[rows, cs] = (u * cdf).astype(BF)
        sl[rows, cs] = (cdf + u * pdf).astype(BF)

    clock.until(gathers[2])
    clock.until(gathers[3])
    clock.loop(tiles * chunks, up, 22.0 / (tiles * chunks))
    clock.until(gathers[4])
    for gather in gathers:
        gather.end()
    loads[1].wait()
    gv[...] = jnp.zeros_like(gv)
    pooled[...] = jnp.zeros_like(pooled)

    def copy_tile(rt):
        return pltpu.make_async_copy(stage, out.at[ds(rt * ROWS, ROWS)], osem.at[0])

    def down(rt):
        rows = ds(rt * ROWS, ROWS)
        h = (n1s[rows, :] * vrow(3) + vrow(4)) + (nn(g[rows, :], wd[...].reshape(hidden, model)) + vrow(5))
        c = h - rmean(h)
        r = lax.rsqrt(rmean(c * c) + EPS)
        n2 = c * r
        y = n2 * vrow(6) + vrow(7)
        y_low = y.astype(BF)

        @pl.when(rt > 0)
        def _():
            copy_tile(rt - 1).wait()

        stage[...] = y_low
        copy_tile(rt).start()
        row = rt * ROWS // length
        ids = seg[pl.ds(row, 1), ds(rt * ROWS % length, ROWS)]
        onehot = (ids == lax.broadcasted_iota(jnp.int32, (SEGS, ROWS), 0)).astype(BF)
        pooled[row] = pooled[row] + (nn(onehot, y_low) + nn(onehot, (y - y_low.astype(F32)).astype(BF)))
        dy = df[rows, :].astype(F32)
        gv[6:7, :] += csum(dy * n2)
        gv[7:8, :] += csum(dy)
        e = dy * vrow(6)
        d = r * (e - rmean(e) - n2 * rmean(e * n2))
        dh[rows, :] = d
        low = d.astype(BF)
        df[rows, :] = low
        gv[5:6, :] += csum(low.astype(F32))

    clock.loop(tiles, down, 3.0)
    copy_tile(tiles - 1).wait()
    for row in range(seqs):
        onehot = (seg[row : row + 1, :] == lax.broadcasted_iota(jnp.int32, (SEGS, length), 0)).astype(F32)
        pooled[row] = pooled[row] / jnp.sum(onehot, axis=1, keepdims=True)

    base = {}
    at = 0
    for name, rows in (("d", sd.shape[0]), ("o", shard), ("u", shard * (hidden // model)), ("q", shard), ("k", shard),
                       ("v", shard), ("small", shard)):
        base[name] = at
        at += rows
    results = {"d": gd_w, "o": go_w, "u": gu_w, "q": gq, "k": gk, "v": gv_w}
    weights = {"d": wd, "o": wo, "u": wu}
    scatters = {}
    for n, (name, r0, rows, c0, cols) in enumerate(cuts):
        landing = []
        if isinstance(name, int):
            first, size = groups[name]
            cs = slice(first * BLOCK, (first + size) * BLOCK)
            spans_of = [(weight, cs.start + at, part * size * BLOCK + at) for part, weight in enumerate("qkv")
                        for at in range(0, size * BLOCK, 2 * BLOCK)]
            for weight, to, at in spans_of:
                if c0 <= at < c0 + cols:
                    ends = slice(to, to + 2 * BLOCK)
                    landing.append((2 * BLOCK, n1s.at[base[weight] : base[weight] + shard, ends], results[weight].at[:, ends]))
            if packed[name][1] and c0 + cols > 3 * size * BLOCK:
                landing.append((BLOCK, n1s.at[base["small"] : base["small"] + shard, :BLOCK], None))
            grad = wa.at[:, :, :, :, packed[name][0] + c0 : packed[name][0] + c0 + cols]
        else:
            for c in range(c0, c0 + cols, model):
                top = base[name] + c // model * shard + r0
                width = min(model, c0 + cols - c)
                at = c % model
                landing.append((width, n1s.at[top : top + rows, at : at + width],
                                results[name].at[r0 : r0 + rows, c : c + width]))
            grad = weights[name].at[:, :, :, r0 : r0 + rows, c0 : c0 + cols]
        kind = HalfScatter if name in LIGHT else Scatter
        scatters.setdefault(name, []).append(kind(place, n, grad, landing, sets[n], ssems))

    for s in scatters["d"]:
        s.pieces = True
    pair_rows = 2 * sd.shape[0]

    def up_back(cc):
        cs = ds(cc * pair_rows, pair_rows, BLOCK)
        weight = wd[cc // 2, cc % 2].reshape(pair_rows, model)
        total = jnp.zeros((1, pair_rows), F32)
        for rt in range(tiles):
            rows = slice(rt * ROWS, (rt + 1) * ROWS)
            du = (nt(df[rows, :], weight) * sl[rows, cs].astype(F32)).astype(BF)
            sl[rows, cs] = du
            total += csum(du.astype(F32))
        gbu[:, cs] = total
        wd[cc // 2, cc % 2] = tn(g[:, cs], df[...]).astype(BF).reshape(2, sd.shape[0], model)
        for s in scatters["d"]:
            s.copy_piece(cc // 2, cc % 2).start()

    clock.loop(hidden // pair_rows, up_back, 1.7)
    links.rate, links.lag = SCATTER

    def send_home(name, number=None):
        for n, s in enumerate(scatters[name]):
            if number is None or n == number:
                if not s.pieces:
                    s.begin()
                links.scatter(s, clock.now)

    send_home("d")
    bring = [
        pltpu.make_async_copy(p_main, g, msem.at[2]),
        pltpu.make_async_copy(p_last, sl.at[: span_rows(final)], msem.at[3]),
    ]
    bring[0].start()

    def first_back(rt):
        rows = ds(rt * ROWS, ROWS)
        dz = dh[rows, :] + nt(sl[rows, :], wu[...].reshape(model, hidden))
        n1 = n1s[rows, :]
        gv[3:4, :] += csum(dz * n1)
        gv[4:5, :] += csum(dz)
        e = dz * vrow(3)
        d = r1s[rows, 0:1] * (e - rmean(e) - n1 * rmean(e * n1))
        dh[rows, :] = d
        da = d.astype(BF)
        df[rows, :] = da
        gv[2:3, :] += csum(da.astype(F32))

    clock.loop(tiles, first_back, 2.0)

    quarter = hidden // 4
    for n in range(2):

        def up_grad(cc, n=n):
            cs = ds((2 * n + cc) * quarter, quarter, BLOCK)
            wu[:, :, :, :, cs] = tn(z_low[...], sl[:, cs]).astype(BF).reshape(depth, 2, 2, shard, quarter)

        clock.loop(2, up_grad, 1.5)
        send_home("u", n)

    bring[1].start()
    do = z_low

    def out_back(rt):
        rows = ds(rt * ROWS, ROWS)
        do[rows, :] = nt(df[rows, :], wo[...].reshape(model, model)).astype(BF)

    clock.loop(tiles, out_back, 0.4)
    half = model // 2

    def halves(left, right, columns, to, at, time):
        width = columns.stop - columns.start

        def step(t):
            value = tn(left[:, ds(t * half, half, BLOCK)], right[:, columns]).astype(BF)
            shaped = value.reshape(depth // 2, 2, 2, shard, width)
            to[pl.ds(t * (depth // 2), depth // 2), :, :, :, at : at + width] = shaped

        clock.loop(2, step, time)

    halves(o, df, slice(0, model), wo, 0, 0.8)
    send_home("o")
    bring[0].wait()
    bring[1].wait()

    dq = o

    def copy_tokens(rt):
        rows = ds(rt * ROWS, ROWS)
        return pltpu.make_async_copy(x.at[rows], gtok.at[rows], psem.at[0, rt])

    for n in reversed(range(len(groups))):
        first, size = groups[n]
        here = group_span(n)

        def back(j, first=first, size=size):
            row, local = j // size, j % size
            c = ds((first + local) * BLOCK, BLOCK)
            attend_back_pair(row, length, (q, c), (k, c), (v, c), (do, c), dq, probs_of(row * pairs + first + local),
                             dk_sum, dv_sum)

        clock.loop(seqs * size, back, BACK)

        def token_step(rt, n=n, here=here):
            rows = ds(rt * ROWS, ROWS)
            total = dh[rows, :]
            for part, d in enumerate((dq, k, v)):
                total = total + nt(d[rows, here], weight_of(weight_span(n, part)))
            dh[rows, :] = total
            gv[0:1, here] += csum(dq[rows, here].astype(F32))
            gv[1:2, here] += csum(v[rows, here].astype(F32))

        clock.loop(tiles, token_step, 0.25 * size)
        for part, d in enumerate((dq, k, v)):
            span = weight_span(n, part)
            halves(x, d, here, wa, span.start, 0.15 * size)
        if n == 0:
            blank = packed[0][0] + 3 * size * BLOCK

            @pl.when(place.z >= 0)
            def _(blank=blank):
                columns = pack_small(gv[...], gbu[...], shard, parts, g).reshape(depth, 2, 2, shard, BLOCK)
                wa[:, :, :, :, blank : blank + BLOCK] = columns

        send_home(n)

    def token_out(rt):
        rows = ds(rt * ROWS, ROWS)
        x[rows, :] = dh[rows, :].astype(BF)
        copy_tokens(rt).start()

    clock.loop(tiles, token_out, 0.2)
    clock.run(links.all())
    for group in scatters.values():
        for s in group:
            s.end()
    for rt in range(tiles):
        copy_tokens(rt).wait()
    last = n1s[base["small"] : base["small"] + shard, :BLOCK]
    square = jnp.concatenate([last, jnp.zeros((BLOCK - shard, BLOCK), F32)], axis=0).T
    small[...] = square[:16, :]


BEGINS = (0.0, 5.0, 13.0, 16.0, 24.0)
HALVED = ()
GATHER, SCATTER = (52.0, 3.0), (50.0, 2.0)
ATTEND, BACK = 1.6, 1.7


def run_layer(depth, x, seg, sq, sk, sv, small, so, su, sd, og):
    tokens, model = x.shape
    hidden = su.shape[1]
    parts = hidden // model
    seqs, length = seg.shape
    spans, offsets, band = key_windows(length)
    final_rows = band - offsets[-1]
    shard = so.shape[0]
    cuts = []
    for at, width in column_cuts(model):
        cuts.append(("d", 0, sd.shape[0], at, width))
    for part in range(2):
        cuts.append(("u", 0, shard, part * (hidden // 2), hidden // 2))
    cuts.append(("o", 0, shard, 0, model))
    groups = head_groups(model // BLOCK)
    for n, (_, blank) in enumerate(group_columns(model // BLOCK)):
        width = 3 * groups[n][1] * BLOCK + blank
        cuts += [(n, 0, shard, part * (width // 2), width // 2) for part in range(2)]
    buffers = []
    for name, _, rows, _, cols in cuts:
        buffers += (scatter_half_buffers if name in LIGHT else scatter_buffers)(rows, cols, depth)

    def own(s):
        return pltpu.VMEM((depth, 2, 2, *s), BF)

    act, wide = pltpu.VMEM((tokens, model), BF), pltpu.VMEM((tokens, hidden), BF)
    full = pltpu.VMEM((tokens, model), F32)
    weight = sds((shard, model), F32)
    iterations = seqs * model // BLOCK
    return pl.pallas_call(
        functools.partial(layer_kernel, depth, parts, tuple(cuts)),
        out_shape=(sds((tokens, model), BF), sds((seqs, SEGS, model), F32), sds((tokens, model), BF),
                   weight, weight, weight, weight, sds(su.shape, F32), sds(sd.shape, F32), sds((16, BLOCK), F32),
                   sds((tokens, hidden), BF), sds((final_rows, hidden), BF)),
        in_specs=[ANY, V] + [ANY] * 8,
        out_specs=(ANY, V, ANY) + (ANY,) * 6 + (V, ANY, ANY),
        scratch_shapes=[act] * 7 + [full, full, pltpu.VMEM((max(tokens, 2 * length), BLOCK), F32), wide, wide,
                        pltpu.VMEM((ROWS, model), BF), own((shard, 3 * model + small.shape[1])), own(so.shape), own(su.shape), own(sd.shape),
                        pltpu.VMEM((8, model), F32), pltpu.VMEM((1, hidden), F32), pltpu.VMEM((8, model), F32),
                        pltpu.VMEM((1, hidden), F32), *buffers, *gather_sems(5, depth),
                        *scatter_sems(len(cuts), depth), pltpu.SemaphoreType.DMA((4,)), pltpu.SemaphoreType.DMA((1,)),
                        pltpu.SemaphoreType.DMA((2, iterations)),
                        pltpu.SemaphoreType.DMA((1 + 3 * len(groups),))],
        compiler_params=params(0),
        name="layer",
    )(x, seg, sq, sk, sv, small, so, su, sd, og)


def hand_over_kernel(count, shard, parts, *refs):
    ins, small = refs[:count], refs[count]
    outs, vectors = refs[count + 1 : 2 * count + 1], refs[2 * count + 1 : 2 * count + 10]
    rooms, sems = refs[2 * count + 10 : -1], refs[-1]
    fetches = [pltpu.make_async_copy(a, b, sems.at[0, n]) for n, (a, b) in enumerate(zip(ins, rooms))]
    copies = [pltpu.make_async_copy(a, b, sems.at[1, n]) for n, (a, b) in enumerate(zip(rooms, outs))]
    for copy in fetches:
        copy.start()
    for n in range(8):
        vectors[n][...] = small[n, :shard]
    rows = jnp.concatenate([small[8:16, :], jnp.zeros((8, BLOCK), F32)], axis=1)
    total = rows[0]
    for i in range(1, parts):
        total = total + pltpu.roll(rows, i * shard, 1)[i]
    vectors[8][...] = total[: parts * shard]
    for fetch, copy in zip(fetches, copies):
        fetch.wait()
        copy.start()
    for copy in copies:
        copy.wait()


def hand_over(results, small, shard, parts):
    count = len(results)
    return pl.pallas_call(
        functools.partial(hand_over_kernel, count, shard, parts),
        out_shape=[sds(r.shape, r.dtype) for r in results] + [sds((shard,), F32)] * 8 + [sds((parts * shard,), F32)],
        in_specs=[ANY] * count + [V],
        out_specs=[ANY] * count + [V] * 9,
        scratch_shapes=[pltpu.VMEM(r.shape, r.dtype) for r in results] + [pltpu.SemaphoreType.DMA((2, count))],
        name="hand_over",
    )(*results, small)


def local_ring(depth, *args):
    (tokens, segments, w_query, b_query, w_key, w_value, b_value, w_out, b_out, gain1, shift1, w_up, b_up, w_down,
     b_down, gain2, shift2, out_grad) = args
    seqs, length, model = tokens.shape
    shard = w_query.shape[0]
    parts = w_up.shape[1] // model
    x = tokens.reshape(seqs * length, model)
    og = out_grad.reshape(seqs * length, model)
    small = jnp.stack([b_query, b_value, b_out, gain1, shift1, b_down, gain2, shift2] + [
        b_up[i * shard : (i + 1) * shard] for i in range(parts)
    ], axis=1)
    small = jnp.pad(small, ((0, 0), (0, 2 * BLOCK - 8 - parts)))
    *results, gs, _, _ = run_layer(depth, x, segments, w_query, w_key, w_value, small, w_out, w_up, w_down, og)
    out, pooled, gtok, gq, gk, gv, go, gu, gd, gbq, gbv, gbo, gg1, gs1, gbd, gg2, gs2, gb_up = hand_over(
        results, gs, shard, parts
    )
    return (
        out.reshape(tokens.shape), pooled, gtok.reshape(tokens.shape),
        gq, gbq, gk, gv, gbv, go, gbo, gg1, gs1, gu, gb_up, gd, gbd, gg2, gs2,
    )


def mid_kernel(*refs):
    (x, o, og, seg, wo, wu, wd, vec, bup, out, pooled, g_down, g_up, g_out, do, dh1, gv, gbu,
     n1s, r1s, z_low, g, sl, df, dh2) = refs
    tokens, model = x.shape
    hidden = wu.shape[1]
    seqs, length = seg.shape
    gv[...] = jnp.zeros_like(gv)
    pooled[...] = jnp.zeros_like(pooled)

    def vrow(i):
        return vec[i : i + 1, :]

    def up(rt):
        rows = ds(rt * ROWS, ROWS)
        h = x[rows, :].astype(F32) + (nn(o[rows, :], wo[...]) + vrow(2))
        c = h - rmean(h)
        r = lax.rsqrt(rmean(c * c) + EPS)
        n = c * r
        n1s[rows, :] = n
        r1s[rows, :] = jnp.broadcast_to(r, (ROWS, BLOCK))
        z_low[rows, :] = (n * vrow(3) + vrow(4)).astype(BF)
        for cc in range(hidden // CHUNK):
            cs = slice(cc * CHUNK, (cc + 1) * CHUNK)
            u = nn(z_low[rows, :], wu[:, cs]) + bup[:, cs]
            cdf, pdf = phi_parts(u)
            g[rows, cs] = (u * cdf).astype(BF)
            sl[rows, cs] = (cdf + u * pdf).astype(BF)

    loop(tokens // ROWS, up)

    def down(rt):
        rows = ds(rt * ROWS, ROWS)
        h = (n1s[rows, :] * vrow(3) + vrow(4)) + (nn(g[rows, :], wd[...]) + vrow(5))
        c = h - rmean(h)
        r = lax.rsqrt(rmean(c * c) + EPS)
        n2 = c * r
        y = n2 * vrow(6) + vrow(7)
        y_low = y.astype(BF)
        out[rows, :] = y_low
        row = rt * ROWS // length
        ids = seg[pl.ds(row, 1), ds(rt * ROWS % length, ROWS)]
        onehot = (ids == lax.broadcasted_iota(jnp.int32, (SEGS, ROWS), 0)).astype(BF)
        pooled[row] = pooled[row] + (nn(onehot, y_low) + nn(onehot, (y - y_low.astype(F32)).astype(BF)))
        dy = og[rows, :].astype(F32)
        gv[6:7, :] += csum(dy * n2)
        gv[7:8, :] += csum(dy)
        e = dy * vrow(6)
        d = r * (e - rmean(e) - n2 * rmean(e * n2))
        dh2[rows, :] = d
        low = d.astype(BF)
        df[rows, :] = low
        gv[5:6, :] += csum(low.astype(F32))

    loop(tokens // ROWS, down)
    for row in range(seqs):
        onehot = (seg[row : row + 1, :] == lax.broadcasted_iota(jnp.int32, (SEGS, length), 0)).astype(F32)
        pooled[row] = pooled[row] / jnp.sum(onehot, axis=1, keepdims=True)

    def down_grad(cc):
        cs = ds(cc * CHUNK, CHUNK)
        g_down[cs, :] = tn(g[:, cs], df[...]).astype(BF)

    loop(hidden // CHUNK, down_grad)

    def up_back(cc):
        cs = ds(cc * CHUNK, CHUNK)
        total = jnp.zeros((1, CHUNK), F32)
        for rt in range(tokens // ROWS):
            rows = slice(rt * ROWS, (rt + 1) * ROWS)
            du = (nt(df[rows, :], wd[cs, :]) * sl[rows, cs].astype(F32)).astype(BF)
            sl[rows, cs] = du
            total += csum(du.astype(F32))
        gbu[:, cs] = total
        g_up[:, cs] = tn(z_low[...], sl[:, cs]).astype(BF)

    loop(hidden // CHUNK, up_back)

    def first_back(rt):
        rows = ds(rt * ROWS, ROWS)
        dz = dh2[rows, :] + nt(sl[rows, :], wu[...])
        n1 = n1s[rows, :]
        gv[3:4, :] += csum(dz * n1)
        gv[4:5, :] += csum(dz)
        e = dz * vrow(3)
        d = r1s[rows, 0:1] * (e - rmean(e) - n1 * rmean(e * n1))
        dh1[rows, :] = d
        da = d.astype(BF)
        df[rows, :] = da
        gv[2:3, :] += csum(da.astype(F32))
        do[rows, :] = nt(da, wo[...]).astype(BF)

    loop(tokens // ROWS, first_back)

    def out_grad_step(cc):
        cs = ds(cc * (model // 2), model // 2)
        g_out[cs, :] = tn(o[:, cs], df[...]).astype(BF)

    loop(2, out_grad_step)


def qkv_grads(x, dqkv, store):
    model = x.shape[1]
    part = model // 2
    for n, d in enumerate(dqkv):

        def step(t, n=n, d=d):
            store(n, t, tn(x[:, ds(t * part, part, BLOCK)], d[...]).astype(BF))

        loop(2, step)


def token_grads(dh1, dqkv, wa, out):
    model = dh1.shape[1]

    def step(rt):
        rows = ds(rt * ROWS, ROWS)
        total = dh1[rows, :]
        for n, d in enumerate(dqkv):
            total = total + nt(d[rows, :], wa[:, n * model : (n + 1) * model])
        out[rows, :] = total.astype(BF)

    loop(dh1.shape[0] // ROWS, step)


def run_mid(x, o, og, seg, wo, wu, wd, vec, bup):
    tokens, model = x.shape
    hidden = wu.shape[1]
    wide = pltpu.VMEM((tokens, hidden), BF)
    act = sds((tokens, model), BF)
    return pl.pallas_call(
        mid_kernel,
        out_shape=(act, sds((seg.shape[0], SEGS, model), F32), sds(wd.shape, BF), sds(wu.shape, BF), sds(wo.shape, BF),
                   act, sds((tokens, model), F32), sds((8, model), F32), sds((1, hidden), F32)),
        in_specs=[V] * 9,
        out_specs=(V,) * 9,
        scratch_shapes=[pltpu.VMEM((tokens, model), F32), pltpu.VMEM((tokens, BLOCK), F32), pltpu.VMEM((tokens, model), BF),
                        wide, wide, pltpu.VMEM((tokens, model), BF), pltpu.VMEM((tokens, model), F32)],
        compiler_params=params(),
        name="middle",
    )(x, o, og, seg, wo, wu, wd, vec, bup)


def plain_views(length, bias, probs):
    spans, offsets, _ = key_windows(length)

    def rows(held, i):
        return lambda qb: held.at[i, pl.ds(offsets[qb], (spans[qb][1] - spans[qb][0]) * BLOCK)]

    return functools.partial(rows, bias), functools.partial(rows, probs)


def pair_columns(pairs, pair):
    return [ds((part * pairs + pair) * BLOCK, BLOCK) for part in range(3)] + [ds(pair * BLOCK, BLOCK)]


def qkv_kernel(x, wa, vec, seg, qkv, o, probs, bias):
    length, model = seg.shape[1], x.shape[1]
    pairs = model // BLOCK
    bias_of, probs_of = plain_views(length, bias, probs)
    make_bias(seg, lambda row, qb: bias_of(row)(qb))
    for n, row in enumerate((0, None, 1)):
        cs = slice(n * model, (n + 1) * model)

        def project(rt, cs=cs, row=row):
            rows = ds(rt * ROWS, ROWS)
            value = nn(x[rows, :], wa[:, cs])
            qkv[rows, cs] = (value if row is None else value + vec[row : row + 1, :]).astype(BF)

        loop(x.shape[0] // ROWS, project)

    def step(i):
        row = i // pairs
        cq, ck, cv, co = pair_columns(pairs, i % pairs)
        attend_pair(row, length, (qkv, cq), (qkv, ck), (qkv, cv), (o, co), probs_of(i), bias_of(row))

    loop(seg.shape[0] * pairs, step)


def back_kernel(length, qkv_in, do, probs, x, dh1, wa, gtok, g_qkv, gb, qkv, dq, dk_sum, dv_sum):
    model = x.shape[1]
    pairs = model // BLOCK
    qkv[...] = qkv_in[...]
    probs_of = plain_views(length, None, probs)[1]

    def step(i):
        row = i // pairs
        cq, ck, cv, co = pair_columns(pairs, i % pairs)
        attend_back_pair(row, length, (qkv, cq), (qkv, ck), (qkv, cv), (do, co), dq, probs_of(i), dk_sum, dv_sum)

    loop(x.shape[0] // length * pairs, step)
    qkv[:, :model] = dq[...]

    def weight_step(t):
        rows = ds(t * (model // 2), model // 2)
        for n in range(3):
            cs = slice(n * model, (n + 1) * model)
            g_qkv[rows, cs] = tn(x[:, rows], qkv[:, cs]).astype(BF)

    loop(2, weight_step)

    def token_step(rt):
        rows = ds(rt * ROWS, ROWS)
        gtok[rows, :] = (dh1[rows, :] + nt(qkv[rows, :], wa[...])).astype(BF)

    loop(x.shape[0] // ROWS, token_step)
    gb[...] = jnp.concatenate(
        [csum(qkv[:, :model].astype(F32)), csum(qkv[:, 2 * model :].astype(F32)), jnp.zeros((6, model), F32)], axis=0
    )


def local_plain(*args):
    (tokens, segments, w_query, b_query, w_key, w_value, b_value, w_out, b_out, gain1, shift1, w_up, b_up, w_down,
     b_down, gain2, shift2, out_grad) = args
    seqs, length, model = tokens.shape
    count = seqs * length
    band = key_windows(length)[2]
    x = tokens.reshape(count, model)
    og = out_grad.reshape(count, model)

    def gathered(t):
        return lax.all_gather(t, "fsdp", axis=0, tiled=True)

    wa = gathered(jnp.concatenate([w_query, w_key, w_value], axis=1))
    small = gathered(jnp.stack([b_query, b_value, b_out, gain1, shift1, b_down, gain2, shift2], axis=1))
    vec = small.T.astype(F32)
    bup = gathered(b_up).astype(F32)[None]
    wo, wu, wd = gathered(w_out), gathered(w_up), gathered(w_down)
    act = sds((count, model), BF)
    wide = sds((count, 3 * model), BF)
    qkv, o, probs = pl.pallas_call(
        qkv_kernel,
        out_shape=(wide, act, sds((seqs * model // BLOCK, band, 2 * BLOCK), BF)),
        in_specs=[V] * 4,
        out_specs=(V,) * 3,
        scratch_shapes=[pltpu.VMEM((seqs, band, BLOCK), F32)],
        compiler_params=params(),
        name="attention",
    )(x, wa, vec, segments)
    out, pooled, g_down, g_up, g_out, do, dh1, gv, gbu = run_mid(x, o, og, segments, wo, wu, wd, vec, bup)
    part = pltpu.VMEM((length, BLOCK), F32)
    gtok, g_qkv, gb = pl.pallas_call(
        functools.partial(back_kernel, length),
        out_shape=(act, sds((model, 3 * model), BF), sds((8, model), F32)),
        in_specs=[V] * 6,
        out_specs=(V,) * 3,
        scratch_shapes=[pltpu.VMEM((count, 3 * model), BF), pltpu.VMEM((count, model), BF), part, part],
        compiler_params=params(),
        name="attention_back",
    )(qkv, do, probs, x, dh1, wa)
    vectors = jnp.concatenate([gb[:2], gv[2:8]], axis=0).T

    def shared(t):
        mine = lax.psum_scatter(t.astype(F32), "fsdp", scatter_dimension=0, tiled=True)
        return lax.psum(mine.astype(BF), "rep").astype(F32)

    ga, gs = shared(g_qkv), shared(vectors)
    go, gu, gd, gb_up = shared(g_out), shared(g_up), shared(g_down), shared(gbu[0])
    gbq, gbv, gbo, gg1, gs1, gbd, gg2, gs2 = [gs[:, i] for i in range(8)]
    return (
        out.reshape(tokens.shape), pooled, gtok.reshape(tokens.shape),
        ga[:, :model], gbq, ga[:, model : 2 * model], ga[:, 2 * model :], gbv,
        go, gbo, gg1, gs1, gu, gb_up, gd, gbd, gg2, gs2,
    )


def solution(mesh):
    rows = P(("fsdp", "rep"))
    split = P("fsdp")
    placed = (rows, rows) + (split,) * 15 + (rows,)
    results = (rows,) * 3 + (split,) * 15
    owners = mesh.shape["fsdp"]

    def whole(*args):
        shard = args[2].shape[0] // owners
        ring = owners % 8 == 0 and mesh.shape["rep"] == 2 and shard % 16 == 0
        body = functools.partial(local_ring, owners // 4) if ring else local_plain
        return jax.shard_map(body, mesh=mesh, in_specs=placed, out_specs=results, check_vma=False)(*args)

    return whole
```
